128 devices in a mesh: dp: 4 (over y), pipe: 4 (over z_hi, core), tensor: 8 (over z_lo, x).
Axes of the slice: x: 4, y: 4, z: 4 (z_hi: 2, z_lo: 2; z = z_hi * 2 + z_lo), core: 2. Of those that a mesh axis runs over, the one named last changes fastest.
Arguments:
- lm_inputs: bfloat16 [4, 4, 96, 8192], P('dp', 'pipe'), may hold values from -180 to 180
- top_grad: bfloat16 [4, 2, 96, 8192], P('dp', None, 'tensor'), may hold values from -6 to 6
- phase_gain: float32 [2, 8192], replicated, may hold values from 0.5 to 2
- query_weight: bfloat16 [4, 8192, 8, 256], P('pipe', None, 'tensor'), may hold values from -1.08275726 to 1.08275726
- kv_weight: bfloat16 [4, 8192, 8, 128], P('pipe', None, 'tensor'), may hold values from -0.06629126 to 0.06629126
- out_weight: bfloat16 [4, 8, 256, 8192], P('pipe', 'tensor'), may hold values from -0.09375 to 0.09375
- segment_ids: int32 [4, 2, 96], P('dp'), may hold values from 0 to 3, never falling along the last dimension, each value on 1 to 48 neighbouring positions
- visual_pos: int32 [4, 96], P('dp'), may hold values from 0 to 191, as said below
- patches: bfloat16 [4, 96, 5120], P('dp', 'pipe'), may hold values from -6 to 6
- ln_gain: float32 [1280], replicated, may hold values from 0.5 to 2
- ln_bias: float32 [1280], replicated, may hold values from -3 to 3
- fc1_weight: bfloat16 [5120, 2560], P(None, 'tensor'), may hold values from -0.078125 to 0.078125
- fc1_bias: float32 [2560], P('tensor'), may hold values from -3 to 3
- fc2_weight: bfloat16 [2560, 8192], P('tensor'), may hold values from -0.125 to 0.125
Outputs:
- patch_grads: bfloat16 [4, 96, 5120], P('dp', 'pipe')
- fc1_grad: float32 [5120, 2560], P(('dp', 'pipe'), 'tensor')
- fc2_grad_t: float32 [8192, 2560], P(('dp', 'pipe'), 'tensor')
The draws below stay inside these ranges and needn't reach their ends.
Inputs may be any that keep to these rules, and one draw needn't show every extreme that they name: `visual_pos`: sorted increasing and distinct; they come in runs of 4 rows starting at multiples of 4, and micro-batch m holds exactly 48 of them, all in rows m * 96 to (m + 1) * 96 - 1. `segment_ids`: numbers never fall along a micro-batch.
All inputs are finite; a program needn't handle non-finite values.
Results may differ from the reference program's by a relative error of at most 0.027.
Values may be sent and summed in bfloat16 or wider, within the bound.
A program may use at most 128 MiB of HBM per device.

```python
import math
import jax
import jax.numpy as jnp
import numpy as np
from jax import lax

D = 8192
KVH = 8
CTX = 1280
HD = 128
QH = 32
MH = 2560
MB = 2
SEQ = 96
HQ = 2
NV = 96
NVP = 24
MC = 5120
N_DP = 4
N_PIPE = 4
N_TENSOR = 8


def shared_keys(key):
    return jnp.clip(jax.random.normal(key, (N_PIPE, D, KVH, HD), jnp.float32), -6.0, 6.0)


def draw_kv_weight(key, part):
    base_draw = shared_keys(key)
    return (base_draw * D ** (-0.5)).astype(jnp.bfloat16)


def draw_query_weight(key, part):
    key = jax.random.fold_in(key, 22)
    full_shape = (N_PIPE, D, KVH, HQ * HD)
    fresh_draw = jnp.clip(jax.random.normal(key, full_shape, jnp.float32), -6.0, 6.0)
    values = fresh_draw
    return (values * D ** (-0.5)).astype(jnp.bfloat16)


def draw_lm_inputs(key, part):
    key = jax.random.fold_in(key, 11)
    subkeys = jax.random.split(key, 3)
    full_shape = (N_DP, N_PIPE, SEQ, D)
    row_scale = jnp.exp(jax.random.uniform(subkeys[0], (N_DP, N_PIPE, SEQ, 1), jnp.float32, 0.0, math.log(10.0)))
    column_scale = jnp.exp(jax.random.uniform(subkeys[1], (1, 1, 1, D), jnp.float32, 0.0, math.log(10.0)))
    base_draw = jnp.clip(jax.random.normal(subkeys[2], full_shape, jnp.float32), -6.0, 6.0)
    values = base_draw * row_scale * column_scale * 0.3
    return values.astype(jnp.bfloat16)


def draw_visual_pos(key, part):
    key = jax.random.fold_in(key, 41)
    unit_count = SEQ // 4
    scores = jax.random.randint(key, (N_DP, MB, unit_count), 0, 1 << 20) * unit_count + jnp.arange(unit_count, dtype=jnp.int32)
    ranking = jnp.argsort(jnp.argsort(scores, axis=-1), axis=-1)
    picked = ranking < unit_count // 2
    order_ids = jnp.arange(unit_count, dtype=jnp.int32)
    chosen = jnp.sort(jnp.where(picked, order_ids, unit_count), axis=-1)[..., :unit_count // 2]
    offsets = jnp.arange(MB, dtype=jnp.int32)[None, :, None, None] * SEQ
    within = jnp.arange(4, dtype=jnp.int32)[None, None, None, :]
    positions = offsets + chosen[..., None] * 4 + within
    return positions.reshape(N_DP, MB * SEQ // 2).astype(jnp.int32)


def shard_levels(key, shape, cuts, least, largest):
    def one(axis_at, shards_of):
        steps = jax.random.uniform(jax.random.fold_in(jax.random.fold_in(key, 6), axis_at), (shards_of,), jnp.float32, least / len(cuts), largest / len(cuts))
        return jnp.repeat(jnp.exp(steps), shape[axis_at] // shards_of).reshape((-1,) + (1,) * (len(shape) - axis_at - 1))

    factor_of = one(*cuts[0])
    for cut in cuts[1:]:
        factor_of = factor_of * one(*cut)
    return factor_of


def length_profile(count, total, most, slope):
    loads = [(1 << 20) // math.isqrt(standing ** slope) + 1 for standing in range(2, count + 1)]
    surplus, holding = total - most - (count - 1), [1] * (count - 1)
    while surplus > 0:
        free = [i for i in range(count - 1) if holding[i] < most]
        mass, left = sum([loads[i] for i in free]), surplus
        for i in free:
            extra = min(most - holding[i], max(1, left * loads[i] // mass), surplus)
            holding[i] = holding[i] + extra
            surplus = surplus - extra
    return np.array([most] + holding)


def uneven_parts(rng, amount, total, reach, lean):
    if amount == 2:
        one = jax.random.randint(rng, (), max(1, total - reach), min(reach, total - 1) + 1)
        return jnp.stack([one, total - one])
    tallies = jnp.asarray(length_profile(amount, total, reach, lean), jnp.int32)
    pairs = (amount - 1) // 2
    giver, taker = tallies[1:1 + 2 * pairs:2], tallies[2:2 + 2 * pairs:2]
    slack = jnp.minimum(giver - 1, reach - taker)
    moved = jax.random.randint(jax.random.fold_in(rng, 1), (pairs,), 0, 1 << 20) % (slack + 1)
    tallies = tallies.at[1:1 + 2 * pairs:2].set(giver - moved).at[2:2 + 2 * pairs:2].set(taker + moved)
    return tallies[jax.random.permutation(jax.random.fold_in(rng, 2), amount)]


def normal_values(rng, shape, spread, limit, cuts=(), held_as=jnp.bfloat16):
    result = spread * jax.random.normal(rng, shape, jnp.float32)
    if cuts:
        result = result * shard_levels(rng, shape, cuts, -0.22, 0.18)
    return jnp.clip(result, -limit, limit).astype(held_as)


def setup_inputs(seed: int = 0) -> dict:
    key_list = jax.random.split(jax.random.key(seed), 15)
    lm_inputs = draw_lm_inputs(jax.random.fold_in(key_list[14], 71), 0)
    top_grad = normal_values(key_list[1], (N_DP, MB, SEQ, D), 1.0, 6.0, ((0, 4), (2, 8)))
    phase_gain = jnp.clip(jnp.exp(jax.random.uniform(key_list[2], (2, D), jnp.float32, math.log(0.5), math.log(2.0))), 0.5, 2.0)
    query_weight = draw_query_weight(jax.random.fold_in(key_list[14], 71), 0)
    kv_weight = draw_kv_weight(jax.random.fold_in(key_list[14], 71), 0)
    out_weight = normal_values(key_list[5], (N_PIPE, KVH, HQ * HD, D), (QH * HD) ** -0.5, 0.09375, ((0, 4), (1, 8)))
    segment_ids = jax.vmap(lambda own: jnp.searchsorted(jnp.cumsum(uneven_parts(own, 4, SEQ, SEQ // 2, 0)), jnp.arange(SEQ), side="right"))(jax.random.split(key_list[6], N_DP * MB)).reshape((N_DP, MB, SEQ)).astype(jnp.int32)
    visual_pos = draw_visual_pos(jax.random.fold_in(key_list[14], 71), 0)
    patches = normal_values(key_list[8], (N_DP, NV, MC), 1.0, 6.0, ((0, 4), (1, 4)))
    ln_gain = jnp.clip(jnp.exp(jax.random.uniform(key_list[9], (CTX,), jnp.float32, math.log(0.5), math.log(2.0))), 0.5, 2.0)
    ln_bias = normal_values(key_list[10], (CTX,), 0.5, 3.0, (), jnp.float32)
    fc1_weight = normal_values(key_list[11], (MC, MH), MC ** -0.5, 0.078125, ((1, 8),))
    fc1_bias = normal_values(key_list[12], (MH,), 0.5, 3.0, ((0, 8),), jnp.float32)
    fc2_weight = normal_values(key_list[13], (MH, D), MH ** -0.5, 0.125, ((0, 8),))
    return dict(lm_inputs=lm_inputs, top_grad=top_grad, phase_gain=phase_gain, query_weight=query_weight, kv_weight=kv_weight, out_weight=out_weight, segment_ids=segment_ids, visual_pos=visual_pos, patches=patches, ln_gain=ln_gain, ln_bias=ln_bias, fc1_weight=fc1_weight, fc1_bias=fc1_bias, fc2_weight=fc2_weight)


EPS_RMS = 1e-06
EPS_LN = 1e-06
THETA = 1000000.0

def hold_value(values):
    return lax.optimization_barrier(values)

def rope_tables(length, head_dim):
    half_dim = head_dim // 2
    freq_table = THETA ** (-(2.0 * jnp.arange(half_dim, dtype=jnp.float32)) / head_dim)
    angles = jnp.arange(length, dtype=jnp.float32)[:, None] * freq_table[None, :]
    return (jnp.cos(angles), jnp.sin(angles))

def rotate(vectors, cosine, sine_table, direction):
    half_dim = vectors.shape[-1] // 2
    first_half = vectors[..., :half_dim]
    second_half = vectors[..., half_dim:]
    return jnp.concatenate([first_half * cosine - direction * second_half * sine_table, second_half * cosine + direction * first_half * sine_table], axis=-1)

def gelu_slope(values):
    normal_cdf = 0.5 * (1.0 + jax.scipy.special.erf(values * 0.7071067811865476))
    density = jnp.exp(-0.5 * values * values) * 0.3989422804014327
    return normal_cdf + values * density

def phase_backward(inputs, incoming, norm_gain, query_w, kv_w, out_w, segments):
    length, model_width = inputs.shape
    heads_kv = kv_w.shape[2]
    head_dim = kv_w.shape[3]
    half_dim = head_dim // 2
    per_half = query_w.shape[3] // head_dim
    values_in = inputs.astype(jnp.float32)
    scale_rms = lax.rsqrt(lax.optimization_barrier(jnp.mean(values_in * values_in, axis=-1, keepdims=True)) + EPS_RMS)
    unit_vals = values_in * scale_rms
    normed = (unit_vals * norm_gain[None, :]).astype(jnp.bfloat16)
    cosine, sine_table = rope_tables(length, head_dim)
    query_list = []
    grad_list = []
    kv_list = []
    for pair_side in range(2):
        query_rows = jnp.dot(normed, query_w[pair_side].reshape(model_width, -1), preferred_element_type=jnp.float32)
        query_rows = query_rows.reshape(length, heads_kv, per_half, head_dim)
        query_list.append(rotate(query_rows, cosine[:, None, None, :], sine_table[:, None, None, :], 1.0).astype(jnp.bfloat16))
        kv_rows = jnp.dot(normed, kv_w[pair_side].reshape(model_width, -1), preferred_element_type=jnp.float32)
        kv_list.append(kv_rows.reshape(length, heads_kv, head_dim).astype(jnp.bfloat16))
        grad_rows = lax.dot_general(incoming, out_w[pair_side].reshape(-1, model_width), (((1,), (1,)), ((), ())), preferred_element_type=jnp.float32)
        grad_list.append(grad_rows.reshape(length, heads_kv, per_half, head_dim).astype(jnp.bfloat16))
    key_heads = jnp.concatenate([kv_list[0][..., :half_dim], kv_list[1][..., :half_dim]], axis=-1)
    value_heads = jnp.concatenate([kv_list[0][..., half_dim:], kv_list[1][..., half_dim:]], axis=-1)
    key_heads = rotate(key_heads.astype(jnp.float32), cosine[:, None, :], sine_table[:, None, :], 1.0).astype(jnp.bfloat16)
    query_all = hold_value(jnp.stack(query_list, axis=2)).astype(jnp.float32)
    grad_all = hold_value(jnp.stack(grad_list, axis=2)).astype(jnp.float32)
    key_float = hold_value(key_heads).astype(jnp.float32)
    value_float = hold_value(value_heads).astype(jnp.float32)
    factor = head_dim ** (-0.5)
    scores = jnp.einsum('sgbhe,tge->gbhst', query_all, key_float) * factor
    positions = jnp.arange(length)
    allowed = (positions[None, :] <= positions[:, None]) & (segments[:, None] == segments[None, :])
    scores = jnp.where(allowed, scores, -1e+30)
    top_score = lax.optimization_barrier(jnp.max(scores, axis=-1, keepdims=True))
    weights = jnp.where(allowed, jnp.exp(scores - top_score), 0.0)
    probs_full = weights / lax.optimization_barrier(jnp.sum(weights, axis=-1, keepdims=True))
    probs_low = hold_value(probs_full.astype(jnp.bfloat16)).astype(jnp.float32)
    grad_prob = jnp.einsum('sgbhe,tge->gbhst', grad_all, value_float)
    delta_rows = lax.optimization_barrier(jnp.sum(probs_full * grad_prob, axis=-1, keepdims=True))
    grad_score = hold_value((probs_full * (grad_prob - delta_rows) * factor).astype(jnp.bfloat16)).astype(jnp.float32)
    grad_query = jnp.einsum('gbhst,tge->sgbhe', grad_score, key_float)
    grad_query = rotate(grad_query, cosine[:, None, None, None, :], sine_table[:, None, None, None, :], -1.0).astype(jnp.bfloat16)
    grad_key = jnp.einsum('gbhst,sgbhe->tge', grad_score, query_all)
    grad_key = rotate(grad_key, cosine[:, None, :], sine_table[:, None, :], -1.0)
    grad_value = jnp.einsum('gbhst,sgbhe->tge', probs_low, grad_all)
    block_size = heads_kv // N_TENSOR
    grad_normed = jnp.zeros((length, model_width), jnp.float32)
    for pair_side in range(2):
        share_start = pair_side * half_dim
        grad_kv = jnp.concatenate([grad_key[..., share_start:share_start + half_dim], grad_value[..., share_start:share_start + half_dim]], axis=-1).astype(jnp.bfloat16)
        for block_index in range(N_TENSOR):
            first_head = block_index * block_size
            last_head = first_head + block_size
            term_rows = jnp.dot(grad_query[:, first_head:last_head, pair_side].reshape(length, -1), query_w[pair_side][:, first_head:last_head].reshape(model_width, -1).T, preferred_element_type=jnp.float32)
            term_rows = term_rows + jnp.dot(grad_kv[:, first_head:last_head].reshape(length, -1), kv_w[pair_side][:, first_head:last_head].reshape(model_width, -1).T, preferred_element_type=jnp.float32)
            grad_normed = grad_normed + hold_value(term_rows.astype(jnp.bfloat16)).astype(jnp.float32)
    grad_unit = grad_normed * norm_gain[None, :]
    inner_mean = lax.optimization_barrier(jnp.mean(grad_unit * unit_vals, axis=-1, keepdims=True))
    grad_norm = scale_rms * (grad_unit - unit_vals * inner_mean)
    return (incoming.astype(jnp.float32) + grad_norm).astype(jnp.bfloat16)

def merger_backward(patch_rows, rows_grad, ln_gain, ln_bias, fc1_weight, fc1_bias, fc2_weight):
    token_count = patch_rows.shape[0]
    context = ln_gain.shape[0]
    patch_vals = patch_rows.astype(jnp.float32).reshape(token_count, -1, context)
    centered = patch_vals - lax.optimization_barrier(jnp.mean(patch_vals, axis=-1, keepdims=True))
    inv_std = lax.rsqrt(lax.optimization_barrier(jnp.mean(centered * centered, axis=-1, keepdims=True)) + EPS_LN)
    patch_unit = centered * inv_std
    merger_normed = (patch_unit * ln_gain + ln_bias).astype(jnp.bfloat16).reshape(token_count, -1)
    hidden_pre = jnp.dot(merger_normed, fc1_weight, preferred_element_type=jnp.float32) + fc1_bias[None, :]
    activated = jax.nn.gelu(hidden_pre, approximate=False).astype(jnp.bfloat16)
    grad_act = lax.dot_general(rows_grad, fc2_weight, (((1,), (1,)), ((), ())), preferred_element_type=jnp.float32)
    grad_pre = (grad_act * gelu_slope(hidden_pre)).astype(jnp.bfloat16)
    grad_merged = lax.dot_general(grad_pre, fc1_weight, (((1,), (1,)), ((), ())), preferred_element_type=jnp.float32)
    patch_grad_unit = grad_merged.reshape(token_count, -1, context) * ln_gain
    patch_grad = inv_std * (patch_grad_unit - lax.optimization_barrier(jnp.mean(patch_grad_unit, axis=-1, keepdims=True)) - patch_unit * lax.optimization_barrier(jnp.mean(patch_grad_unit * patch_unit, axis=-1, keepdims=True)))
    fc1_term = lax.dot_general(merger_normed, grad_pre, (((0,), (0,)), ((), ())), preferred_element_type=jnp.float32)
    fc2_term = lax.dot_general(rows_grad, activated, (((0,), (0,)), ((), ())), preferred_element_type=jnp.float32)
    return (patch_grad.reshape(token_count, -1).astype(jnp.bfloat16), fc1_term, fc2_term)

def reference(lm_inputs, top_grad, phase_gain, query_weight, kv_weight, out_weight, segment_ids, visual_pos, patches, ln_gain, ln_bias, fc1_weight, fc1_bias, fc2_weight):
    fc1_total = jnp.zeros(fc1_weight.shape, jnp.float32)
    fc2_total = jnp.zeros((fc2_weight.shape[1], fc2_weight.shape[0]), jnp.float32)
    patch_list = []
    for data_group in range(N_DP):
        lower_list = []
        for micro_batch in range(MB):
            upper_out = phase_backward(lm_inputs[data_group, 2 + micro_batch], top_grad[data_group, micro_batch], phase_gain[1], query_weight[2:4], kv_weight[2:4], out_weight[2:4], segment_ids[data_group, micro_batch])
            lower_list.append(phase_backward(lm_inputs[data_group, micro_batch], upper_out, phase_gain[0], query_weight[0:2], kv_weight[0:2], out_weight[0:2], segment_ids[data_group, micro_batch]))
        phase_rows = jnp.concatenate(lower_list, axis=0)
        visual_grad = jnp.take(phase_rows, visual_pos[data_group], axis=0)
        owner_list = []
        for owner_index in range(N_PIPE):
            first_token = owner_index * NVP
            patch_grad, fc1_term, fc2_term = merger_backward(patches[data_group, first_token:first_token + NVP], visual_grad[first_token:first_token + NVP], ln_gain, ln_bias, fc1_weight, fc1_bias, fc2_weight)
            owner_list.append(patch_grad)
            fc1_total = fc1_total + hold_value(fc1_term.astype(jnp.bfloat16)).astype(jnp.float32)
            fc2_total = fc2_total + hold_value(fc2_term.astype(jnp.bfloat16)).astype(jnp.float32)
        patch_list.append(jnp.concatenate(owner_list, axis=0))
    return (jnp.stack(patch_list, axis=0), fc1_total, fc2_total)
```

```python
import functools

import jax
import jax.numpy as jnp
import numpy as np
from jax import lax
from jax.experimental import pallas as pl
from jax.experimental.pallas import tpu as pltpu
from jax.sharding import PartitionSpec as P

EPS_RMS = 1e-06
EPS_LN = 1e-06
THETA = 1000000.0
MESH = pl.DeviceIdType.MESH
F32 = jnp.float32
BF16 = jnp.bfloat16
SEQ = 96
WIDTH = 8192
HALF = 4096
BLK = 512
HEAD = 128
FACTOR = HEAD**-0.5
VIS = 48
CTX = 1280
PIECE = 320
LANES = 384


def nn(a, b):
    return lax.dot_general(a, b, (((1,), (0,)), ((), ())), preferred_element_type=F32)


def nt(a, b):
    return lax.dot_general(a, b, (((1,), (1,)), ((), ())), preferred_element_type=F32)


def tn(a, b):
    return lax.dot_general(a, b, (((0,), (0,)), ((), ())), preferred_element_type=F32)


def each(count, body):
    def step(i, carry):
        body(i)
        return carry

    lax.fori_loop(0, count, step, 0)


def eye_mask(size):
    return lax.broadcasted_iota(jnp.int32, (size, size), 0) == lax.broadcasted_iota(
        jnp.int32, (size, size), 1
    )


def to_row(column):
    size = column.shape[0]
    return jnp.sum(jnp.where(eye_mask(size), column, 0.0), axis=0, keepdims=True)


def to_column(row):
    size = row.shape[1]
    return jnp.sum(jnp.where(eye_mask(size), row, 0.0), axis=1, keepdims=True)


class Sems:
    def __init__(self):
        self.numbers = {}

    def __call__(self, *name):
        return self.numbers.setdefault(name, len(self.numbers))


def kernel(
    x_hbm,
    tg_hbm,
    gain_ref,
    wq_hbm,
    wkv_hbm,
    wo_hbm,
    seg_ref,
    pos_ref,
    patches_ref,
    lng_ref,
    lnb_ref,
    fc1_hbm,
    fc1b_ref,
    fc2_hbm,
    cos_ref,
    sin_ref,
    tgsel_ref,
    pg_out,
    fc1_out,
    fc2_out,
    w3,
    wo,
    f1,
    f2,
    xo,
    xb,
    sc,
    gb,
    tg,
    inc,
    own_p,
    other_p,
    pf,
    qs,
    ks,
    vs,
    probs,
    gx_own,
    gx_other,
    acts,
    ins,
    inr,
    part,
    r1,
    r2,
    r3_send,
    r3,
    xsum,
    out_block,
    vis,
    pu,
    iv,
    mn,
    mns,
    act,
    slope,
    nblk,
    lgb,
    ga_own,
    ga_other,
    gpre,
    mnr,
    actr,
    gpr,
    visr,
    pgp,
    pgpr,
    pgs,
    pgr,
    send_sem,
    recv_sem,
    local_sem,
):
    dp = lax.axis_index("dp")
    pipe = lax.axis_index("pipe")
    ten = lax.axis_index("tensor")
    phase = pipe // 2
    core = pipe % 2
    zl = ten // 4
    xx = ten % 4
    sems = Sems()
    locals_ = Sems()

    def device(s=None, b=None, z=None, x=None, d=None, t=None):
        s = phase if s is None else s
        b = core if b is None else b
        if t is None:
            t = (zl if z is None else z) * 4 + (xx if x is None else x)
        return (dp if d is None else d, 2 * s + b, t)

    sibling = device(b=1 - core)
    right_x = lax.rem(xx + 1, 4)
    left_x = lax.rem(xx + 3, 4)
    far_x = lax.rem(xx + 2, 4)
    right = device(x=right_x)
    left = device(x=left_x)
    zmate = device(z=1 - zl)
    cross = device(s=1 - phase, z=1 - zl)

    barrier = pltpu.get_barrier_semaphore()
    count = 0
    for o in range(1, 16):
        code = lax.rem(core * 8 + ten + o, 16)
        pl.semaphore_signal(
            barrier, inc=1, device_id=device(b=code // 8, t=lax.rem(code, 8)), device_id_type=MESH
        )
        code = lax.rem(dp * 4 + pipe + o, 16)
        pl.semaphore_signal(
            barrier, inc=1, device_id=(code // 4, lax.rem(code, 4), ten), device_id_type=MESH
        )
        count += 2
    pl.semaphore_signal(barrier, inc=1, device_id=cross, device_id_type=MESH)
    count += 1

    def local(name, src, dst):
        copy = pltpu.make_async_copy(src, dst, local_sem.at[locals_(name)])
        copy.start()
        return copy

    def remote(name, src, dst, to):
        number = sems(*name)
        copy = pltpu.make_async_remote_copy(
            src_ref=src,
            dst_ref=dst,
            send_sem=send_sem.at[number],
            recv_sem=recv_sem.at[number],
            device_id=to,
            device_id_type=MESH,
        )
        copy.start()
        return copy

    def arrive(name, ref):
        pltpu.make_async_copy(ref, ref, recv_sem.at[sems(*name)]).wait()

    mine = core * HALF
    theirs = (1 - core) * HALF
    lx = local("x", x_hbm, xo)
    lxh = local("xh", x_hbm.at[:, pl.ds(mine, HALF)], xb.at[core])
    lq = local("q", wq_hbm.at[pl.ds(mine, HALF), :], w3.at[core])
    lkv = local(
        "kv", wkv_hbm.at[pl.ds(mine, HALF), :], w3.at[2, :, pl.ds(core * HEAD, HEAD)]
    )
    lo = local("o", wo_hbm.at[:, pl.ds(mine, HALF)], wo.at[pl.ds(core * 256, 256), :])
    lf1 = local("f1", fc1_hbm, f1)
    lf2 = local("f2", fc2_hbm.at[:, pl.ds(mine, HALF)], f2)

    pl.semaphore_wait(barrier, count)

    class Gather:
        def __init__(self, name, ref, width, hz):
            self.name, self.ref, self.width = name, ref, width
            self.slots = {
                "h": hz * 4 + xx,
                "hr": hz * 4 + right_x,
                "hl": hz * 4 + left_x,
                "hf": hz * 4 + far_x,
                "k": (1 - hz) * 4 + xx,
                "kr": (1 - hz) * 4 + right_x,
                "kl": (1 - hz) * 4 + left_x,
                "kf": (1 - hz) * 4 + far_x,
            }
            self.sent = []

        def view(self, slot, part_):
            ref = self.ref.at[self.slots[slot]]
            if part_ is not None:
                ref = ref.at[:, pl.ds(part_ * (self.width // 2), self.width // 2)]
            return ref

        def send(self, tag, slot, to, part_=None):
            ref = self.view(slot, part_)
            self.sent.append((sems(self.name, tag), ref))
            remote((self.name, tag), ref, ref, to)

        def got(self, tag, slot, part_=None):
            arrive((self.name, tag), self.view(slot, part_))

        def start(self):
            self.sent = []
            self.send("r1", "h", right)
            self.send("l1", "h", left)
            self.send("z", "h", zmate)

        def second(self):
            self.got("z", "k")
            self.send("r2", "k", right)
            self.send("l2", "k", left)

        def third(self):
            self.got("r1", "hl")
            self.send("fr1", "hl", right, 0)
            self.got("l1", "hr")
            self.send("fl1", "hr", left, 1)

        def fourth(self):
            self.got("r2", "kl")
            self.send("fr2", "kl", right, 0)
            self.got("l2", "kr")
            self.send("fl2", "kr", left, 1)

        def last(self):
            self.got("fr1", "hf", 0)
            self.got("fl1", "hf", 1)
            self.got("fr2", "kf", 0)
            self.got("fl2", "kf", 1)

        def rest(self):
            self.second()
            self.third()
            self.fourth()
            self.last()

        def drain(self):
            for number, ref in self.sent:
                pltpu.make_async_copy(ref, ref, send_sem.at[number]).wait()

    class Scatter:
        def __init__(self, m, rows):
            self.m, self.rows, self.sent = m, rows, []

        def block(self, z, x, cols=None):
            cols = slice(None) if cols is None else pl.ds(cols * 256, 256)
            return part.at[self.m, z * 4 + x, pl.ds(0, self.rows), cols]

        def one(self, side, z):
            return r1.at[self.m, side, z, pl.ds(0, self.rows), :]

        def two(self, side, z):
            return r2.at[self.m, side, z, pl.ds(0, self.rows), :]

        def three(self, ref):
            return ref.at[self.m, pl.ds(0, self.rows), :]

        def first(self, z):
            self.sent.append(
                remote(("s1r", self.m, z), self.block(z, far_x, 0), self.one(0, z), right)
            )
            self.sent.append(
                remote(("s1l", self.m, z), self.block(z, far_x, 1), self.one(1, z), left)
            )

        def second(self, z):
            arrive(("s1r", self.m, z), self.one(0, z))
            ref = self.block(z, right_x, 0)
            ref[...] = (ref[...].astype(F32) + self.one(0, z)[...].astype(F32)).astype(BF16)
            self.sent.append(
                remote(("s2r", self.m, z), self.block(z, right_x), self.two(0, z), right)
            )
            arrive(("s1l", self.m, z), self.one(1, z))
            ref = self.block(z, left_x, 1)
            ref[...] = (ref[...].astype(F32) + self.one(1, z)[...].astype(F32)).astype(BF16)
            self.sent.append(
                remote(("s2l", self.m, z), self.block(z, left_x), self.two(1, z), left)
            )

        def total(self, z):
            return (
                self.block(z, xx)[...].astype(F32)
                + self.two(0, z)[...].astype(F32)
                + self.two(1, z)[...].astype(F32)
            )

        def third(self):
            for z in range(2):
                arrive(("s2r", self.m, z), self.two(0, z))
                arrive(("s2l", self.m, z), self.two(1, z))
            self.three(r3_send)[...] = self.total(1 - zl).astype(BF16)
            self.sent.append(
                remote(("s3", self.m), self.three(r3_send), self.three(r3), zmate)
            )
            self.three(xsum)[...] = self.total(zl)

        def result(self):
            arrive(("s3", self.m), self.three(r3))
            return self.three(xsum)[...] + self.three(r3)[...].astype(F32)

        def drain(self):
            for copy in self.sent:
                copy.wait_send()

    sent = []
    tg_gathers = {m: Gather(("tg", m), tg.at[m], 1024, zl) for m in range(2)}
    upper = phase == 1

    @pl.when(upper)
    def _():
        for m in (1, 0):
            copy = local(("tg", m), tg_hbm.at[m, core], tg.at[m, ten])
            copy.wait()
            tg_gathers[m].start()

    sent.append(remote(("x",), x_hbm.at[:, pl.ds(theirs, HALF)], xb.at[core], sibling))
    sent.append(remote(("wq",), wq_hbm.at[pl.ds(theirs, HALF), :], w3.at[core], sibling))
    sent.append(
        remote(
            ("wkv",),
            wkv_hbm.at[pl.ds(theirs, HALF), :],
            w3.at[2, :, pl.ds(core * HEAD, HEAD)],
            sibling,
        )
    )
    sent.append(
        remote(
            ("wo",),
            wo_hbm.at[:, pl.ds(theirs, HALF)],
            wo.at[pl.ds(core * 256, 256), :],
            sibling,
        )
    )

    for i in range(8):
        pair = gain_ref[:, pl.ds(pl.multiple_of(mine + i * BLK, BLK), BLK)]
        gb[i] = jnp.where(upper, pair[1:2, :], pair[0:1, :])

    lx.wait()
    acc = jnp.zeros((SEQ, 1), F32)

    def square(i, acc):
        v = xo[:, pl.ds(pl.multiple_of(i * 1024, 1024), 1024)].astype(F32)
        return acc + jnp.sum(v * v, axis=1, keepdims=True)

    acc = lax.fori_loop(0, 8, square, acc)
    sc[core] = jnp.broadcast_to(lax.rsqrt(acc / WIDTH + EPS_RMS), (SEQ, HEAD))
    sent.append(remote(("sc",), sc.at[core], sc.at[core], sibling))

    for q in range(4):
        v = patches_ref[:, q * CTX : (q + 1) * CTX].astype(F32)
        v = v - jnp.mean(v, axis=1, keepdims=True)
        inv = lax.rsqrt(jnp.mean(v * v, axis=1, keepdims=True) + EPS_LN)
        pu[core, q] = v * inv
        iv[core, q] = jnp.broadcast_to(inv, (24, HEAD))
    sent.append(remote(("pu",), pu.at[core], pu.at[core], sibling))
    sent.append(remote(("iv",), iv.at[core], iv.at[core], sibling))

    @pl.when(upper)
    def _():
        for m in (1, 0):
            tg_gathers[m].second()
            tg_gathers[m].third()

    lxh.wait()
    lq.wait()
    lkv.wait()
    arrive(("x",), xb.at[1 - core])
    arrive(("sc",), sc.at[1 - core])
    arrive(("wq",), w3.at[1 - core])
    arrive(("wkv",), w3.at[2, :, pl.ds((1 - core) * HEAD, HEAD)])
    own_p[...] = jnp.zeros_like(own_p)

    def project(i):
        cols = pl.ds(pl.multiple_of(i * BLK, BLK), BLK)
        rows = [
            (xb[m, :, cols].astype(F32) * sc[m][:, 0:1] * gb[i]).astype(BF16) for m in range(2)
        ]
        normed = jnp.concatenate(rows, axis=0)
        for j in range(3):
            own_p[:, j * 256 : (j + 1) * 256] += nn(normed, w3[j, cols, :])

    each(8, project)
    sent.append(remote(("p",), own_p, other_p, sibling))

    @pl.when(upper)
    def _():
        for m in (1, 0):
            tg_gathers[m].fourth()

    arrive(("p",), other_p)
    pf[...] = own_p[...] + other_p[...]

    lane = lax.broadcasted_iota(jnp.int32, (SEQ, HEAD), 1)
    low = lane < 64

    def rope(v, direction):
        return v * cos_ref[...] + direction * pltpu.roll(v, 64, 1) * sin_ref[...]

    def stacked(v):
        return jnp.concatenate([v[:, h * HEAD : (h + 1) * HEAD] for h in range(4)], axis=0)

    def forward(m):
        rows = pf[m * SEQ : (m + 1) * SEQ, :]
        q = jnp.concatenate(
            [rope(rows[:, h * HEAD : (h + 1) * HEAD], 1.0) for h in range(4)], axis=0
        ).astype(BF16)
        kv0 = rows[:, 512:640].astype(BF16).astype(F32)
        kv1 = rows[:, 640:768].astype(BF16).astype(F32)
        k = rope(jnp.where(low, kv0, pltpu.roll(kv1, 64, 1)), 1.0).astype(BF16)
        v = jnp.where(low, pltpu.roll(kv0, 64, 1), kv1).astype(BF16)
        qs[m] = q
        ks[m] = k
        vs[m] = v
        scores = nt(q, k) * FACTOR
        seg = seg_ref[m : m + 1, :].astype(F32)
        seg_col = to_column(seg)
        index_row = lax.broadcasted_iota(jnp.int32, (SEQ, SEQ), 0)
        index_col = lax.broadcasted_iota(jnp.int32, (SEQ, SEQ), 1)
        allowed = jnp.where((index_col <= index_row) & (seg_col == seg), 1.0, 0.0)
        allowed = jnp.concatenate([allowed] * 4, axis=0) > 0.5
        scores = jnp.where(allowed, scores, -1e30)
        top = jnp.max(scores, axis=1, keepdims=True)
        weights = jnp.where(allowed, jnp.exp(scores - top), 0.0)
        probs[m] = weights / jnp.sum(weights, axis=1, keepdims=True)

    for m in (1, 0):
        forward(m)

    def head_grads(m):
        gx_own[m] = jnp.zeros((SEQ, 512), F32)

        def step(i):
            cols = pl.ds(pl.multiple_of(i * BLK, BLK), BLK)
            gx_own[m] += nt(inc[m, i], wo[:, cols])

        each(8, step)
        return remote(("gx", m), gx_own.at[m], gx_other.at[m], sibling)

    def backward(m):
        arrive(("gx", m), gx_other.at[m])
        go = stacked(gx_own[m] + gx_other[m]).astype(BF16)
        pr = probs[m]
        gp = nt(go, vs[m])
        delta = jnp.sum(pr * gp, axis=1, keepdims=True)
        gs = (pr * (gp - delta) * FACTOR).astype(BF16)
        gq = nn(gs, ks[m])
        gk = rope(tn(gs, qs[m]), -1.0)
        gv = tn(pr.astype(BF16), go)
        pieces = [rope(gq[h * SEQ : (h + 1) * SEQ, :], -1.0) for h in range(4)]
        pieces.append(jnp.where(low, gk, pltpu.roll(gv, 64, 1)))
        pieces.append(jnp.where(low, pltpu.roll(gk, 64, 1), gv))
        inner = jnp.zeros((SEQ, 1), F32)
        for h in range(6):
            low_piece = pieces[h].astype(BF16)
            acts[m, :, h * HEAD : (h + 1) * HEAD] = low_piece
            inner += jnp.sum(
                low_piece.astype(F32) * pf[m * SEQ : (m + 1) * SEQ, h * HEAD : (h + 1) * HEAD],
                axis=1,
                keepdims=True,
            )
        row = to_row(inner / WIDTH)
        ins[m, :, 0:SEQ] = jnp.broadcast_to(row, (8, SEQ))
        out = []
        for o in range(1, 8):
            to = lax.rem(ten + o, 8)
            out.append(remote(("in", m, o), ins.at[m], inr.at[m, ten], device(t=to)))
        return out

    def inner_row(m):
        total = ins[m, 0:1, 0:SEQ]
        for o in range(1, 8):
            src = lax.rem(ten + 8 - o, 8)
            arrive(("in", m, o), inr.at[m, src])
            total += inr[m, src, 0:1, 0:SEQ]
        return total

    def back_project(m, z, x, left_side):
        i = z * 4 + x
        rows = pl.ds(pl.multiple_of(i * BLK, BLK), BLK)
        acc = nt(left_side[:, 0:256], w3[0, rows, :])
        acc += nt(left_side[:, 256:512], w3[1, rows, :])
        acc += nt(left_side[:, 512:768], w3[2, rows, :])
        part[m, i, pl.ds(0, left_side.shape[0]), :] = acc.astype(BF16)

    def scatter_first(m, rows, left_side):
        s = Scatter(m, rows)
        for z in range(2):
            back_project(m, z, far_x, left_side)
            s.first(z)
        for x in (right_x, left_x, xx):
            for z in range(2):
                back_project(m, z, x, left_side)
        return s

    def merger_forward():
        lf1.wait()
        lf2.wait()
        arrive(("pu",), pu.at[1 - core])
        arrive(("iv",), iv.at[1 - core])
        gain = lng_ref[...]
        bias = lnb_ref[...]
        hidden = jnp.zeros((VIS, PIECE), F32)
        for q in range(4):
            n = jnp.concatenate([pu[0, q], pu[1, q]], axis=0)
            low_n = (n * gain + bias).astype(BF16)
            mn[:, q * CTX : (q + 1) * CTX] = low_n
            for j in range(4):
                mns[q * 4 + j, :, 0:PIECE] = low_n[:, j * PIECE : (j + 1) * PIECE]
            hidden += nt(low_n, f1[:, q * CTX : (q + 1) * CTX])
            lgb[q] = gain[:, q * PIECE : (q + 1) * PIECE]
        for q in range(2):
            n = jnp.concatenate([pu[0, 2 * core + q], pu[1, 2 * core + q]], axis=0)
            for j in range(4):
                nblk[q * 4 + j] = n[:, j * PIECE : (j + 1) * PIECE]
        hidden += fc1b_ref[...]
        cdf = 0.5 * (1.0 + lax.erf(hidden * 0.7071067811865476))
        density = jnp.exp(-0.5 * hidden * hidden) * 0.3989422804014327
        slope[...] = cdf + hidden * density
        act[:, 0:PIECE] = (hidden * cdf).astype(BF16)
        spread("mn", lambda k: mns.at[8 * core + k], mnr)
        spread("act", lambda k: act, actr)

    my_slot = dp * 2 + phase

    def target(k):
        return (2 * core + k // 4, (k // 2) % 2 * 2 + k % 2, ten)

    def is_self(k):
        to = target(k)
        return (to[0] == dp) & (to[1] == pipe)

    def spread(name, source, slots):
        for k in range(8):
            number = sems(name, k)

            def send(k=k, number=number):
                pltpu.make_async_remote_copy(
                    src_ref=source(k),
                    dst_ref=slots.at[my_slot],
                    send_sem=send_sem.at[number],
                    recv_sem=recv_sem.at[sems(name, "got") + my_slot],
                    device_id=target(k),
                    device_id_type=MESH,
                ).start()

            def keep(k=k, number=number):
                pltpu.make_async_copy(
                    source(k), slots.at[my_slot], recv_sem.at[sems(name, "got") + my_slot]
                ).start()

            pl.when(jnp.logical_not(is_self(k)))(send)
            pl.when(is_self(k))(keep)

    def spread_numbers():
        for name in ("mn", "act", "gp", "vis"):
            sems(name, "got")
            for i in range(1, 8):
                sems(name, "got+", i)
            for k in range(8):
                sems(name, k)

    spread_numbers()

    def collect(name, slots):
        for i in range(8):
            pltpu.make_async_copy(
                slots.at[i], slots.at[i], recv_sem.at[sems(name, "got") + i]
            ).wait()

    def drain_spread(name, source):
        for k in range(8):
            number = sems(name, k)

            @pl.when(jnp.logical_not(is_self(k)))
            def _(k=k, number=number):
                pltpu.make_async_copy(source(k), source(k), send_sem.at[number]).wait()

    vis_gather = Gather(("vis",), vis, BLK, jnp.where(upper, 1 - zl, zl))

    @pl.when(upper)
    def _():
        out = []
        scatters = {}
        for m in (1, 0):
            tg_gathers[m].last()
            flat = tg[m].reshape(8 * 48, 1024)
            for e in range(4):
                wide = nn(tgsel_ref[e], flat).astype(BF16)
                inc[m, 2 * e] = wide[:, 0:BLK]
                inc[m, 2 * e + 1] = wide[:, BLK : 2 * BLK]
            if m == 1:
                lo.wait()
                arrive(("wo",), wo.at[pl.ds((1 - core) * 256, 256), :])
            out.append(head_grads(m))
            out.extend(backward(m))
            scatters[m] = scatter_first(m, SEQ, acts[m])

        for m in (1, 0):
            for z in range(2):
                scatters[m].second(z)
            scatters[m].third()
        for m in (1, 0):
            total = scatters[m].result()
            inner = to_column(inner_row(m))
            scale = sc[m][:, 0:1]
            cols = pl.ds(pl.multiple_of(ten * BLK, BLK), BLK)
            unit = xb[m, :, cols].astype(F32) * scale
            w = total * gb[ten]
            out_block[m] = (inc[m, ten].astype(F32) + scale * (w - unit * inner)).astype(BF16)
            out.append(remote(("down", m), out_block.at[m], inc.at[m, ten], cross))
        merger_forward()
        for copy in out:
            copy.wait_send()
        for m in (1, 0):
            tg_gathers[m].drain()
            scatters[m].drain()
        arrive(("up",), vis.at[(1 - zl) * 4 + xx])
        vis_gather.start()
        vis_gather.rest()
        vis_gather.drain()

    @pl.when(jnp.logical_not(upper))
    def _():
        merger_forward()
        lo.wait()
        arrive(("wo",), wo.at[pl.ds((1 - core) * 256, 256), :])
        out = []
        gathers = {m: Gather(("inc", m), inc.at[m], BLK, 1 - zl) for m in range(2)}
        scatters = {}
        picks = {}
        for m in (1, 0):
            arrive(("down", m), inc.at[m, (1 - zl) * 4 + xx])
            gathers[m].start()
            gathers[m].rest()
            out.append(head_grads(m))
            out.extend(backward(m))
            wide = lax.broadcasted_iota(jnp.int32, (VIS, SEQ), 0) + m * VIS
            across = lax.broadcasted_iota(jnp.int32, (VIS, SEQ), 1)
            tokens = jnp.sum(
                jnp.where(across == wide, pos_ref[...], 0), axis=1, keepdims=True
            )
            picks[m] = (tokens - m * SEQ) == across
            pick = jnp.where(picks[m], 1.0, 0.0).astype(BF16)
            scatters[m] = scatter_first(m, VIS, nn(pick, acts[m]).astype(BF16))
        for m in (1, 0):
            for z in range(2):
                scatters[m].second(z)
            scatters[m].third()
        for m in (1, 0):
            total = scatters[m].result()
            mask = picks[m]
            pick = jnp.where(mask, 1.0, 0.0).astype(BF16)
            inner = jnp.sum(jnp.where(mask, inner_row(m), 0.0), axis=1, keepdims=True)
            scale_row = to_row(sc[m][:, 0:1])
            scale = jnp.sum(jnp.where(mask, scale_row, 0.0), axis=1, keepdims=True)
            cols = pl.ds(pl.multiple_of(ten * BLK, BLK), BLK)
            unit = nn(pick, xb[m, :, cols]) * scale
            w = total * gb[ten]
            block = (nn(pick, inc[m, ten]) + scale * (w - unit * inner)).astype(BF16)
            if m == 1:
                out_block[0, 0:VIS, :] = block
                out.append(
                    remote(("up",), out_block.at[0, pl.ds(0, VIS), :], vis.at[ten], cross)
                )
            else:
                vis[ten] = block
        vis_gather.start()
        vis_gather.rest()
        for copy in out:
            copy.wait_send()
        for m in (1, 0):
            gathers[m].drain()
            scatters[m].drain()
        vis_gather.drain()

    spread("vis", lambda k: vis.at[k], visr)
    ga_own[...] = jnp.zeros_like(ga_own)
    for i in range(8):
        ga_own[...] += nt(vis[i], f2[:, i * BLK : (i + 1) * BLK])
    sent.append(remote(("ga",), ga_own, ga_other, sibling))
    arrive(("ga",), ga_other)
    grad_pre = ((ga_own[...] + ga_other[...]) * slope[...]).astype(BF16)
    gpre[:, 0:PIECE] = grad_pre
    spread("gp", lambda k: gpre, gpr)
    stat_lane = lax.broadcasted_iota(jnp.int32, (VIS, LANES - PIECE), 1)
    for q in range(2):
        cols = pl.ds(pl.multiple_of(core * 2 * CTX + q * CTX, CTX), CTX)
        gm = nn(grad_pre, f1[:, cols])
        u = gm * lng_ref[...]
        n = jnp.concatenate([pu[0, 2 * core + q], pu[1, 2 * core + q]], axis=0)
        s1 = jnp.sum(u, axis=1, keepdims=True)
        s2 = jnp.sum(u * n, axis=1, keepdims=True)
        h1 = s1.astype(BF16).astype(F32)
        h2 = s2.astype(BF16).astype(F32)
        stats = jnp.where(
            stat_lane == 0,
            h1,
            jnp.where(
                stat_lane == 1,
                s1 - h1,
                jnp.where(stat_lane == 2, h2, jnp.where(stat_lane == 3, s2 - h2, 0.0)),
            ),
        ).astype(BF16)
        for j in range(4):
            pgp[q * 4 + j, :, 0:PIECE] = gm[:, j * PIECE : (j + 1) * PIECE].astype(BF16)
            pgp[q * 4 + j, :, PIECE:LANES] = stats
    for o in range(1, 8):
        to = lax.rem(ten + o, 8)
        sent.append(remote(("pg", o), pgp.at[to], pgpr.at[ten], device(t=to)))

    collect("act", actr)
    collect("vis", visr)
    fc2_out[...] = tn(
        actr[...].reshape(8 * VIS, LANES)[:, 0:PIECE], visr[...].reshape(8 * VIS, BLK)
    )

    total = pgp[ten].astype(F32)
    for o in range(1, 8):
        src = lax.rem(ten + 8 - o, 8)
        arrive(("pg", o), pgpr.at[src])
        total += pgpr[src].astype(F32)
    s1 = (total[:, PIECE : PIECE + 1] + total[:, PIECE + 1 : PIECE + 2]) / CTX
    s2 = (total[:, PIECE + 2 : PIECE + 3] + total[:, PIECE + 3 : PIECE + 4]) / CTX
    patch = 2 * core + zl
    inv = jnp.concatenate([iv[0, patch], iv[1, patch]], axis=0)[:, 0:1]
    block = inv * (total[:, 0:PIECE] * lgb[xx] - s1 - nblk[ten] * s2)
    for b in range(2):
        rows = jnp.concatenate(
            [block[b * 24 : (b + 1) * 24, :], jnp.zeros((8, PIECE), F32)], axis=0
        )
        pgs[b, :, 0:PIECE] = rows.astype(BF16)
    my_code = core * 8 + ten
    for o in range(1, 16):
        code = lax.rem(my_code + o, 16)
        sent.append(
            remote(
                ("po", o),
                pgs.at[code // 8],
                pgr.at[my_code],
                device(b=code // 8, t=lax.rem(code, 8)),
            )
        )
    pgr[my_code] = pgs[core]

    collect("mn", mnr)
    collect("gp", gpr)
    fc1_out[...] = tn(
        mnr[...].reshape(8 * VIS, LANES)[:, 0:PIECE], gpr[...].reshape(8 * VIS, LANES)[:, 0:PIECE]
    )
    for o in range(1, 16):
        arrive(("po", o), pgr.at[lax.rem(my_code + 16 - o, 16)])
    pg_out[...] = pgr[...]

    for copy in sent:
        copy.wait_send()
    drain_spread("mn", lambda k: mns.at[8 * core + k])
    drain_spread("act", lambda k: act)
    drain_spread("gp", lambda k: gpre)
    drain_spread("vis", lambda k: vis.at[k])


def tables():
    freq = THETA ** (-(2.0 * np.arange(64, dtype=np.float64)) / HEAD)
    angles = np.arange(SEQ, dtype=np.float64)[:, None] * freq[None, :]
    cosine, sine = np.cos(angles), np.sin(angles)
    pick = np.zeros((4, SEQ, 8 * 48), np.float32)
    for e in range(4):
        for t in range(8):
            for i in range(12):
                pick[e, t * 12 + i, t * 48 + e * 12 + i] = 1.0
    return (
        np.concatenate([cosine, cosine], axis=1).astype(np.float32),
        np.concatenate([-sine, sine], axis=1).astype(np.float32),
        pick,
    )


def local(
    lm_inputs,
    top_grad,
    phase_gain,
    query_weight,
    kv_weight,
    out_weight,
    segment_ids,
    visual_pos,
    patches,
    ln_gain,
    ln_bias,
    fc1_weight,
    fc1_bias,
    fc2_weight,
):
    cosine, sine, pick = tables()
    shards = top_grad[0].reshape(2, 12, 2, 4, 1024).transpose(0, 2, 3, 1, 4)
    shards = shards.reshape(2, 2, 48, 1024)
    vmem = pl.BlockSpec(memory_space=pltpu.VMEM)
    hbm = pl.BlockSpec(memory_space=pl.ANY)
    v = pltpu.VMEM
    pg, fc1_grad, fc2_grad = pl.pallas_call(
        kernel,
        out_shape=(
            jax.ShapeDtypeStruct((16, 32, LANES), BF16),
            jax.ShapeDtypeStruct((PIECE, PIECE), F32),
            jax.ShapeDtypeStruct((PIECE, BLK), F32),
        ),
        in_specs=[
            hbm, hbm, vmem, hbm, hbm, hbm, vmem, vmem, vmem, vmem, vmem, hbm, vmem, hbm,
            vmem, vmem, vmem,
        ],
        out_specs=(vmem, vmem, vmem),
        scratch_shapes=[
            v((3, HALF, 256), BF16),
            v((512, HALF), BF16),
            v((PIECE, 4 * CTX), BF16),
            v((PIECE, HALF), BF16),
            v((SEQ, WIDTH), BF16),
            v((2, SEQ, HALF), BF16),
            v((2, SEQ, HEAD), F32),
            v((8, 1, BLK), F32),
            v((2, 8, 48, 1024), BF16),
            v((2, 8, SEQ, BLK), BF16),
            v((2 * SEQ, 768), F32),
            v((2 * SEQ, 768), F32),
            v((2 * SEQ, 768), F32),
            v((2, 4 * SEQ, HEAD), BF16),
            v((2, SEQ, HEAD), BF16),
            v((2, SEQ, HEAD), BF16),
            v((2, 4 * SEQ, SEQ), F32),
            v((2, SEQ, 512), F32),
            v((2, SEQ, 512), F32),
            v((2, SEQ, 768), BF16),
            v((2, 8, HEAD), F32),
            v((2, 8, 8, HEAD), F32),
            v((2, 8, SEQ, BLK), BF16),
            v((2, 2, 2, SEQ, 256), BF16),
            v((2, 2, 2, SEQ, BLK), BF16),
            v((2, SEQ, BLK), BF16),
            v((2, SEQ, BLK), BF16),
            v((2, SEQ, BLK), F32),
            v((2, SEQ, BLK), BF16),
            v((8, VIS, BLK), BF16),
            v((2, 4, 24, CTX), F32),
            v((2, 4, 24, HEAD), F32),
            v((VIS, 4 * CTX), BF16),
            v((16, VIS, LANES), BF16),
            v((VIS, LANES), BF16),
            v((VIS, PIECE), F32),
            v((8, VIS, PIECE), F32),
            v((4, 1, PIECE), F32),
            v((VIS, PIECE), F32),
            v((VIS, PIECE), F32),
            v((VIS, LANES), BF16),
            v((8, VIS, LANES), BF16),
            v((8, VIS, LANES), BF16),
            v((8, VIS, LANES), BF16),
            v((8, VIS, BLK), BF16),
            v((8, VIS, LANES), BF16),
            v((8, VIS, LANES), BF16),
            v((2, 32, LANES), BF16),
            v((16, 32, LANES), BF16),
            pltpu.SemaphoreType.DMA((192,)),
            pltpu.SemaphoreType.DMA((192,)),
            pltpu.SemaphoreType.DMA((12,)),
        ],
        compiler_params=pltpu.CompilerParams(
            collective_id=0, has_side_effects=True, vmem_limit_bytes=60 * 1024 * 1024
        ),
    )(
        lm_inputs[0, 0],
        shards,
        phase_gain,
        query_weight.reshape(WIDTH, 256),
        kv_weight.reshape(WIDTH, HEAD),
        out_weight.reshape(256, WIDTH),
        segment_ids[0],
        visual_pos,
        patches[0],
        ln_gain.reshape(1, CTX),
        ln_bias.reshape(1, CTX),
        fc1_weight.T,
        fc1_bias.reshape(1, PIECE),
        fc2_weight,
        cosine,
        sine,
        jnp.asarray(pick, BF16),
    )
    patch_grad = pg[:, 0:24, 0:PIECE].transpose(1, 0, 2).reshape(1, 24, 4 * CTX)
    return (patch_grad, fc1_grad, fc2_grad.T)


def solution(mesh):
    in_specs = (
        P("dp", "pipe", None, None),
        P("dp", None, "tensor", None),
        P(),
        P("pipe", None, "tensor", None),
        P("pipe", None, "tensor", None),
        P("pipe", "tensor", None, None),
        P("dp", None, None),
        P("dp", None),
        P("dp", "pipe", None),
        P(),
        P(),
        P(None, "tensor"),
        P("tensor"),
        P("tensor", None),
    )
    out_specs = (P("dp", "pipe", None), P(("dp", "pipe"), "tensor"), P(("dp", "pipe"), "tensor"))
    return jax.shard_map(local, mesh=mesh, in_specs=in_specs, out_specs=out_specs, check_vma=False)
```

```python
import functools

import jax
import jax.numpy as jnp
import numpy as np
from jax import lax
from jax.experimental import pallas as pl
from jax.experimental.pallas import tpu as pltpu
from jax.sharding import PartitionSpec as P

EPS_RMS = 1e-06
EPS_LN = 1e-06
THETA = 1000000.0
MESH = pl.DeviceIdType.MESH
F32 = jnp.float32
BF16 = jnp.bfloat16
SEQ = 96
WIDTH = 8192
HALF = 4096
BLK = 512
HEAD = 128
FACTOR = HEAD**-0.5
VIS = 48
CTX = 1280
PIECE = 320
LANES = 384


def nn(a, b):
    return lax.dot_general(a, b, (((1,), (0,)), ((), ())), preferred_element_type=F32)


def nt(a, b):
    return lax.dot_general(a, b, (((1,), (1,)), ((), ())), preferred_element_type=F32)


def tn(a, b):
    return lax.dot_general(a, b, (((0,), (0,)), ((), ())), preferred_element_type=F32)


def each(count, body):
    def step(i, carry):
        body(i)
        return carry

    lax.fori_loop(0, count, step, 0)


def eye_mask(size):
    return lax.broadcasted_iota(jnp.int32, (size, size), 0) == lax.broadcasted_iota(
        jnp.int32, (size, size), 1
    )


def to_row(column):
    size = column.shape[0]
    return jnp.sum(jnp.where(eye_mask(size), column, 0.0), axis=0, keepdims=True)


def to_column(row):
    size = row.shape[1]
    return jnp.sum(jnp.where(eye_mask(size), row, 0.0), axis=1, keepdims=True)


class Sems:
    def __init__(self):
        self.numbers = {}

    def __call__(self, *name):
        return self.numbers.setdefault(name, len(self.numbers))


def kernel(
    x_hbm,
    tg_hbm,
    gain_ref,
    wq_hbm,
    wkv_hbm,
    wo_hbm,
    seg_ref,
    pos_ref,
    patches_ref,
    lng_ref,
    lnb_ref,
    fc1_hbm,
    fc1b_ref,
    fc2_hbm,
    cos_hbm,
    sin_hbm,
    tgsel_hbm,
    pg_out,
    fc1_out,
    fc2_out,
    cos_ref,
    sin_ref,
    tgsel_ref,
    fc1_val,
    fc2_val,
    w3,
    wo,
    f1,
    f2,
    xo,
    xb,
    sc,
    gb,
    tg,
    inc,
    own_p,
    other_p,
    pf,
    qs,
    ks,
    vs,
    probs,
    gx_own,
    gx_other,
    acts,
    ins,
    inr,
    part,
    r1,
    out_block,
    vis,
    pu,
    iv,
    mn,
    mns,
    act,
    slope,
    nblk,
    lgb,
    ga_own,
    ga_other,
    gpre,
    mnr,
    actr,
    gpr,
    visr,
    pgp,
    pgpr,
    pgs,
    pgr,
    send_sem,
    recv_sem,
    local_sem,
    y_sem,
):
    dp = lax.axis_index("dp")
    pipe = lax.axis_index("pipe")
    ten = lax.axis_index("tensor")
    phase = pipe // 2
    core = pipe % 2
    zl = ten // 4
    xx = ten % 4
    sems = Sems()
    locals_ = Sems()

    def device(s=None, b=None, z=None, x=None, d=None, t=None):
        s = phase if s is None else s
        b = core if b is None else b
        if t is None:
            t = (zl if z is None else z) * 4 + (xx if x is None else x)
        return (dp if d is None else d, 2 * s + b, t)

    sibling = device(b=1 - core)
    cross = device(s=1 - phase, z=1 - zl)

    barrier = pltpu.get_barrier_semaphore()
    up_y = device(d=lax.rem(dp + 1, 4))
    down_y = device(d=lax.rem(dp + 3, 4))
    greeted = [sibling, up_y, down_y, device(s=1 - phase)]
    greeted += [device(t=lax.rem(ten + o, 8)) for o in range(1, 8)]
    greeted += [device(s=1 - phase, z=1 - zl, x=lax.rem(xx + o, 4)) for o in range(4)]
    for to in greeted:
        pl.semaphore_signal(barrier, inc=1, device_id=to, device_id_type=MESH)

    def local(name, src, dst):
        copy = pltpu.make_async_copy(src, dst, local_sem.at[locals_(name)])
        copy.start()
        return copy

    def remote(name, src, dst, to):
        number = sems(*name)
        copy = pltpu.make_async_remote_copy(
            src_ref=src,
            dst_ref=dst,
            send_sem=send_sem.at[number],
            recv_sem=recv_sem.at[number],
            device_id=to,
            device_id_type=MESH,
        )
        copy.start()
        return copy

    def arrive(name, ref):
        pltpu.make_async_copy(ref, ref, recv_sem.at[sems(*name)]).wait()

    mine = core * HALF
    theirs = (1 - core) * HALF
    lx = local("x", x_hbm, xo)
    lxh = local("xh", x_hbm.at[:, pl.ds(mine, HALF)], xb.at[core])
    lq = local("q", wq_hbm.at[pl.ds(mine, HALF), :], w3.at[core])
    lkv = local(
        "kv", wkv_hbm.at[pl.ds(mine, HALF), :], w3.at[2, :, pl.ds(core * HEAD, HEAD)]
    )
    lo = local("o", wo_hbm.at[:, pl.ds(mine, HALF)], wo.at[pl.ds(core * 256, 256), :])
    lsel = local("sel", tgsel_hbm, tgsel_ref)
    lcos = local("cos", cos_hbm, cos_ref)
    lsin = local("sin", sin_hbm, sin_ref)
    lf1 = local("f1", fc1_hbm, f1)
    lf2 = local("f2", fc2_hbm.at[:, pl.ds(mine, HALF)], f2)

    pl.semaphore_wait(barrier, len(greeted))

    def peer(o):
        return lax.rem(ten + o, 8)

    def push(name, src, slots, slot, to=None):
        return [remote((name, o), src, slots.at[slot], device(t=peer(o))) for o in range(1, 8)]

    def terms(m):
        return r1.at[m]

    def send_terms(m, rows, left_side):
        out = []
        for o in list(range(1, 8)) + [0]:
            j = peer(o)
            cols = pl.ds(pl.multiple_of(j * BLK, BLK), BLK)
            acc = nt(left_side[:, 0:256], w3[0, cols, :])
            acc += nt(left_side[:, 256:512], w3[1, cols, :])
            acc += nt(left_side[:, 512:768], w3[2, cols, :])
            part[m, j, pl.ds(0, rows), :] = acc.astype(BF16)
            if o:
                out.append(
                    remote(
                        ("rs", m, o),
                        part.at[m, j, pl.ds(0, rows), :],
                        r1.at[m, ten, pl.ds(0, rows), :],
                        device(t=j),
                    )
                )
        return out

    def sum_terms(m, rows):
        total = part[m, ten, pl.ds(0, rows), :].astype(F32)
        for o in range(1, 8):
            src = peer(8 - o)
            ref = r1.at[m, src, pl.ds(0, rows), :]
            arrive(("rs", m, o), ref)
            total += ref[...].astype(F32)
        return total

    sent = []
    upper = phase == 1
    lower = jnp.logical_not(upper)
    cut_at = 384

    for m in (1, 0):

        @pl.when(upper)
        def _(m=m):
            local(("tg", m), tg_hbm.at[m, core], tg.at[m, ten])
            for o in range(1, 4):
                remote(
                    ("tgx", m, o),
                    tg_hbm.at[m, core],
                    tg.at[m, ten],
                    device(x=lax.rem(xx + o, 4)),
                )
            for o in range(4):
                remote(
                    ("tgz", m, o),
                    tg_hbm.at[m, core, :, pl.ds(0, cut_at)],
                    tg.at[m, ten, :, pl.ds(0, cut_at)],
                    device(z=1 - zl, x=lax.rem(xx + o, 4)),
                )

        @pl.when(lower)
        def _(m=m):
            for o in range(4):
                remote(
                    ("tgc", m, o),
                    tg_hbm.at[m, core, :, pl.ds(cut_at, 1024 - cut_at)],
                    tg.at[m, ten, :, pl.ds(cut_at, 1024 - cut_at)],
                    device(s=1, z=1 - zl, x=lax.rem(xx + o, 4)),
                )

    def tg_wait(m):
        pltpu.make_async_copy(
            tg.at[m, ten], tg.at[m, ten], local_sem.at[locals_(("tg", m))]
        ).wait()
        for o in range(1, 4):
            arrive(("tgx", m, o), tg.at[m, zl * 4 + lax.rem(xx + 4 - o, 4)])
        for o in range(4):
            slot = (1 - zl) * 4 + lax.rem(xx + 4 - o, 4)
            arrive(("tgz", m, o), tg.at[m, slot, :, pl.ds(0, cut_at)])
            arrive(("tgc", m, o), tg.at[m, slot, :, pl.ds(cut_at, 1024 - cut_at)])

    def sent_wait(name, ref):
        pltpu.make_async_copy(ref, ref, send_sem.at[sems(*name)]).wait()

    def tg_drain():
        for m in (1, 0):

            @pl.when(upper)
            def _(m=m):
                for o in range(1, 4):
                    sent_wait(("tgx", m, o), tg_hbm.at[m, core])
                for o in range(4):
                    sent_wait(("tgz", m, o), tg_hbm.at[m, core, :, pl.ds(0, cut_at)])

            @pl.when(lower)
            def _(m=m):
                for o in range(4):
                    sent_wait(
                        ("tgc", m, o), tg_hbm.at[m, core, :, pl.ds(cut_at, 1024 - cut_at)]
                    )

    sent.append(remote(("x",), x_hbm.at[:, pl.ds(theirs, HALF)], xb.at[core], sibling))
    sent.append(remote(("wq",), wq_hbm.at[pl.ds(theirs, HALF), :], w3.at[core], sibling))
    sent.append(
        remote(
            ("wkv",),
            wkv_hbm.at[pl.ds(theirs, HALF), :],
            w3.at[2, :, pl.ds(core * HEAD, HEAD)],
            sibling,
        )
    )
    sent.append(
        remote(
            ("wo",),
            wo_hbm.at[:, pl.ds(theirs, HALF)],
            wo.at[pl.ds(core * 256, 256), :],
            sibling,
        )
    )

    for i in range(8):
        pair = gain_ref[:, pl.ds(pl.multiple_of(mine + i * BLK, BLK), BLK)]
        gb[i] = jnp.where(upper, pair[1:2, :], pair[0:1, :])

    lx.wait()
    acc = jnp.zeros((SEQ, 1), F32)

    def square(i, acc):
        v = xo[:, pl.ds(pl.multiple_of(i * 1024, 1024), 1024)].astype(F32)
        return acc + jnp.sum(v * v, axis=1, keepdims=True)

    acc = lax.fori_loop(0, 8, square, acc)
    sc[core] = jnp.broadcast_to(lax.rsqrt(acc / WIDTH + EPS_RMS), (SEQ, HEAD))
    sent.append(remote(("sc",), sc.at[core], sc.at[core], sibling))

    lxh.wait()
    lq.wait()
    lkv.wait()
    arrive(("x",), xb.at[1 - core])
    arrive(("sc",), sc.at[1 - core])
    arrive(("wq",), w3.at[1 - core])
    arrive(("wkv",), w3.at[2, :, pl.ds((1 - core) * HEAD, HEAD)])
    own_p[...] = jnp.zeros_like(own_p)

    def project(i):
        cols = pl.ds(pl.multiple_of(i * BLK, BLK), BLK)
        rows = [
            (xb[m, :, cols].astype(F32) * sc[m][:, 0:1] * gb[i]).astype(BF16) for m in range(2)
        ]
        normed = jnp.concatenate(rows, axis=0)
        for j in range(3):
            own_p[:, j * 256 : (j + 1) * 256] += nn(normed, w3[j, cols, :])

    each(8, project)
    sent.append(remote(("p",), own_p, other_p, sibling))

    arrive(("p",), other_p)
    pf[...] = own_p[...] + other_p[...]

    lane = lax.broadcasted_iota(jnp.int32, (SEQ, HEAD), 1)
    low = lane < 64

    def rope(v, direction):
        return v * cos_ref[...] + direction * pltpu.roll(v, 64, 1) * sin_ref[...]

    def stacked(v):
        return jnp.concatenate([v[:, h * HEAD : (h + 1) * HEAD] for h in range(4)], axis=0)

    def forward(m):
        rows = pf[m * SEQ : (m + 1) * SEQ, :]
        q = jnp.concatenate(
            [rope(rows[:, h * HEAD : (h + 1) * HEAD], 1.0) for h in range(4)], axis=0
        ).astype(BF16)
        kv0 = rows[:, 512:640].astype(BF16).astype(F32)
        kv1 = rows[:, 640:768].astype(BF16).astype(F32)
        k = rope(jnp.where(low, kv0, pltpu.roll(kv1, 64, 1)), 1.0).astype(BF16)
        v = jnp.where(low, pltpu.roll(kv0, 64, 1), kv1).astype(BF16)
        qs[m] = q
        ks[m] = k
        vs[m] = v
        scores = nt(q, k) * FACTOR
        seg = seg_ref[0, m : m + 1, :].astype(F32)
        seg_col = to_column(seg)
        index_row = lax.broadcasted_iota(jnp.int32, (SEQ, SEQ), 0)
        index_col = lax.broadcasted_iota(jnp.int32, (SEQ, SEQ), 1)
        allowed = jnp.where((index_col <= index_row) & (seg_col == seg), 1.0, 0.0)
        allowed = jnp.concatenate([allowed] * 4, axis=0) > 0.5
        scores = jnp.where(allowed, scores, -1e30)
        top = jnp.max(scores, axis=1, keepdims=True)
        weights = jnp.where(allowed, jnp.exp(scores - top), 0.0)
        probs[m] = weights / jnp.sum(weights, axis=1, keepdims=True)

    lcos.wait()
    lsin.wait()
    for m in (1, 0):
        forward(m)

    def head_grads(m, slots):
        acc = jnp.zeros((SEQ, 512), F32)
        for slot in slots():
            cols = pl.ds(pl.multiple_of(slot * BLK, BLK), BLK)
            acc += nt(inc[m, slot], wo[:, cols])
        gx_own[m] = acc
        return remote(("gx", m), gx_own.at[m], gx_other.at[m], sibling)

    def backward(m):
        arrive(("gx", m), gx_other.at[m])
        go = stacked(gx_own[m] + gx_other[m]).astype(BF16)
        pr = probs[m]
        gp = nt(go, vs[m])
        delta = jnp.sum(pr * gp, axis=1, keepdims=True)
        gs = (pr * (gp - delta) * FACTOR).astype(BF16)
        gq = nn(gs, ks[m])
        gk = rope(tn(gs, qs[m]), -1.0)
        gv = tn(pr.astype(BF16), go)
        pieces = [rope(gq[h * SEQ : (h + 1) * SEQ, :], -1.0) for h in range(4)]
        pieces.append(jnp.where(low, gk, pltpu.roll(gv, 64, 1)))
        pieces.append(jnp.where(low, pltpu.roll(gk, 64, 1), gv))
        inner = jnp.zeros((SEQ, 1), F32)
        for h in range(6):
            low_piece = pieces[h].astype(BF16)
            acts[m, :, h * HEAD : (h + 1) * HEAD] = low_piece
            inner += jnp.sum(
                low_piece.astype(F32) * pf[m * SEQ : (m + 1) * SEQ, h * HEAD : (h + 1) * HEAD],
                axis=1,
                keepdims=True,
            )
        row = to_row(inner / WIDTH)
        ins[m, :, 0:SEQ] = jnp.broadcast_to(row, (8, SEQ))
        out = []
        for o in range(1, 8):
            out.append(remote(("in", m, o), ins.at[m], inr.at[m, ten], device(t=peer(o))))
        return out

    def inner_row(m):
        total = ins[m, 0:1, 0:SEQ]
        for o in range(1, 8):
            src = peer(8 - o)
            arrive(("in", m, o), inr.at[m, src])
            total += inr[m, src, 0:1, 0:SEQ]
        return total

    def merger_forward():
        for q in range(4):
            v = patches_ref[0, :, q * CTX : (q + 1) * CTX].astype(F32)
            v = v - jnp.mean(v, axis=1, keepdims=True)
            inv = lax.rsqrt(jnp.mean(v * v, axis=1, keepdims=True) + EPS_LN)
            pu[core, q] = v * inv
            iv[core, q] = jnp.broadcast_to(inv, (24, HEAD))
        remote(("pu",), pu.at[core], pu.at[core], sibling)
        remote(("iv",), iv.at[core], iv.at[core], sibling)
        for name in ("y1", "y2"):
            number = ("y1", "y2").index(name)
            for to in (up_y, down_y):
                pl.semaphore_signal(y_sem.at[number], inc=1, device_id=to, device_id_type=MESH)
            pl.semaphore_wait(y_sem.at[number], 2)
        lf1.wait()
        lf2.wait()
        arrive(("pu",), pu.at[1 - core])
        arrive(("iv",), iv.at[1 - core])
        gain = lng_ref[...].reshape(1, CTX)
        bias = lnb_ref[...].reshape(1, CTX)
        hidden = jnp.zeros((VIS, PIECE), F32)
        for q in range(4):
            n = jnp.concatenate([pu[0, q], pu[1, q]], axis=0)
            low_n = (n * gain + bias).astype(BF16)
            mn[:, q * CTX : (q + 1) * CTX] = low_n
            for j in range(4):
                mns[q * 4 + j, :, 0:PIECE] = low_n[:, j * PIECE : (j + 1) * PIECE]
            hidden += nt(low_n, f1[:, q * CTX : (q + 1) * CTX])
            lgb[q] = gain[:, q * PIECE : (q + 1) * PIECE]
        for q in range(2):
            n = jnp.concatenate([pu[0, 2 * core + q], pu[1, 2 * core + q]], axis=0)
            for j in range(4):
                nblk[q * 4 + j] = n[:, j * PIECE : (j + 1) * PIECE]
        hidden += fc1b_ref[...].reshape(1, PIECE)
        cdf = 0.5 * (1.0 + lax.erf(hidden * 0.7071067811865476))
        density = jnp.exp(-0.5 * hidden * hidden) * 0.3989422804014327
        slope[...] = cdf + hidden * density
        act[:, 0:PIECE] = (hidden * cdf).astype(BF16)
        spread("mn", lambda k: mns.at[8 * core + k], mnr)
        spread("act", lambda k: act, actr)

    my_slot = dp * 2 + phase

    def target(k):
        return (2 * core + k // 4, (k // 2) % 2 * 2 + k % 2, ten)

    def is_self(k):
        to = target(k)
        return (to[0] == dp) & (to[1] == pipe)

    def spread(name, source, slots):
        for k in range(8):
            number = sems(name, k)

            def send(k=k, number=number):
                pltpu.make_async_remote_copy(
                    src_ref=source(k),
                    dst_ref=slots.at[my_slot],
                    send_sem=send_sem.at[number],
                    recv_sem=recv_sem.at[sems(name, "got") + my_slot],
                    device_id=target(k),
                    device_id_type=MESH,
                ).start()

            def keep(k=k, number=number):
                pltpu.make_async_copy(
                    source(k), slots.at[my_slot], recv_sem.at[sems(name, "got") + my_slot]
                ).start()

            pl.when(jnp.logical_not(is_self(k)))(send)
            pl.when(is_self(k))(keep)

    def spread_numbers():
        for name in ("mn", "act", "gp", "vis"):
            sems(name, "got")
            for i in range(1, 8):
                sems(name, "got+", i)
            for k in range(8):
                sems(name, k)

    spread_numbers()

    def collect(name, slots):
        for i in range(8):
            pltpu.make_async_copy(
                slots.at[i], slots.at[i], recv_sem.at[sems(name, "got") + i]
            ).wait()

    def drain_spread(name, source):
        for k in range(8):
            number = sems(name, k)

            @pl.when(jnp.logical_not(is_self(k)))
            def _(k=k, number=number):
                pltpu.make_async_copy(source(k), source(k), send_sem.at[number]).wait()

    @pl.when(upper)
    def _():
        out = []
        for m in (1, 0):
            tg_wait(m)
            if m == 1:
                lsel.wait()
                lo.wait()
                arrive(("wo",), wo.at[pl.ds((1 - core) * 256, 256), :])
            flat = tg[m].reshape(8 * 48, 1024)
            for e in range(4):
                wide = nn(tgsel_ref[e], flat).astype(BF16)
                inc[m, 2 * e] = wide[:, 0:BLK]
                inc[m, 2 * e + 1] = wide[:, BLK : 2 * BLK]
            out.append(head_grads(m, lambda: range(8)))
        for m in (1, 0):
            out.extend(backward(m))
            out.extend(send_terms(m, SEQ, acts[m]))
        for m in (1, 0):
            total = sum_terms(m, SEQ)
            inner = to_column(inner_row(m))
            scale = sc[m][:, 0:1]
            cols = pl.ds(pl.multiple_of(ten * BLK, BLK), BLK)
            unit = xb[m, :, cols].astype(F32) * scale
            w = total * gb[ten]
            out_block[m] = (inc[m, ten].astype(F32) + scale * (w - unit * inner)).astype(BF16)
            out.append(remote(("down", m), out_block.at[m], inc.at[m, ten], cross))
        merger_forward()
        for copy in out:
            copy.wait_send()
        for o in range(8):
            arrive(("up", o), vis.at[peer(8 - o)])

    @pl.when(lower)
    def _():
        merger_forward()
        lsel.wait()
        lo.wait()
        arrive(("wo",), wo.at[pl.ds((1 - core) * 256, 256), :])
        out = []
        held = (1 - zl) * 4 + xx

        def pass_on(m):
            arrive(("down", m), inc.at[m, held])
            out.extend(push(("inc", m), inc.at[m, held], inc.at[m], held))

        def blocks(m):
            yield held
            for o in range(1, 8):
                if m == 1 and o == 5:
                    pass_on(0)
                src = peer(8 - o)
                slot = lax.rem(src + 4, 8)
                arrive((("inc", m), o), inc.at[m, slot])
                yield slot

        pass_on(1)
        picks = {}
        for m in (1, 0):
            out.append(head_grads(m, lambda: blocks(m)))
            out.extend(backward(m))
            wide = lax.broadcasted_iota(jnp.int32, (VIS, SEQ), 0) + m * VIS
            across = lax.broadcasted_iota(jnp.int32, (VIS, SEQ), 1)
            tokens = jnp.sum(jnp.where(across == wide, pos_ref[...], 0), axis=1, keepdims=True)
            picks[m] = (tokens - m * SEQ) == across
            pick = jnp.where(picks[m], 1.0, 0.0).astype(BF16)
            out.extend(send_terms(m, VIS, nn(pick, acts[m]).astype(BF16)))
        for m in (1, 0):
            total = sum_terms(m, VIS)
            mask = picks[m]
            pick = jnp.where(mask, 1.0, 0.0).astype(BF16)
            inner = jnp.sum(jnp.where(mask, inner_row(m), 0.0), axis=1, keepdims=True)
            scale_row = to_row(sc[m][:, 0:1])
            scale = jnp.sum(jnp.where(mask, scale_row, 0.0), axis=1, keepdims=True)
            cols = pl.ds(pl.multiple_of(ten * BLK, BLK), BLK)
            unit = nn(pick, xb[m, :, cols]) * scale
            w = total * gb[ten]
            block = (nn(pick, inc[m, ten]) + scale * (w - unit * inner)).astype(BF16)
            if m == 1:
                out_block[0, 0:VIS, :] = block
                for o in range(8):
                    out.append(
                        remote(
                            ("up", o),
                            out_block.at[0, pl.ds(0, VIS), :],
                            vis.at[ten],
                            device(s=1, t=peer(o)),
                        )
                    )
            else:
                vis[ten] = block
                out.extend(push("visp", vis.at[ten], vis, ten))
        for o in range(1, 8):
            arrive(("visp", o), vis.at[peer(8 - o)])
        for copy in out:
            copy.wait_send()

    spread("vis", lambda k: vis.at[k], visr)
    ga_own[...] = jnp.zeros_like(ga_own)
    for i in range(8):
        ga_own[...] += nt(vis[i], f2[:, i * BLK : (i + 1) * BLK])
    sent.append(remote(("ga",), ga_own, ga_other, sibling))
    arrive(("ga",), ga_other)
    grad_pre = ((ga_own[...] + ga_other[...]) * slope[...]).astype(BF16)
    gpre[:, 0:PIECE] = grad_pre
    spread("gp", lambda k: gpre, gpr)
    stat_lane = lax.broadcasted_iota(jnp.int32, (VIS, LANES - PIECE), 1)
    for q in range(2):
        cols = pl.ds(pl.multiple_of(core * 2 * CTX + q * CTX, CTX), CTX)
        gm = nn(grad_pre, f1[:, cols])
        u = gm * lng_ref[...].reshape(1, CTX)
        n = jnp.concatenate([pu[0, 2 * core + q], pu[1, 2 * core + q]], axis=0)
        s1 = jnp.sum(u, axis=1, keepdims=True)
        s2 = jnp.sum(u * n, axis=1, keepdims=True)
        h1 = s1.astype(BF16).astype(F32)
        h2 = s2.astype(BF16).astype(F32)
        stats = jnp.where(
            stat_lane == 0,
            h1,
            jnp.where(
                stat_lane == 1,
                s1 - h1,
                jnp.where(stat_lane == 2, h2, jnp.where(stat_lane == 3, s2 - h2, 0.0)),
            ),
        ).astype(BF16)
        for j in range(4):
            pgp[q * 4 + j, :, 0:PIECE] = gm[:, j * PIECE : (j + 1) * PIECE].astype(BF16)
            pgp[q * 4 + j, :, PIECE:LANES] = stats
    for o in range(1, 8):
        to = lax.rem(ten + o, 8)
        sent.append(remote(("pg", o), pgp.at[to], pgpr.at[ten], device(t=to)))

    collect("act", actr)
    collect("vis", visr)
    fc2_val[...] = tn(
        actr[...].reshape(8 * VIS, LANES)[:, 0:PIECE], visr[...].reshape(8 * VIS, BLK)
    )
    out2 = local("fc2", fc2_val, fc2_out)

    total = pgp[ten].astype(F32)
    for o in range(1, 8):
        src = lax.rem(ten + 8 - o, 8)
        arrive(("pg", o), pgpr.at[src])
        total += pgpr[src].astype(F32)
    s1 = (total[:, PIECE : PIECE + 1] + total[:, PIECE + 1 : PIECE + 2]) / CTX
    s2 = (total[:, PIECE + 2 : PIECE + 3] + total[:, PIECE + 3 : PIECE + 4]) / CTX
    patch = 2 * core + zl
    inv = jnp.concatenate([iv[0, patch], iv[1, patch]], axis=0)[:, 0:1]
    block = inv * (total[:, 0:PIECE] * lgb[xx] - s1 - nblk[ten] * s2)
    for b in range(2):
        rows = block[b * 24 : (b + 1) * 24, :]
        pgs[b, :, 0:PIECE] = rows[0:16, :].astype(BF16)
        pgs[b, :, PIECE : PIECE + 160] = jnp.concatenate(
            [rows[16:24, 0:160], rows[16:24, 160:320]], axis=0
        ).astype(BF16)
    my_code = core * 8 + ten
    for o in range(1, 16):
        code = lax.rem(my_code + o, 16)
        sent.append(
            remote(
                ("po", o),
                pgs.at[code // 8],
                pgr.at[my_code],
                device(b=code // 8, t=lax.rem(code, 8)),
            )
        )
    pgr[my_code] = pgs[core]

    collect("mn", mnr)
    collect("gp", gpr)
    fc1_val[...] = tn(
        mnr[...].reshape(8 * VIS, LANES)[:, 0:PIECE], gpr[...].reshape(8 * VIS, LANES)[:, 0:PIECE]
    )
    out1 = local("fc1", fc1_val, fc1_out)
    for o in range(1, 16):
        arrive(("po", o), pgr.at[lax.rem(my_code + 16 - o, 16)])
    for q in range(4):
        pieces = []
        for j in range(4):
            msg = pgr[q * 4 + j].astype(F32)
            tail = jnp.concatenate(
                [msg[0:8, PIECE : PIECE + 160], msg[8:16, PIECE : PIECE + 160]], axis=1
            )
            pieces.append(jnp.concatenate([msg[:, 0:PIECE], tail], axis=0))
        pg_out[0, :, q * CTX : (q + 1) * CTX] = jnp.concatenate(pieces, axis=1).astype(BF16)

    for copy in sent:
        copy.wait_send()
    out1.wait()
    out2.wait()
    tg_drain()
    sent_wait(("pu",), pu.at[core])
    sent_wait(("iv",), iv.at[core])
    drain_spread("mn", lambda k: mns.at[8 * core + k])
    drain_spread("act", lambda k: act)
    drain_spread("gp", lambda k: gpre)
    drain_spread("vis", lambda k: vis.at[k])


def hand_over(a, b, c, a_out, b_out, c_out):
    a_out[...] = a[...]
    b_out[...] = b[...]
    c_out[...] = c[...]


def tables():
    freq = THETA ** (-(2.0 * np.arange(64, dtype=np.float64)) / HEAD)
    angles = np.arange(SEQ, dtype=np.float64)[:, None] * freq[None, :]
    cosine, sine = np.cos(angles), np.sin(angles)
    pick = np.zeros((4, SEQ, 8 * 48), np.float32)
    for e in range(4):
        for t in range(8):
            for i in range(12):
                pick[e, t * 12 + i, t * 48 + e * 12 + i] = 1.0
    return (
        np.concatenate([cosine, cosine], axis=1).astype(np.float32),
        np.concatenate([-sine, sine], axis=1).astype(np.float32),
        pick,
    )


def local(
    lm_inputs,
    top_grad,
    phase_gain,
    query_weight,
    kv_weight,
    out_weight,
    segment_ids,
    visual_pos,
    patches,
    ln_gain,
    ln_bias,
    fc1_weight,
    fc1_bias,
    fc2_weight,
):
    cosine, sine, pick = tables()
    shards = top_grad[0].reshape(2, 12, 2, 4, 1024).transpose(0, 2, 3, 1, 4)
    shards = shards.reshape(2, 2, 48, 1024)
    vmem = pl.BlockSpec(memory_space=pltpu.VMEM)
    hbm = pl.BlockSpec(memory_space=pl.ANY)
    v = pltpu.VMEM
    pg, fc1_grad, fc2_grad = pl.pallas_call(
        kernel,
        out_shape=(
            jax.ShapeDtypeStruct((1, 24, 4 * CTX), BF16),
            jax.ShapeDtypeStruct((PIECE, PIECE), F32),
            jax.ShapeDtypeStruct((PIECE, BLK), F32),
        ),
        in_specs=[
            hbm, hbm, vmem, hbm, hbm, hbm, vmem, vmem, vmem, vmem, vmem, hbm, vmem, hbm,
            hbm, hbm, hbm,
        ],
        out_specs=(vmem, hbm, hbm),
        scratch_shapes=[
            v((SEQ, HEAD), F32),
            v((SEQ, HEAD), F32),
            v((4, SEQ, 8 * 48), BF16),
            v((PIECE, PIECE), F32),
            v((PIECE, BLK), F32),
            v((3, HALF, 256), BF16),
            v((512, HALF), BF16),
            v((PIECE, 4 * CTX), BF16),
            v((PIECE, HALF), BF16),
            v((SEQ, WIDTH), BF16),
            v((2, SEQ, HALF), BF16),
            v((2, SEQ, HEAD), F32),
            v((8, 1, BLK), F32),
            v((2, 8, 48, 1024), BF16),
            v((2, 8, SEQ, BLK), BF16),
            v((2 * SEQ, 768), F32),
            v((2 * SEQ, 768), F32),
            v((2 * SEQ, 768), F32),
            v((2, 4 * SEQ, HEAD), BF16),
            v((2, SEQ, HEAD), BF16),
            v((2, SEQ, HEAD), BF16),
            v((2, 4 * SEQ, SEQ), F32),
            v((2, SEQ, 512), F32),
            v((2, SEQ, 512), F32),
            v((2, SEQ, 768), BF16),
            v((2, 8, HEAD), F32),
            v((2, 8, 8, HEAD), F32),
            v((2, 8, SEQ, BLK), BF16),
            v((2, 8, SEQ, BLK), BF16),
            v((2, SEQ, BLK), BF16),
            v((8, VIS, BLK), BF16),
            v((2, 4, 24, CTX), F32),
            v((2, 4, 24, HEAD), F32),
            v((VIS, 4 * CTX), BF16),
            v((16, VIS, LANES), BF16),
            v((VIS, LANES), BF16),
            v((VIS, PIECE), F32),
            v((8, VIS, PIECE), F32),
            v((4, 1, PIECE), F32),
            v((VIS, PIECE), F32),
            v((VIS, PIECE), F32),
            v((VIS, LANES), BF16),
            v((8, VIS, LANES), BF16),
            v((8, VIS, LANES), BF16),
            v((8, VIS, LANES), BF16),
            v((8, VIS, BLK), BF16),
            v((8, VIS, LANES), BF16),
            v((8, VIS, LANES), BF16),
            v((2, 16, BLK), BF16),
            v((16, 16, BLK), BF16),
            pltpu.SemaphoreType.DMA((224,)),
            pltpu.SemaphoreType.DMA((224,)),
            pltpu.SemaphoreType.DMA((20,)),
            pltpu.SemaphoreType.REGULAR((2,)),
        ],
        compiler_params=pltpu.CompilerParams(
            collective_id=0, has_side_effects=True, vmem_limit_bytes=60 * 1024 * 1024
        ),
    )(
        lm_inputs[0, 0],
        shards,
        phase_gain,
        query_weight.reshape(WIDTH, 256),
        kv_weight.reshape(WIDTH, HEAD),
        out_weight.reshape(256, WIDTH),
        segment_ids,
        visual_pos,
        patches,
        ln_gain,
        ln_bias,
        fc1_weight.T,
        fc1_bias,
        fc2_weight,
        cosine,
        sine,
        jnp.asarray(pick, BF16),
    )
    pg, fc1_grad, fc2_grad = pl.pallas_call(
        hand_over,
        out_shape=tuple(jax.ShapeDtypeStruct(a.shape, a.dtype) for a in (pg, fc1_grad, fc2_grad)),
        in_specs=[vmem, vmem, vmem],
        out_specs=(vmem, vmem, vmem),
    )(pg, fc1_grad, fc2_grad)
    return (pg, fc1_grad, fc2_grad.T)


def solution(mesh):
    in_specs = (
        P("dp", "pipe", None, None),
        P("dp", None, "tensor", None),
        P(),
        P("pipe", None, "tensor", None),
        P("pipe", None, "tensor", None),
        P("pipe", "tensor", None, None),
        P("dp", None, None),
        P("dp", None),
        P("dp", "pipe", None),
        P(),
        P(),
        P(None, "tensor"),
        P("tensor"),
        P("tensor", None),
    )
    out_specs = (P("dp", "pipe", None), P(("dp", "pipe"), "tensor"), P(("dp", "pipe"), "tensor"))
    return jax.shard_map(local, mesh=mesh, in_specs=in_specs, out_specs=out_specs, check_vma=False)
```

```python
import functools

import jax
import jax.numpy as jnp
import numpy as np
from jax import lax
from jax.experimental import pallas as pl
from jax.experimental.pallas import tpu as pltpu
from jax.sharding import PartitionSpec as P

EPS_RMS = 1e-06
EPS_LN = 1e-06
THETA = 1000000.0
MESH = pl.DeviceIdType.MESH
F32 = jnp.float32
BF16 = jnp.bfloat16
SEQ = 96
WIDTH = 8192
HALF = 4096
BLK = 512
HEAD = 128
FACTOR = HEAD**-0.5
VIS = 48
CTX = 1280
PIECE = 320
LANES = 384


def nn(a, b):
    return lax.dot_general(a, b, (((1,), (0,)), ((), ())), preferred_element_type=F32)


def nt(a, b):
    return lax.dot_general(a, b, (((1,), (1,)), ((), ())), preferred_element_type=F32)


def tn(a, b):
    return lax.dot_general(a, b, (((0,), (0,)), ((), ())), preferred_element_type=F32)


def each(count, body):
    def step(i, carry):
        body(i)
        return carry

    lax.fori_loop(0, count, step, 0)


def eye_mask(size):
    return lax.broadcasted_iota(jnp.int32, (size, size), 0) == lax.broadcasted_iota(
        jnp.int32, (size, size), 1
    )


def to_row(column):
    size = column.shape[0]
    return jnp.sum(jnp.where(eye_mask(size), column, 0.0), axis=0, keepdims=True)


def to_column(row):
    size = row.shape[1]
    return jnp.sum(jnp.where(eye_mask(size), row, 0.0), axis=1, keepdims=True)


class Sems:
    def __init__(self):
        self.numbers = {}

    def __call__(self, *name):
        return self.numbers.setdefault(name, len(self.numbers))


def kernel(
    x_hbm,
    tg_hbm,
    gain_ref,
    wq_hbm,
    wkv_hbm,
    wo_hbm,
    seg_ref,
    pos_ref,
    patches_ref,
    lng_ref,
    lnb_ref,
    fc1_hbm,
    fc1b_ref,
    fc2_hbm,
    cos_hbm,
    sin_hbm,
    tgsel_hbm,
    pg_out,
    fc1_out,
    fc2_out,
    cos_ref,
    sin_ref,
    tgsel_ref,
    fc1_val,
    fc2_val,
    w3,
    wo,
    w3t,
    wot,
    f1,
    f2,
    xo,
    xb,
    sc,
    gb,
    tg,
    inc,
    normed,
    own_p,
    other_p,
    pf,
    qs,
    ks,
    vs,
    probs,
    gx_own,
    gx_other,
    acts,
    ins,
    inr,
    part,
    r1,
    out_block,
    vis,
    pu,
    iv,
    mn,
    mns,
    act,
    slope,
    nblk,
    lgb,
    ga_own,
    ga_other,
    gpre,
    mnr,
    actr,
    gpr,
    visr,
    pgp,
    pgpr,
    pgs,
    pgr,
    send_sem,
    recv_sem,
    local_sem,
    y_sem,
):
    dp = lax.axis_index("dp")
    pipe = lax.axis_index("pipe")
    ten = lax.axis_index("tensor")
    phase = pipe // 2
    core = pipe % 2
    zl = ten // 4
    xx = ten % 4
    sems = Sems()
    locals_ = Sems()

    def device(s=None, b=None, z=None, x=None, d=None, t=None):
        s = phase if s is None else s
        b = core if b is None else b
        if t is None:
            t = (zl if z is None else z) * 4 + (xx if x is None else x)
        return (dp if d is None else d, 2 * s + b, t)

    sibling = device(b=1 - core)
    cross = device(s=1 - phase, z=1 - zl)

    barrier = pltpu.get_barrier_semaphore()
    up_y = device(d=lax.rem(dp + 1, 4))
    down_y = device(d=lax.rem(dp + 3, 4))
    greeted = [sibling, up_y, down_y, device(s=1 - phase)]
    greeted += [device(t=lax.rem(ten + o, 8)) for o in range(1, 8)]
    greeted += [device(s=1 - phase, z=1 - zl, x=lax.rem(xx + o, 4)) for o in range(4)]
    for to in greeted:
        pl.semaphore_signal(barrier, inc=1, device_id=to, device_id_type=MESH)

    def local(name, src, dst):
        copy = pltpu.make_async_copy(src, dst, local_sem.at[locals_(name)])
        copy.start()
        return copy

    def remote(name, src, dst, to):
        number = sems(*name)
        copy = pltpu.make_async_remote_copy(
            src_ref=src,
            dst_ref=dst,
            send_sem=send_sem.at[number],
            recv_sem=recv_sem.at[number],
            device_id=to,
            device_id_type=MESH,
        )
        copy.start()
        return copy

    def arrive(name, ref):
        pltpu.make_async_copy(ref, ref, recv_sem.at[sems(*name)]).wait()

    mine = core * HALF
    theirs = (1 - core) * HALF
    lx = local("x", x_hbm, xo)
    lxh = local("xh", x_hbm.at[:, pl.ds(mine, HALF)], xb.at[core])
    lq = local("q", wq_hbm.at[pl.ds(mine, HALF), :], w3.at[core])
    lkv = local(
        "kv", wkv_hbm.at[pl.ds(mine, HALF), :], w3.at[2, :, pl.ds(core * HEAD, HEAD)]
    )
    lo = local("o", wo_hbm.at[:, pl.ds(mine, HALF)], wo.at[pl.ds(core * 256, 256), :])
    lsel = local("sel", tgsel_hbm, tgsel_ref)
    lcos = local("cos", cos_hbm, cos_ref)
    lsin = local("sin", sin_hbm, sin_ref)
    lf1 = local("f1", fc1_hbm, f1)
    lf2 = local("f2", fc2_hbm.at[:, pl.ds(mine, HALF)], f2)

    pl.semaphore_wait(barrier, len(greeted))

    def peer(o):
        return lax.rem(ten + o, 8)

    def push(name, src, dst):
        return [remote((name, o), src, dst, device(t=peer(o))) for o in range(1, 8)]

    def part_rows(h):
        return pl.ds(h * VIS, VIS)

    def send_term(m, h, o):
        j = peer(o)
        return remote(
            ("rs", m, h, o),
            part.at[m, j, part_rows(h), :],
            r1.at[m, ten, part_rows(h), :],
            device(t=j),
        )

    def send_terms(m, product):
        halves = 0
        for o in list(range(1, 8)) + [0]:
            j = peer(o)
            acc = product(pl.ds(pl.multiple_of(j * BLK, BLK), BLK))
            halves = acc.shape[0] // VIS
            part[m, j, pl.ds(0, acc.shape[0]), :] = acc.astype(BF16)
            if o:
                send_term(m, 0, o)
        for h in range(1, halves):
            for o in range(1, 8):
                send_term(m, h, o)

    def drain_phase(halves):
        for m in (1, 0):
            sent_wait(("gx", m), gx_own.at[m])
            for o in range(1, 8):
                sent_wait(("in", m, o), ins.at[m])
                for h in range(halves):
                    sent_wait(("rs", m, h, o), part.at[m, peer(o), part_rows(h), :])

    def sum_terms(m, h):
        total = part[m, ten, part_rows(h), :].astype(F32)
        for o in range(1, 8):
            src = peer(8 - o)
            ref = r1.at[m, src, part_rows(h), :]
            arrive(("rs", m, h, o), ref)
            total += ref[...].astype(F32)
        return total

    sent = []
    upper = phase == 1
    lower = jnp.logical_not(upper)
    cut_at = 384

    def tg_send(m):
        @pl.when(upper)
        def _():
            local(("tg", m), tg_hbm.at[m, core], tg.at[m, ten])
            for o in range(1, 4):
                remote(
                    ("tgx", m, o),
                    tg_hbm.at[m, core],
                    tg.at[m, ten],
                    device(x=lax.rem(xx + o, 4)),
                )
            for o in range(4):
                remote(
                    ("tgz", m, o),
                    tg_hbm.at[m, core, :, pl.ds(0, cut_at)],
                    tg.at[m, ten, :, pl.ds(0, cut_at)],
                    device(z=1 - zl, x=lax.rem(xx + o, 4)),
                )

        @pl.when(lower)
        def _():
            for o in range(4):
                remote(
                    ("tgc", m, o),
                    tg_hbm.at[m, core, :, pl.ds(cut_at, 1024 - cut_at)],
                    tg.at[m, ten, :, pl.ds(cut_at, 1024 - cut_at)],
                    device(s=1, z=1 - zl, x=lax.rem(xx + o, 4)),
                )

    tg_send(1)

    def tg_wait(m):
        pltpu.make_async_copy(
            tg.at[m, ten], tg.at[m, ten], local_sem.at[locals_(("tg", m))]
        ).wait()
        for o in range(1, 4):
            arrive(("tgx", m, o), tg.at[m, zl * 4 + lax.rem(xx + 4 - o, 4)])
        for o in range(4):
            slot = (1 - zl) * 4 + lax.rem(xx + 4 - o, 4)
            arrive(("tgz", m, o), tg.at[m, slot, :, pl.ds(0, cut_at)])
            arrive(("tgc", m, o), tg.at[m, slot, :, pl.ds(cut_at, 1024 - cut_at)])

    def sent_wait(name, ref):
        pltpu.make_async_copy(ref, ref, send_sem.at[sems(*name)]).wait()

    def tg_drain():
        for m in (1, 0):

            @pl.when(upper)
            def _(m=m):
                for o in range(1, 4):
                    sent_wait(("tgx", m, o), tg_hbm.at[m, core])
                for o in range(4):
                    sent_wait(("tgz", m, o), tg_hbm.at[m, core, :, pl.ds(0, cut_at)])

            @pl.when(lower)
            def _(m=m):
                for o in range(4):
                    sent_wait(
                        ("tgc", m, o), tg_hbm.at[m, core, :, pl.ds(cut_at, 1024 - cut_at)]
                    )

    sent.append(remote(("x",), x_hbm.at[:, pl.ds(theirs, HALF)], xb.at[core], sibling))
    sent.append(remote(("wq",), wq_hbm.at[pl.ds(theirs, HALF), :], w3.at[core], sibling))
    sent.append(
        remote(
            ("wkv",),
            wkv_hbm.at[pl.ds(theirs, HALF), :],
            w3.at[2, :, pl.ds(core * HEAD, HEAD)],
            sibling,
        )
    )
    sent.append(
        remote(
            ("wo",),
            wo_hbm.at[:, pl.ds(theirs, HALF)],
            wo.at[pl.ds(core * 256, 256), :],
            sibling,
        )
    )

    for i in range(8):
        pair = gain_ref[:, pl.ds(pl.multiple_of(mine + i * BLK, BLK), BLK)]
        gb[i] = jnp.where(upper, pair[1:2, :], pair[0:1, :])

    lx.wait()
    acc = jnp.zeros((SEQ, 1), F32)

    def square(i, acc):
        v = xo[:, pl.ds(pl.multiple_of(i * 1024, 1024), 1024)].astype(F32)
        return acc + jnp.sum(v * v, axis=1, keepdims=True)

    acc = lax.fori_loop(0, 8, square, acc)
    sc[core] = jnp.broadcast_to(lax.rsqrt(acc / WIDTH + EPS_RMS), (SEQ, HEAD))
    sent.append(remote(("sc",), sc.at[core], sc.at[core], sibling))

    def normalize(i):
        cols = pl.ds(pl.multiple_of(i * BLK, BLK), BLK)
        rows = [
            (xb[m, :, cols].astype(F32) * sc[m][:, 0:1] * gb[i]).astype(BF16) for m in range(2)
        ]
        normed[i] = jnp.concatenate(rows, axis=0)

    def own_product(j):
        acc = jnp.zeros((2 * SEQ, 256), F32)
        for i in range(8):
            acc += nn(normed[i], w3[j, i * BLK : (i + 1) * BLK, :])
        return acc

    lxh.wait()
    arrive(("x",), xb.at[1 - core])
    arrive(("sc",), sc.at[1 - core])
    each(8, normalize)
    lq.wait()
    own_p[core] = own_product(core)
    sent.append(remote(("p", 0), own_p.at[core], other_p.at[core], sibling))
    tg_send(0)
    arrive(("wq",), w3.at[1 - core])
    own_p[1 - core] = own_product(1 - core)
    sent.append(remote(("p", 1), own_p.at[1 - core], other_p.at[1 - core], sibling))
    lkv.wait()
    arrive(("wkv",), w3.at[2, :, pl.ds((1 - core) * HEAD, HEAD)])
    own_p[2] = own_product(2)
    sent.append(remote(("p", 2), own_p.at[2], other_p.at[2], sibling))

    def head_grads(m, slots, product):
        acc = jnp.zeros((SEQ, 512), F32)
        for slot in slots():
            acc += product(inc[m, slot], pl.ds(pl.multiple_of(slot * BLK, BLK), BLK))
        gx_own[m] = acc
        remote(("gx", m), gx_own.at[m], gx_other.at[m], sibling)

    def upper_heads(m):
        tg_wait(m)
        flat = tg[m].reshape(8 * 48, 1024)
        for e in range(4):
            wide = nn(tgsel_ref[e], flat).astype(BF16)
            inc[m, 2 * e] = wide[:, 0:BLK]
            inc[m, 2 * e + 1] = wide[:, BLK : 2 * BLK]
        head_grads(m, lambda: range(8), lambda block, cols: nt(block, wo[:, cols]))

    lsel.wait()
    lo.wait()
    arrive(("wo",), wo.at[pl.ds((1 - core) * 256, 256), :])
    pl.when(upper)(lambda: upper_heads(1))

    arrive(("p", 0), other_p.at[1 - core])
    arrive(("p", 1), other_p.at[core])
    arrive(("p", 2), other_p.at[2])
    for j in range(3):
        pf[:, j * 256 : (j + 1) * 256] = own_p[j] + other_p[j]

    lane = lax.broadcasted_iota(jnp.int32, (SEQ, HEAD), 1)
    low = lane < 64

    def rope(v, direction):
        return v * cos_ref[...] + direction * pltpu.roll(v, 64, 1) * sin_ref[...]

    def stacked(v):
        return jnp.concatenate([v[:, h * HEAD : (h + 1) * HEAD] for h in range(4)], axis=0)

    def forward(m):
        rows = pf[m * SEQ : (m + 1) * SEQ, :]
        q = jnp.concatenate(
            [rope(rows[:, h * HEAD : (h + 1) * HEAD], 1.0) for h in range(4)], axis=0
        ).astype(BF16)
        kv0 = rows[:, 512:640].astype(BF16).astype(F32)
        kv1 = rows[:, 640:768].astype(BF16).astype(F32)
        k = rope(jnp.where(low, kv0, pltpu.roll(kv1, 64, 1)), 1.0).astype(BF16)
        v = jnp.where(low, pltpu.roll(kv0, 64, 1), kv1).astype(BF16)
        qs[m] = q
        ks[m] = k
        vs[m] = v
        scores = nt(q, k) * FACTOR
        seg = seg_ref[0, m : m + 1, :].astype(F32)
        seg_col = to_column(seg)
        index_row = lax.broadcasted_iota(jnp.int32, (SEQ, SEQ), 0)
        index_col = lax.broadcasted_iota(jnp.int32, (SEQ, SEQ), 1)
        allowed = jnp.where((index_col <= index_row) & (seg_col == seg), 1.0, 0.0)
        allowed = jnp.concatenate([allowed] * 4, axis=0) > 0.5
        scores = jnp.where(allowed, scores, -1e30)
        top = jnp.max(scores, axis=1, keepdims=True)
        weights = jnp.where(allowed, jnp.exp(scores - top), 0.0)
        probs[m] = weights / jnp.sum(weights, axis=1, keepdims=True)

    def backward(m):
        arrive(("gx", m), gx_other.at[m])
        go = stacked(gx_own[m] + gx_other[m]).astype(BF16)
        pr = probs[m]
        gp = nt(go, vs[m])
        delta = jnp.sum(pr * gp, axis=1, keepdims=True)
        gs = (pr * (gp - delta) * FACTOR).astype(BF16)
        gq = nn(gs, ks[m])
        gk = rope(tn(gs, qs[m]), -1.0)
        gv = tn(pr.astype(BF16), go)
        pieces = [rope(gq[h * SEQ : (h + 1) * SEQ, :], -1.0) for h in range(4)]
        pieces.append(jnp.where(low, gk, pltpu.roll(gv, 64, 1)))
        pieces.append(jnp.where(low, pltpu.roll(gk, 64, 1), gv))
        inner = jnp.zeros((SEQ, 1), F32)
        for h in range(6):
            low_piece = pieces[h].astype(BF16)
            acts[m, :, h * HEAD : (h + 1) * HEAD] = low_piece
            inner += jnp.sum(
                low_piece.astype(F32) * pf[m * SEQ : (m + 1) * SEQ, h * HEAD : (h + 1) * HEAD],
                axis=1,
                keepdims=True,
            )
        row = to_row(inner / WIDTH)
        ins[m, :, 0:SEQ] = jnp.broadcast_to(row, (8, SEQ))
        for o in range(1, 8):
            remote(("in", m, o), ins.at[m], inr.at[m, ten], device(t=peer(o)))

    def inner_row(m):
        total = ins[m, 0:1, 0:SEQ]
        for o in range(1, 8):
            src = peer(8 - o)
            arrive(("in", m, o), inr.at[m, src])
            total += inr[m, src, 0:1, 0:SEQ]
        return total

    def merger_forward():
        for q in range(4):
            v = patches_ref[0, :, q * CTX : (q + 1) * CTX].astype(F32)
            v = v - jnp.mean(v, axis=1, keepdims=True)
            inv = lax.rsqrt(jnp.mean(v * v, axis=1, keepdims=True) + EPS_LN)
            pu[core, q] = v * inv
            iv[core, q] = jnp.broadcast_to(inv, (24, HEAD))
        remote(("pu",), pu.at[core], pu.at[core], sibling)
        remote(("iv",), iv.at[core], iv.at[core], sibling)
        for name in ("y1", "y2"):
            number = ("y1", "y2").index(name)
            for to in (up_y, down_y):
                pl.semaphore_signal(y_sem.at[number], inc=1, device_id=to, device_id_type=MESH)
            pl.semaphore_wait(y_sem.at[number], 2)
        lf1.wait()
        lf2.wait()
        arrive(("pu",), pu.at[1 - core])
        arrive(("iv",), iv.at[1 - core])
        gain = lng_ref[...].reshape(1, CTX)
        bias = lnb_ref[...].reshape(1, CTX)
        hidden = jnp.zeros((VIS, PIECE), F32)
        for q in range(4):
            n = jnp.concatenate([pu[0, q], pu[1, q]], axis=0)
            low_n = (n * gain + bias).astype(BF16)
            mn[:, q * CTX : (q + 1) * CTX] = low_n
            for j in range(4):
                mns[q * 4 + j, :, 0:PIECE] = low_n[:, j * PIECE : (j + 1) * PIECE]
            hidden += nt(low_n, f1[:, q * CTX : (q + 1) * CTX])
            lgb[q] = gain[:, q * PIECE : (q + 1) * PIECE]
        for q in range(2):
            n = jnp.concatenate([pu[0, 2 * core + q], pu[1, 2 * core + q]], axis=0)
            for j in range(4):
                nblk[q * 4 + j] = n[:, j * PIECE : (j + 1) * PIECE]
        hidden += fc1b_ref[...].reshape(1, PIECE)
        cdf = 0.5 * (1.0 + lax.erf(hidden * 0.7071067811865476))
        density = jnp.exp(-0.5 * hidden * hidden) * 0.3989422804014327
        slope[...] = cdf + hidden * density
        act[:, 0:PIECE] = (hidden * cdf).astype(BF16)
        spread("mn", lambda k: mns.at[8 * core + k], mnr)
        spread("act", lambda k: act, actr)

    my_slot = dp * 2 + phase

    def target(k):
        return (2 * core + k // 4, (k // 2) % 2 * 2 + k % 2, ten)

    def is_self(k):
        to = target(k)
        return (to[0] == dp) & (to[1] == pipe)

    def spread_one(name, k, source, slots):
        number = sems(name, 0) + k
        got = recv_sem.at[sems(name, "got") + my_slot]

        @pl.when(jnp.logical_not(is_self(k)))
        def _():
            pltpu.make_async_remote_copy(
                src_ref=source,
                dst_ref=slots.at[my_slot],
                send_sem=send_sem.at[number],
                recv_sem=got,
                device_id=target(k),
                device_id_type=MESH,
            ).start()

        @pl.when(is_self(k))
        def _():
            pltpu.make_async_copy(source, slots.at[my_slot], got).start()

    def spread(name, source, slots):
        for k in range(8):
            spread_one(name, k, source(k), slots)

    def spread_numbers():
        for name in ("mn", "act", "gp", "vis"):
            sems(name, "got")
            for i in range(1, 8):
                sems(name, "got+", i)
            for k in range(8):
                sems(name, k)

    spread_numbers()

    def collect(name, slots):
        for i in range(8):
            pltpu.make_async_copy(
                slots.at[i], slots.at[i], recv_sem.at[sems(name, "got") + i]
            ).wait()

    def drain_spread(name, source):
        for k in range(8):
            number = sems(name, k)

            @pl.when(jnp.logical_not(is_self(k)))
            def _(k=k, number=number):
                pltpu.make_async_copy(source(k), source(k), send_sem.at[number]).wait()

    own_cols = pl.ds(pl.multiple_of(ten * BLK, BLK), BLK)

    def ga_send():
        remote(("ga",), ga_own, ga_other, sibling)

    def upper_product(m):
        def product(cols):
            acc = nt(acts[m, :, 0:256], w3[0, cols, :])
            acc += nt(acts[m, :, 256:512], w3[1, cols, :])
            return acc + nt(acts[m, :, 512:768], w3[2, cols, :])

        return product

    lcos.wait()
    lsin.wait()
    forward(1)

    @pl.when(upper)
    def _():
        backward(1)
        send_terms(1, upper_product(1))

    forward(0)

    @pl.when(upper)
    def _():
        out = []
        upper_heads(0)
        backward(0)
        send_terms(0, upper_product(0))
        for m in (1, 0):
            inner = None
            for h in range(2):
                total = sum_terms(m, h)
                if h == 0:
                    inner = to_column(inner_row(m))
                low_row, high_row = h * VIS, (h + 1) * VIS
                scale = sc[m, low_row:high_row, 0:1]
                cols = pl.ds(pl.multiple_of(ten * BLK, BLK), BLK)
                unit = xb[m, low_row:high_row, cols].astype(F32) * scale
                w = total * gb[ten]
                out_block[m, low_row:high_row, :] = (
                    inc[m, ten, part_rows(h), :].astype(F32)
                    + scale * (w - unit * inner[low_row:high_row, :])
                ).astype(BF16)
                out.append(
                    remote(
                        ("down", m, h),
                        out_block.at[m, part_rows(h), :],
                        inc.at[m, ten, part_rows(h), :],
                        cross,
                    )
                )
        merger_forward()
        for copy in out:
            copy.wait_send()
        drain_phase(2)
        ga_own[...] = jnp.zeros_like(ga_own)
        for o in range(8):
            slot = peer(8 - o)
            arrive(("up", o), vis.at[slot])
            spread_one("vis", slot, vis.at[slot], visr)
            ga_own[...] += nt(vis[slot], f2[:, pl.ds(pl.multiple_of(slot * BLK, BLK), BLK)])
        ga_send()

    @pl.when(lower)
    def _():
        merger_forward()
        out = []
        held = (1 - zl) * 4 + xx

        def pass_on(m, h):
            ref = inc.at[m, held, part_rows(h), :]
            arrive(("down", m, h), ref)
            out.extend(push(("inc", m, h), ref, ref))

        def blocks(m):
            yield held
            for o in range(1, 8):
                if m == 1 and o == 4:
                    pass_on(0, 1)
                slot = lax.rem(peer(8 - o) + 4, 8)
                for h in range(2):
                    arrive((("inc", m, h), o), inc.at[m, slot, part_rows(h), :])
                yield slot

        def turn(i):
            cols = pl.ds(pl.multiple_of(i * BLK, BLK), BLK)
            wot[cols, :] = wo[:, cols].T
            for j in range(3):
                w3t[j, :, cols] = w3[j, cols, :].T

        each(8, turn)
        pass_on(1, 0)
        pass_on(1, 1)
        pass_on(0, 0)
        picks = {}

        def pick_rows(m):
            wide = lax.broadcasted_iota(jnp.int32, (VIS, SEQ), 0) + m * VIS
            across = lax.broadcasted_iota(jnp.int32, (VIS, SEQ), 1)
            tokens = jnp.sum(jnp.where(across == wide, pos_ref[...], 0), axis=1, keepdims=True)
            picks[m] = (tokens - m * SEQ) == across

        def lower_terms(m):
            pick = jnp.where(picks[m], 1.0, 0.0).astype(BF16)
            picked = nn(pick, acts[m]).astype(BF16)

            def product(cols):
                acc = nn(picked[:, 0:256], w3t[0, :, cols])
                acc += nn(picked[:, 256:512], w3t[1, :, cols])
                return acc + nn(picked[:, 512:768], w3t[2, :, cols])

            send_terms(m, product)

        def lower_block(m):
            mask = picks[m]
            pick = jnp.where(mask, 1.0, 0.0).astype(BF16)
            scale_row = to_row(sc[m][:, 0:1])
            scale = jnp.sum(jnp.where(mask, scale_row, 0.0), axis=1, keepdims=True)
            unit = nn(pick, xb[m, :, own_cols]) * scale
            rows = nn(pick, inc[m, ten])
            total = sum_terms(m, 0)
            inner = jnp.sum(jnp.where(mask, inner_row(m), 0.0), axis=1, keepdims=True)
            w = total * gb[ten]
            return (rows + scale * (w - unit * inner)).astype(BF16)

        for m in (1, 0):
            pick_rows(m)
            head_grads(m, lambda: blocks(m), lambda block, cols: nn(block, wot[cols, :]))
            backward(m)
            lower_terms(m)
        out_block[0, 0:VIS, :] = lower_block(1)
        for o in range(8):
            out.append(
                remote(
                    ("up", o),
                    out_block.at[0, pl.ds(0, VIS), :],
                    vis.at[ten],
                    device(s=1, t=peer(o)),
                )
            )
        vis[ten] = lower_block(0)
        out.extend(push("visp", vis.at[ten], vis.at[ten]))
        spread_one("vis", ten, vis.at[ten], visr)
        ga_own[...] = nt(vis[ten], f2[:, own_cols])
        for o in range(1, 8):
            slot = peer(8 - o)
            arrive(("visp", o), vis.at[slot])
            spread_one("vis", slot, vis.at[slot], visr)
            ga_own[...] += nt(vis[slot], f2[:, pl.ds(pl.multiple_of(slot * BLK, BLK), BLK)])
        ga_send()
        for copy in out:
            copy.wait_send()
        drain_phase(1)

    arrive(("ga",), ga_other)
    grad_pre = ((ga_own[...] + ga_other[...]) * slope[...]).astype(BF16)
    gpre[:, 0:PIECE] = grad_pre
    stat_lane = lax.broadcasted_iota(jnp.int32, (VIS, LANES - PIECE), 1)
    for q in range(2):
        cols = pl.ds(pl.multiple_of(core * 2 * CTX + q * CTX, CTX), CTX)
        gm = nn(grad_pre, f1[:, cols])
        u = gm * lng_ref[...].reshape(1, CTX)
        n = jnp.concatenate([pu[0, 2 * core + q], pu[1, 2 * core + q]], axis=0)
        s1 = jnp.sum(u, axis=1, keepdims=True)
        s2 = jnp.sum(u * n, axis=1, keepdims=True)
        h1 = s1.astype(BF16).astype(F32)
        h2 = s2.astype(BF16).astype(F32)
        stats = jnp.where(
            stat_lane == 0,
            h1,
            jnp.where(
                stat_lane == 1,
                s1 - h1,
                jnp.where(stat_lane == 2, h2, jnp.where(stat_lane == 3, s2 - h2, 0.0)),
            ),
        ).astype(BF16)
        for j in range(4):
            pgp[q * 4 + j, :, 0:PIECE] = gm[:, j * PIECE : (j + 1) * PIECE].astype(BF16)
            pgp[q * 4 + j, :, PIECE:LANES] = stats
    for o in range(1, 8):
        to = lax.rem(ten + o, 8)
        sent.append(remote(("pg", o), pgp.at[to], pgpr.at[ten], device(t=to)))
    spread("gp", lambda k: gpre, gpr)

    total = pgp[ten].astype(F32)
    for o in range(1, 8):
        src = lax.rem(ten + 8 - o, 8)
        arrive(("pg", o), pgpr.at[src])
        total += pgpr[src].astype(F32)
    s1 = (total[:, PIECE : PIECE + 1] + total[:, PIECE + 1 : PIECE + 2]) / CTX
    s2 = (total[:, PIECE + 2 : PIECE + 3] + total[:, PIECE + 3 : PIECE + 4]) / CTX
    patch = 2 * core + zl
    inv = jnp.concatenate([iv[0, patch], iv[1, patch]], axis=0)[:, 0:1]
    block = inv * (total[:, 0:PIECE] * lgb[xx] - s1 - nblk[ten] * s2)
    for b in range(2):
        rows = block[b * 24 : (b + 1) * 24, :]
        pgs[b, :, 0:PIECE] = rows[0:16, :].astype(BF16)
        pgs[b, :, PIECE : PIECE + 160] = jnp.concatenate(
            [rows[16:24, 0:160], rows[16:24, 160:320]], axis=0
        ).astype(BF16)
    my_code = core * 8 + ten
    for o in range(1, 16):
        code = lax.rem(my_code + o, 16)
        sent.append(
            remote(
                ("po", o),
                pgs.at[code // 8],
                pgr.at[my_code],
                device(b=code // 8, t=lax.rem(code, 8)),
            )
        )
    pgr[my_code] = pgs[core]

    collect("act", actr)
    collect("vis", visr)
    fc2_val[...] = tn(
        actr[...].reshape(8 * VIS, LANES)[:, 0:PIECE], visr[...].reshape(8 * VIS, BLK)
    )
    out2 = local("fc2", fc2_val, fc2_out)
    collect("mn", mnr)
    collect("gp", gpr)
    fc1_val[...] = tn(
        mnr[...].reshape(8 * VIS, LANES)[:, 0:PIECE], gpr[...].reshape(8 * VIS, LANES)[:, 0:PIECE]
    )
    out1 = local("fc1", fc1_val, fc1_out)
    for o in range(1, 16):
        arrive(("po", o), pgr.at[lax.rem(my_code + 16 - o, 16)])
    for q in range(4):
        pieces = []
        for j in range(4):
            msg = pgr[q * 4 + j].astype(F32)
            tail = jnp.concatenate(
                [msg[0:8, PIECE : PIECE + 160], msg[8:16, PIECE : PIECE + 160]], axis=1
            )
            pieces.append(jnp.concatenate([msg[:, 0:PIECE], tail], axis=0))
        pg_out[0, :, q * CTX : (q + 1) * CTX] = jnp.concatenate(pieces, axis=1).astype(BF16)

    for copy in sent:
        copy.wait_send()
    out1.wait()
    out2.wait()
    tg_drain()
    sent_wait(("ga",), ga_own)
    sent_wait(("pu",), pu.at[core])
    sent_wait(("iv",), iv.at[core])
    drain_spread("mn", lambda k: mns.at[8 * core + k])
    drain_spread("act", lambda k: act)
    drain_spread("gp", lambda k: gpre)
    drain_spread("vis", lambda k: vis.at[k])


def hand_over(a, b, c, a_out, b_out, c_out):
    a_out[...] = a[...]
    b_out[...] = b[...]
    c_out[...] = c[...]


def tables():
    freq = THETA ** (-(2.0 * np.arange(64, dtype=np.float64)) / HEAD)
    angles = np.arange(SEQ, dtype=np.float64)[:, None] * freq[None, :]
    cosine, sine = np.cos(angles), np.sin(angles)
    pick = np.zeros((4, SEQ, 8 * 48), np.float32)
    for e in range(4):
        for t in range(8):
            for i in range(12):
                pick[e, t * 12 + i, t * 48 + e * 12 + i] = 1.0
    return (
        np.concatenate([cosine, cosine], axis=1).astype(np.float32),
        np.concatenate([-sine, sine], axis=1).astype(np.float32),
        pick,
    )


def local(
    lm_inputs,
    top_grad,
    phase_gain,
    query_weight,
    kv_weight,
    out_weight,
    segment_ids,
    visual_pos,
    patches,
    ln_gain,
    ln_bias,
    fc1_weight,
    fc1_bias,
    fc2_weight,
):
    cosine, sine, pick = tables()
    shards = top_grad[0].reshape(2, 12, 2, 4, 1024).transpose(0, 2, 3, 1, 4)
    shards = shards.reshape(2, 2, 48, 1024)
    vmem = pl.BlockSpec(memory_space=pltpu.VMEM)
    hbm = pl.BlockSpec(memory_space=pl.ANY)
    v = pltpu.VMEM
    pg, fc1_grad, fc2_grad = pl.pallas_call(
        kernel,
        out_shape=(
            jax.ShapeDtypeStruct((1, 24, 4 * CTX), BF16),
            jax.ShapeDtypeStruct((PIECE, PIECE), F32),
            jax.ShapeDtypeStruct((PIECE, BLK), F32),
        ),
        in_specs=[
            hbm, hbm, vmem, hbm, hbm, hbm, vmem, vmem, vmem, vmem, vmem, hbm, vmem, hbm,
            hbm, hbm, hbm,
        ],
        out_specs=(vmem, hbm, hbm),
        scratch_shapes=[
            v((SEQ, HEAD), F32),
            v((SEQ, HEAD), F32),
            v((4, SEQ, 8 * 48), BF16),
            v((PIECE, PIECE), F32),
            v((PIECE, BLK), F32),
            v((3, HALF, 256), BF16),
            v((512, HALF), BF16),
            v((3, 256, HALF), BF16),
            v((HALF, 512), BF16),
            v((PIECE, 4 * CTX), BF16),
            v((PIECE, HALF), BF16),
            v((SEQ, WIDTH), BF16),
            v((2, SEQ, HALF), BF16),
            v((2, SEQ, HEAD), F32),
            v((8, 1, BLK), F32),
            v((2, 8, 48, 1024), BF16),
            v((2, 8, SEQ, BLK), BF16),
            v((8, 2 * SEQ, BLK), BF16),
            v((3, 2 * SEQ, 256), F32),
            v((3, 2 * SEQ, 256), F32),
            v((2 * SEQ, 768), F32),
            v((2, 4 * SEQ, HEAD), BF16),
            v((2, SEQ, HEAD), BF16),
            v((2, SEQ, HEAD), BF16),
            v((2, 4 * SEQ, SEQ), F32),
            v((2, SEQ, 512), F32),
            v((2, SEQ, 512), F32),
            v((2, SEQ, 768), BF16),
            v((2, 8, HEAD), F32),
            v((2, 8, 8, HEAD), F32),
            v((2, 8, SEQ, BLK), BF16),
            v((2, 8, SEQ, BLK), BF16),
            v((2, SEQ, BLK), BF16),
            v((8, VIS, BLK), BF16),
            v((2, 4, 24, CTX), F32),
            v((2, 4, 24, HEAD), F32),
            v((VIS, 4 * CTX), BF16),
            v((16, VIS, LANES), BF16),
            v((VIS, LANES), BF16),
            v((VIS, PIECE), F32),
            v((8, VIS, PIECE), F32),
            v((4, 1, PIECE), F32),
            v((VIS, PIECE), F32),
            v((VIS, PIECE), F32),
            v((VIS, LANES), BF16),
            v((8, VIS, LANES), BF16),
            v((8, VIS, LANES), BF16),
            v((8, VIS, LANES), BF16),
            v((8, VIS, BLK), BF16),
            v((8, VIS, LANES), BF16),
            v((8, VIS, LANES), BF16),
            v((2, 16, BLK), BF16),
            v((16, 16, BLK), BF16),
            pltpu.SemaphoreType.DMA((288,)),
            pltpu.SemaphoreType.DMA((288,)),
            pltpu.SemaphoreType.DMA((20,)),
            pltpu.SemaphoreType.REGULAR((2,)),
        ],
        compiler_params=pltpu.CompilerParams(
            collective_id=0, has_side_effects=True, vmem_limit_bytes=60 * 1024 * 1024
        ),
    )(
        lm_inputs[0, 0],
        shards,
        phase_gain,
        query_weight.reshape(WIDTH, 256),
        kv_weight.reshape(WIDTH, HEAD),
        out_weight.reshape(256, WIDTH),
        segment_ids,
        visual_pos,
        patches,
        ln_gain,
        ln_bias,
        fc1_weight.T,
        fc1_bias,
        fc2_weight,
        cosine,
        sine,
        jnp.asarray(pick, BF16),
    )
    pg, fc1_grad, fc2_grad = pl.pallas_call(
        hand_over,
        out_shape=tuple(jax.ShapeDtypeStruct(a.shape, a.dtype) for a in (pg, fc1_grad, fc2_grad)),
        in_specs=[vmem, vmem, vmem],
        out_specs=(vmem, vmem, vmem),
    )(pg, fc1_grad, fc2_grad)
    return (pg, fc1_grad, fc2_grad.T)


def solution(mesh):
    in_specs = (
        P("dp", "pipe", None, None),
        P("dp", None, "tensor", None),
        P(),
        P("pipe", None, "tensor", None),
        P("pipe", None, "tensor", None),
        P("pipe", "tensor", None, None),
        P("dp", None, None),
        P("dp", None),
        P("dp", "pipe", None),
        P(),
        P(),
        P(None, "tensor"),
        P("tensor"),
        P("tensor", None),
    )
    out_specs = (P("dp", "pipe", None), P(("dp", "pipe"), "tensor"), P(("dp", "pipe"), "tensor"))
    return jax.shard_map(local, mesh=mesh, in_specs=in_specs, out_specs=out_specs, check_vma=False)
```

```python
import functools

import jax
import jax.numpy as jnp
import numpy as np
from jax import lax
from jax.experimental import pallas as pl
from jax.experimental.pallas import tpu as pltpu
from jax.sharding import PartitionSpec as P

EPS_RMS = 1e-06
EPS_LN = 1e-06
THETA = 1000000.0
MESH = pl.DeviceIdType.MESH
F32 = jnp.float32
BF16 = jnp.bfloat16
SEQ = 96
WIDTH = 8192
HALF = 4096
BLK = 512
HEAD = 128
FACTOR = HEAD**-0.5
VIS = 48
CTX = 1280
PIECE = 320
LANES = 384


def nn(a, b):
    return lax.dot_general(a, b, (((1,), (0,)), ((), ())), preferred_element_type=F32)


def nt(a, b):
    return lax.dot_general(a, b, (((1,), (1,)), ((), ())), preferred_element_type=F32)


def tn(a, b):
    return lax.dot_general(a, b, (((0,), (0,)), ((), ())), preferred_element_type=F32)


def each(count, body):
    def step(i, carry):
        body(i)
        return carry

    lax.fori_loop(0, count, step, 0)


def eye_mask(size):
    return lax.broadcasted_iota(jnp.int32, (size, size), 0) == lax.broadcasted_iota(
        jnp.int32, (size, size), 1
    )


def to_row(column):
    size = column.shape[0]
    return jnp.sum(jnp.where(eye_mask(size), column, 0.0), axis=0, keepdims=True)


def to_column(row):
    size = row.shape[1]
    return jnp.sum(jnp.where(eye_mask(size), row, 0.0), axis=1, keepdims=True)


class Sems:
    def __init__(self):
        self.numbers = {}

    def __call__(self, *name):
        return self.numbers.setdefault(name, len(self.numbers))


def kernel(
    x_hbm,
    tg_hbm,
    gain_ref,
    wq_hbm,
    wkv_hbm,
    wo_hbm,
    seg_ref,
    pos_ref,
    patches_ref,
    lng_ref,
    lnb_ref,
    fc1_hbm,
    fc1b_ref,
    fc2_hbm,
    cos_hbm,
    sin_hbm,
    tgsel_hbm,
    pg_out,
    fc1_out,
    fc2_out,
    cos_ref,
    sin_ref,
    tgsel_ref,
    fc1_val,
    fc2_val,
    w3,
    wo,
    w3t,
    wot,
    f1,
    f2,
    xo,
    xb,
    sc,
    gb,
    tg,
    inc,
    normed,
    own_p,
    other_p,
    pf,
    qs,
    ks,
    vs,
    probs,
    gx_own,
    gx_other,
    acts,
    ins,
    inr,
    part,
    r1,
    out_block,
    vis,
    pu,
    iv,
    mn,
    mns,
    act,
    slope,
    nblk,
    lgb,
    ga_own,
    ga_other,
    gpre,
    mnr,
    actr,
    gpr,
    visr,
    pgp,
    pgpr,
    pgs,
    pgr,
    send_sem,
    recv_sem,
    local_sem,
    y_sem,
):
    dp = lax.axis_index("dp")
    pipe = lax.axis_index("pipe")
    ten = lax.axis_index("tensor")
    phase = pipe // 2
    core = pipe % 2
    zl = ten // 4
    xx = ten % 4
    sems = Sems()
    locals_ = Sems()

    def device(s=None, b=None, z=None, x=None, d=None, t=None):
        s = phase if s is None else s
        b = core if b is None else b
        if t is None:
            t = (zl if z is None else z) * 4 + (xx if x is None else x)
        return (dp if d is None else d, 2 * s + b, t)

    sibling = device(b=1 - core)
    cross = device(s=1 - phase, z=1 - zl)

    barrier = pltpu.get_barrier_semaphore()
    up_y = device(d=lax.rem(dp + 1, 4))
    down_y = device(d=lax.rem(dp + 3, 4))
    greeted = [sibling, up_y, down_y, device(s=1 - phase)]
    greeted += [device(t=lax.rem(ten + o, 8)) for o in range(1, 8)]
    greeted += [device(s=1 - phase, z=1 - zl, x=lax.rem(xx + o, 4)) for o in range(4)]
    for to in greeted:
        pl.semaphore_signal(barrier, inc=1, device_id=to, device_id_type=MESH)

    def local(name, src, dst):
        copy = pltpu.make_async_copy(src, dst, local_sem.at[locals_(name)])
        copy.start()
        return copy

    def remote(name, src, dst, to):
        number = sems(*name)
        copy = pltpu.make_async_remote_copy(
            src_ref=src,
            dst_ref=dst,
            send_sem=send_sem.at[number],
            recv_sem=recv_sem.at[number],
            device_id=to,
            device_id_type=MESH,
        )
        copy.start()
        return copy

    def arrive(name, ref):
        pltpu.make_async_copy(ref, ref, recv_sem.at[sems(*name)]).wait()

    mine = core * HALF
    theirs = (1 - core) * HALF
    lx = local("x", x_hbm, xo)
    lxh = local("xh", x_hbm.at[:, pl.ds(mine, HALF)], xb.at[core])
    lq = local("q", wq_hbm.at[pl.ds(mine, HALF), :], w3.at[core])
    lkv = local(
        "kv", wkv_hbm.at[pl.ds(mine, HALF), :], w3.at[2, :, pl.ds(core * HEAD, HEAD)]
    )
    lo = local("o", wo_hbm.at[:, pl.ds(mine, HALF)], wo.at[pl.ds(core * 256, 256), :])
    lsel = local("sel", tgsel_hbm, tgsel_ref)
    lcos = local("cos", cos_hbm, cos_ref)
    lsin = local("sin", sin_hbm, sin_ref)
    lf1 = local("f1", fc1_hbm, f1)
    lf2 = local("f2", fc2_hbm.at[:, pl.ds(mine, HALF)], f2)

    pl.semaphore_wait(barrier, len(greeted))

    def peer(o):
        return lax.rem(ten + o, 8)

    def push(name, src, dst):
        return [remote((name, o), src, dst, device(t=peer(o))) for o in range(1, 8)]

    def part_rows(h):
        return pl.ds(h * VIS, VIS)

    def send_term(m, h, o):
        j = peer(o)
        return remote(
            ("rs", m, h, o),
            part.at[m, j, part_rows(h), :],
            r1.at[m, ten, part_rows(h), :],
            device(t=j),
        )

    def send_terms(m, product):
        halves = 0
        for o in list(range(1, 8)) + [0]:
            j = peer(o)
            acc = product(pl.ds(pl.multiple_of(j * BLK, BLK), BLK))
            halves = acc.shape[0] // VIS
            part[m, j, pl.ds(0, acc.shape[0]), :] = acc.astype(BF16)
            if o:
                send_term(m, 0, o)
        for h in range(1, halves):
            for o in range(1, 8):
                send_term(m, h, o)

    def drain_phase(halves):
        for m in (1, 0):
            sent_wait(("gx", m), gx_own.at[m])
            for o in range(1, 8):
                sent_wait(("in", m, o), ins.at[m])
                for h in range(halves):
                    sent_wait(("rs", m, h, o), part.at[m, peer(o), part_rows(h), :])

    def sum_terms(m, h):
        total = part[m, ten, part_rows(h), :].astype(F32)
        for o in range(1, 8):
            src = peer(8 - o)
            ref = r1.at[m, src, part_rows(h), :]
            arrive(("rs", m, h, o), ref)
            total += ref[...].astype(F32)
        return total

    sent = []
    upper = phase == 1
    lower = jnp.logical_not(upper)
    cut_at = 384

    def tg_send(m):
        @pl.when(upper)
        def _():
            local(("tg", m), tg_hbm.at[m, core], tg.at[m, ten])
            for o in range(1, 4):
                remote(
                    ("tgx", m, o),
                    tg_hbm.at[m, core],
                    tg.at[m, ten],
                    device(x=lax.rem(xx + o, 4)),
                )
            for o in range(4):
                remote(
                    ("tgz", m, o),
                    tg_hbm.at[m, core, :, pl.ds(0, cut_at)],
                    tg.at[m, ten, :, pl.ds(0, cut_at)],
                    device(z=1 - zl, x=lax.rem(xx + o, 4)),
                )

        @pl.when(lower)
        def _():
            for o in range(4):
                remote(
                    ("tgc", m, o),
                    tg_hbm.at[m, core, :, pl.ds(cut_at, 1024 - cut_at)],
                    tg.at[m, ten, :, pl.ds(cut_at, 1024 - cut_at)],
                    device(s=1, z=1 - zl, x=lax.rem(xx + o, 4)),
                )

    tg_send(1)

    def tg_wait(m):
        pltpu.make_async_copy(
            tg.at[m, ten], tg.at[m, ten], local_sem.at[locals_(("tg", m))]
        ).wait()
        for o in range(1, 4):
            arrive(("tgx", m, o), tg.at[m, zl * 4 + lax.rem(xx + 4 - o, 4)])
        for o in range(4):
            slot = (1 - zl) * 4 + lax.rem(xx + 4 - o, 4)
            arrive(("tgz", m, o), tg.at[m, slot, :, pl.ds(0, cut_at)])
            arrive(("tgc", m, o), tg.at[m, slot, :, pl.ds(cut_at, 1024 - cut_at)])

    def sent_wait(name, ref):
        pltpu.make_async_copy(ref, ref, send_sem.at[sems(*name)]).wait()

    def tg_drain():
        for m in (1, 0):

            @pl.when(upper)
            def _(m=m):
                for o in range(1, 4):
                    sent_wait(("tgx", m, o), tg_hbm.at[m, core])
                for o in range(4):
                    sent_wait(("tgz", m, o), tg_hbm.at[m, core, :, pl.ds(0, cut_at)])

            @pl.when(lower)
            def _(m=m):
                for o in range(4):
                    sent_wait(
                        ("tgc", m, o), tg_hbm.at[m, core, :, pl.ds(cut_at, 1024 - cut_at)]
                    )

    sent.append(remote(("x",), x_hbm.at[:, pl.ds(theirs, HALF)], xb.at[core], sibling))
    sent.append(remote(("wq",), wq_hbm.at[pl.ds(theirs, HALF), :], w3.at[core], sibling))
    sent.append(
        remote(
            ("wkv",),
            wkv_hbm.at[pl.ds(theirs, HALF), :],
            w3.at[2, :, pl.ds(core * HEAD, HEAD)],
            sibling,
        )
    )
    sent.append(
        remote(
            ("wo",),
            wo_hbm.at[:, pl.ds(theirs, HALF)],
            wo.at[pl.ds(core * 256, 256), :],
            sibling,
        )
    )

    for i in range(8):
        pair = gain_ref[:, pl.ds(pl.multiple_of(mine + i * BLK, BLK), BLK)]
        gb[i] = jnp.where(upper, pair[1:2, :], pair[0:1, :])

    lx.wait()
    acc = jnp.zeros((SEQ, 1), F32)

    def square(i, acc):
        v = xo[:, pl.ds(pl.multiple_of(i * 1024, 1024), 1024)].astype(F32)
        return acc + jnp.sum(v * v, axis=1, keepdims=True)

    acc = lax.fori_loop(0, 8, square, acc)
    sc[core] = jnp.broadcast_to(lax.rsqrt(acc / WIDTH + EPS_RMS), (SEQ, HEAD))
    sent.append(remote(("sc",), sc.at[core], sc.at[core], sibling))

    def normalize(i):
        cols = pl.ds(pl.multiple_of(i * BLK, BLK), BLK)
        rows = [
            (xb[m, :, cols].astype(F32) * sc[m][:, 0:1] * gb[i]).astype(BF16) for m in range(2)
        ]
        normed[i] = jnp.concatenate(rows, axis=0)

    def own_product(j):
        acc = jnp.zeros((2 * SEQ, 256), F32)
        for i in range(8):
            acc += nn(normed[i], w3[j, i * BLK : (i + 1) * BLK, :])
        return acc

    lxh.wait()
    arrive(("x",), xb.at[1 - core])
    arrive(("sc",), sc.at[1 - core])
    each(8, normalize)
    lq.wait()
    own_p[core] = own_product(core)
    sent.append(remote(("p", 0), own_p.at[core], other_p.at[core], sibling))
    tg_send(0)
    arrive(("wq",), w3.at[1 - core])
    own_p[1 - core] = own_product(1 - core)
    sent.append(remote(("p", 1), own_p.at[1 - core], other_p.at[1 - core], sibling))
    lkv.wait()
    arrive(("wkv",), w3.at[2, :, pl.ds((1 - core) * HEAD, HEAD)])
    own_p[2] = own_product(2)
    sent.append(remote(("p", 2), own_p.at[2], other_p.at[2], sibling))

    def head_grads(m, slots, product):
        acc = jnp.zeros((SEQ, 512), F32)
        for slot in slots():
            acc += product(inc[m, slot], pl.ds(pl.multiple_of(slot * BLK, BLK), BLK))
        gx_own[m] = acc
        remote(("gx", m), gx_own.at[m], gx_other.at[m], sibling)

    def upper_heads(m):
        tg_wait(m)
        flat = tg[m].reshape(8 * 48, 1024)
        for e in range(4):
            wide = nn(tgsel_ref[e], flat).astype(BF16)
            inc[m, 2 * e] = wide[:, 0:BLK]
            inc[m, 2 * e + 1] = wide[:, BLK : 2 * BLK]
        head_grads(m, lambda: range(8), lambda block, cols: nt(block, wo[:, cols]))

    lsel.wait()
    lo.wait()
    arrive(("wo",), wo.at[pl.ds((1 - core) * 256, 256), :])
    pl.when(upper)(lambda: upper_heads(1))

    arrive(("p", 0), other_p.at[1 - core])
    arrive(("p", 1), other_p.at[core])
    arrive(("p", 2), other_p.at[2])
    for j in range(3):
        pf[:, j * 256 : (j + 1) * 256] = own_p[j] + other_p[j]

    lane = lax.broadcasted_iota(jnp.int32, (SEQ, HEAD), 1)
    low = lane < 64

    def rope(v, direction):
        return v * cos_ref[...] + direction * pltpu.roll(v, 64, 1) * sin_ref[...]

    def stacked(v):
        return jnp.concatenate([v[:, h * HEAD : (h + 1) * HEAD] for h in range(4)], axis=0)

    def forward(m):
        rows = pf[m * SEQ : (m + 1) * SEQ, :]
        q = jnp.concatenate(
            [rope(rows[:, h * HEAD : (h + 1) * HEAD], 1.0) for h in range(4)], axis=0
        ).astype(BF16)
        kv0 = rows[:, 512:640].astype(BF16).astype(F32)
        kv1 = rows[:, 640:768].astype(BF16).astype(F32)
        k = rope(jnp.where(low, kv0, pltpu.roll(kv1, 64, 1)), 1.0).astype(BF16)
        v = jnp.where(low, pltpu.roll(kv0, 64, 1), kv1).astype(BF16)
        qs[m] = q
        ks[m] = k
        vs[m] = v
        scores = nt(q, k) * FACTOR
        seg = seg_ref[0, m : m + 1, :].astype(F32)
        seg_col = to_column(seg)
        index_row = lax.broadcasted_iota(jnp.int32, (SEQ, SEQ), 0)
        index_col = lax.broadcasted_iota(jnp.int32, (SEQ, SEQ), 1)
        allowed = jnp.where((index_col <= index_row) & (seg_col == seg), 1.0, 0.0)
        allowed = jnp.concatenate([allowed] * 4, axis=0) > 0.5
        scores = jnp.where(allowed, scores, -1e30)
        top = jnp.max(scores, axis=1, keepdims=True)
        weights = jnp.where(allowed, jnp.exp(scores - top), 0.0)
        probs[m] = weights / jnp.sum(weights, axis=1, keepdims=True)

    def backward(m):
        arrive(("gx", m), gx_other.at[m])
        go = stacked(gx_own[m] + gx_other[m]).astype(BF16)
        pr = probs[m]
        gp = nt(go, vs[m])
        delta = jnp.sum(pr * gp, axis=1, keepdims=True)
        gs = (pr * (gp - delta) * FACTOR).astype(BF16)
        gq = nn(gs, ks[m])
        gk = rope(tn(gs, qs[m]), -1.0)
        gv = tn(pr.astype(BF16), go)
        pieces = [rope(gq[h * SEQ : (h + 1) * SEQ, :], -1.0) for h in range(4)]
        pieces.append(jnp.where(low, gk, pltpu.roll(gv, 64, 1)))
        pieces.append(jnp.where(low, pltpu.roll(gk, 64, 1), gv))
        inner = jnp.zeros((SEQ, 1), F32)
        for h in range(6):
            low_piece = pieces[h].astype(BF16)
            acts[m, :, h * HEAD : (h + 1) * HEAD] = low_piece
            inner += jnp.sum(
                low_piece.astype(F32) * pf[m * SEQ : (m + 1) * SEQ, h * HEAD : (h + 1) * HEAD],
                axis=1,
                keepdims=True,
            )
        row = to_row(inner / WIDTH)
        ins[m, :, 0:SEQ] = jnp.broadcast_to(row, (8, SEQ))
        for o in range(1, 8):
            remote(("in", m, o), ins.at[m], inr.at[m, ten], device(t=peer(o)))

    def inner_row(m):
        total = ins[m, 0:1, 0:SEQ]
        for o in range(1, 8):
            src = peer(8 - o)
            arrive(("in", m, o), inr.at[m, src])
            total += inr[m, src, 0:1, 0:SEQ]
        return total

    def merger_forward():
        for q in range(4):
            v = patches_ref[0, :, q * CTX : (q + 1) * CTX].astype(F32)
            v = v - jnp.mean(v, axis=1, keepdims=True)
            inv = lax.rsqrt(jnp.mean(v * v, axis=1, keepdims=True) + EPS_LN)
            pu[core, q] = v * inv
            iv[core, q] = jnp.broadcast_to(inv, (24, HEAD))
        remote(("pu",), pu.at[core], pu.at[core], sibling)
        remote(("iv",), iv.at[core], iv.at[core], sibling)
        for name in ("y1", "y2"):
            number = ("y1", "y2").index(name)
            for to in (up_y, down_y):
                pl.semaphore_signal(y_sem.at[number], inc=1, device_id=to, device_id_type=MESH)
            pl.semaphore_wait(y_sem.at[number], 2)
        lf1.wait()
        lf2.wait()
        arrive(("pu",), pu.at[1 - core])
        arrive(("iv",), iv.at[1 - core])
        gain = lng_ref[...].reshape(1, CTX)
        bias = lnb_ref[...].reshape(1, CTX)
        hidden = jnp.zeros((VIS, PIECE), F32)
        for q in range(4):
            n = jnp.concatenate([pu[0, q], pu[1, q]], axis=0)
            low_n = (n * gain + bias).astype(BF16)
            mn[:, q * CTX : (q + 1) * CTX] = low_n
            for j in range(4):
                mns[q * 4 + j, :, 0:PIECE] = low_n[:, j * PIECE : (j + 1) * PIECE]
            hidden += nt(low_n, f1[:, q * CTX : (q + 1) * CTX])
            lgb[q] = gain[:, q * PIECE : (q + 1) * PIECE]
        for q in range(2):
            n = jnp.concatenate([pu[0, 2 * core + q], pu[1, 2 * core + q]], axis=0)
            for j in range(4):
                nblk[q * 4 + j] = n[:, j * PIECE : (j + 1) * PIECE]
        hidden += fc1b_ref[...].reshape(1, PIECE)
        cdf = 0.5 * (1.0 + lax.erf(hidden * 0.7071067811865476))
        density = jnp.exp(-0.5 * hidden * hidden) * 0.3989422804014327
        slope[...] = cdf + hidden * density
        act[:, 0:PIECE] = (hidden * cdf).astype(BF16)
        spread("mn", lambda k: mns.at[8 * core + k], mnr)
        spread("act", lambda k: act, actr)

    my_slot = dp * 2 + phase

    def target(k):
        return (2 * core + k // 4, (k // 2) % 2 * 2 + k % 2, ten)

    def is_self(k):
        to = target(k)
        return (to[0] == dp) & (to[1] == pipe)

    def spread_one(name, k, source, slots):
        number = sems(name, 0) + k
        got = recv_sem.at[sems(name, "got") + my_slot]

        @pl.when(jnp.logical_not(is_self(k)))
        def _():
            pltpu.make_async_remote_copy(
                src_ref=source,
                dst_ref=slots.at[my_slot],
                send_sem=send_sem.at[number],
                recv_sem=got,
                device_id=target(k),
                device_id_type=MESH,
            ).start()

        @pl.when(is_self(k))
        def _():
            pltpu.make_async_copy(source, slots.at[my_slot], got).start()

    def spread(name, source, slots):
        for k in range(8):
            spread_one(name, k, source(k), slots)

    def spread_numbers():
        for name in ("mn", "act", "gp", "vis"):
            sems(name, "got")
            for i in range(1, 8):
                sems(name, "got+", i)
            for k in range(8):
                sems(name, k)

    spread_numbers()

    def collect(name, slots):
        for i in range(8):
            pltpu.make_async_copy(
                slots.at[i], slots.at[i], recv_sem.at[sems(name, "got") + i]
            ).wait()

    def drain_spread(name, source):
        for k in range(8):
            number = sems(name, k)

            @pl.when(jnp.logical_not(is_self(k)))
            def _(k=k, number=number):
                pltpu.make_async_copy(source(k), source(k), send_sem.at[number]).wait()

    own_cols = pl.ds(pl.multiple_of(ten * BLK, BLK), BLK)

    def ga_send():
        remote(("ga",), ga_own, ga_other, sibling)

    def upper_product(m):
        def product(cols):
            acc = nt(acts[m, :, 0:256], w3[0, cols, :])
            acc += nt(acts[m, :, 256:512], w3[1, cols, :])
            return acc + nt(acts[m, :, 512:768], w3[2, cols, :])

        return product

    lcos.wait()
    lsin.wait()
    forward(1)

    @pl.when(upper)
    def _():
        backward(1)
        send_terms(1, upper_product(1))

    forward(0)

    @pl.when(upper)
    def _():
        out = []
        upper_heads(0)
        backward(0)
        send_terms(0, upper_product(0))
        for m in (1, 0):
            inner = None
            for h in range(2):
                total = sum_terms(m, h)
                if h == 0:
                    inner = to_column(inner_row(m))
                low_row, high_row = h * VIS, (h + 1) * VIS
                scale = sc[m, low_row:high_row, 0:1]
                cols = pl.ds(pl.multiple_of(ten * BLK, BLK), BLK)
                unit = xb[m, low_row:high_row, cols].astype(F32) * scale
                w = total * gb[ten]
                out_block[m, low_row:high_row, :] = (
                    inc[m, ten, part_rows(h), :].astype(F32)
                    + scale * (w - unit * inner[low_row:high_row, :])
                ).astype(BF16)
                out.append(
                    remote(
                        ("down", m, h),
                        out_block.at[m, part_rows(h), :],
                        inc.at[m, ten, part_rows(h), :],
                        cross,
                    )
                )
        merger_forward()
        for copy in out:
            copy.wait_send()
        drain_phase(2)
        ga_own[...] = jnp.zeros_like(ga_own)
        for o in range(8):
            slot = peer(8 - o)
            arrive(("up", o), vis.at[slot])
            spread_one("vis", slot, vis.at[slot], visr)
            ga_own[...] += nt(vis[slot], f2[:, pl.ds(pl.multiple_of(slot * BLK, BLK), BLK)])
        ga_send()

    @pl.when(lower)
    def _():
        merger_forward()
        out = []
        held = (1 - zl) * 4 + xx

        def pass_on(m, h):
            ref = inc.at[m, held, part_rows(h), :]
            arrive(("down", m, h), ref)
            out.extend(push(("inc", m, h), ref, ref))

        def blocks(m):
            yield held
            for o in range(1, 8):
                if m == 1 and o == 4:
                    pass_on(0, 1)
                slot = lax.rem(peer(8 - o) + 4, 8)
                for h in range(2):
                    arrive((("inc", m, h), o), inc.at[m, slot, part_rows(h), :])
                yield slot

        def turn(i):
            cols = pl.ds(pl.multiple_of(i * BLK, BLK), BLK)
            wot[cols, :] = wo[:, cols].T
            for j in range(3):
                w3t[j, :, cols] = w3[j, cols, :].T

        each(8, turn)
        pass_on(1, 0)
        pass_on(1, 1)
        pass_on(0, 0)
        picks = {}

        def pick_rows(m):
            wide = lax.broadcasted_iota(jnp.int32, (VIS, SEQ), 0) + m * VIS
            across = lax.broadcasted_iota(jnp.int32, (VIS, SEQ), 1)
            tokens = jnp.sum(jnp.where(across == wide, pos_ref[...], 0), axis=1, keepdims=True)
            picks[m] = (tokens - m * SEQ) == across

        def lower_terms(m):
            pick = jnp.where(picks[m], 1.0, 0.0).astype(BF16)
            picked = nn(pick, acts[m]).astype(BF16)

            def product(cols):
                acc = nn(picked[:, 0:256], w3t[0, :, cols])
                acc += nn(picked[:, 256:512], w3t[1, :, cols])
                return acc + nn(picked[:, 512:768], w3t[2, :, cols])

            send_terms(m, product)

        def lower_block(m):
            mask = picks[m]
            pick = jnp.where(mask, 1.0, 0.0).astype(BF16)
            scale_row = to_row(sc[m][:, 0:1])
            scale = jnp.sum(jnp.where(mask, scale_row, 0.0), axis=1, keepdims=True)
            unit = nn(pick, xb[m, :, own_cols]) * scale
            rows = nn(pick, inc[m, ten])
            total = sum_terms(m, 0)
            inner = jnp.sum(jnp.where(mask, inner_row(m), 0.0), axis=1, keepdims=True)
            w = total * gb[ten]
            return (rows + scale * (w - unit * inner)).astype(BF16)

        for m in (1, 0):
            pick_rows(m)
            head_grads(m, lambda: blocks(m), lambda block, cols: nn(block, wot[cols, :]))
            backward(m)
            lower_terms(m)
        out_block[0, 0:VIS, :] = lower_block(1)
        for o in range(8):
            out.append(
                remote(
                    ("up", o),
                    out_block.at[0, pl.ds(0, VIS), :],
                    vis.at[ten],
                    device(s=1, t=peer(o)),
                )
            )
        vis[ten] = lower_block(0)
        out.extend(push("visp", vis.at[ten], vis.at[ten]))
        spread_one("vis", ten, vis.at[ten], visr)
        ga_own[...] = nt(vis[ten], f2[:, own_cols])
        for o in range(1, 8):
            slot = peer(8 - o)
            arrive(("visp", o), vis.at[slot])
            spread_one("vis", slot, vis.at[slot], visr)
            ga_own[...] += nt(vis[slot], f2[:, pl.ds(pl.multiple_of(slot * BLK, BLK), BLK)])
        ga_send()

    arrive(("ga",), ga_other)
    grad_pre = ((ga_own[...] + ga_other[...]) * slope[...]).astype(BF16)
    gpre[:, 0:PIECE] = grad_pre
    stat_lane = lax.broadcasted_iota(jnp.int32, (VIS, LANES - PIECE), 1)
    for q in range(2):
        cols = pl.ds(pl.multiple_of(core * 2 * CTX + q * CTX, CTX), CTX)
        gm = nn(grad_pre, f1[:, cols])
        u = gm * lng_ref[...].reshape(1, CTX)
        n = jnp.concatenate([pu[0, 2 * core + q], pu[1, 2 * core + q]], axis=0)
        s1 = jnp.sum(u, axis=1, keepdims=True)
        s2 = jnp.sum(u * n, axis=1, keepdims=True)
        h1 = s1.astype(BF16).astype(F32)
        h2 = s2.astype(BF16).astype(F32)
        stats = jnp.where(
            stat_lane == 0,
            h1,
            jnp.where(
                stat_lane == 1,
                s1 - h1,
                jnp.where(stat_lane == 2, h2, jnp.where(stat_lane == 3, s2 - h2, 0.0)),
            ),
        ).astype(BF16)
        for j in range(4):
            pgp[q * 4 + j, :, 0:PIECE] = gm[:, j * PIECE : (j + 1) * PIECE].astype(BF16)
            pgp[q * 4 + j, :, PIECE:LANES] = stats
    for o in range(1, 8):
        to = lax.rem(ten + o, 8)
        sent.append(remote(("pg", o), pgp.at[to], pgpr.at[ten], device(t=to)))
    spread("gp", lambda k: gpre, gpr)

    total = pgp[ten].astype(F32)
    for o in range(1, 8):
        src = lax.rem(ten + 8 - o, 8)
        arrive(("pg", o), pgpr.at[src])
        total += pgpr[src].astype(F32)
    s1 = (total[:, PIECE : PIECE + 1] + total[:, PIECE + 1 : PIECE + 2]) / CTX
    s2 = (total[:, PIECE + 2 : PIECE + 3] + total[:, PIECE + 3 : PIECE + 4]) / CTX
    patch = 2 * core + zl
    inv = jnp.concatenate([iv[0, patch], iv[1, patch]], axis=0)[:, 0:1]
    block = inv * (total[:, 0:PIECE] * lgb[xx] - s1 - nblk[ten] * s2)
    for b in range(2):
        rows = block[b * 24 : (b + 1) * 24, :]
        pgs[b, :, 0:PIECE] = rows[0:16, :].astype(BF16)
        pgs[b, :, PIECE : PIECE + 160] = jnp.concatenate(
            [rows[16:24, 0:160], rows[16:24, 160:320]], axis=0
        ).astype(BF16)
    my_code = core * 8 + ten
    for o in range(1, 16):
        code = lax.rem(my_code + o, 16)
        remote(
            ("po", o),
            pgs.at[code // 8],
            pgr.at[my_code],
            device(b=code // 8, t=lax.rem(code, 8)),
        )
    pgr[my_code] = pgs[core]

    collect("act", actr)
    collect("vis", visr)
    fc2_val[...] = tn(
        actr[...].reshape(8 * VIS, LANES)[:, 0:PIECE], visr[...].reshape(8 * VIS, BLK)
    )
    out2 = local("fc2", fc2_val, fc2_out)
    collect("mn", mnr)
    collect("gp", gpr)
    fc1_val[...] = tn(
        mnr[...].reshape(8 * VIS, LANES)[:, 0:PIECE], gpr[...].reshape(8 * VIS, LANES)[:, 0:PIECE]
    )
    out1 = local("fc1", fc1_val, fc1_out)

    @pl.when(lower)
    def _():
        held = (1 - zl) * 4 + xx
        for m in range(2):
            for h in range(2):
                for o in range(1, 8):
                    sent_wait((("inc", m, h), o), inc.at[m, held, part_rows(h), :])
        for o in range(8):
            sent_wait(("up", o), out_block.at[0, pl.ds(0, VIS), :])
        for o in range(1, 8):
            sent_wait(("visp", o), vis.at[ten])
        drain_phase(1)

    for copy in sent:
        copy.wait_send()
    tg_drain()
    sent_wait(("ga",), ga_own)
    sent_wait(("pu",), pu.at[core])
    sent_wait(("iv",), iv.at[core])
    drain_spread("mn", lambda k: mns.at[8 * core + k])
    drain_spread("act", lambda k: act)
    drain_spread("gp", lambda k: gpre)
    drain_spread("vis", lambda k: vis.at[k])
    for o in range(1, 16):
        arrive(("po", o), pgr.at[lax.rem(my_code + 16 - o, 16)])
    for q in range(4):
        pieces = []
        for j in range(4):
            msg = pgr[q * 4 + j].astype(F32)
            tail = jnp.concatenate(
                [msg[0:8, PIECE : PIECE + 160], msg[8:16, PIECE : PIECE + 160]], axis=1
            )
            pieces.append(jnp.concatenate([msg[:, 0:PIECE], tail], axis=0))
        pg_out[0, :, q * CTX : (q + 1) * CTX] = jnp.concatenate(pieces, axis=1).astype(BF16)

    for b_code in range(1, 16):
        sent_wait(("po", b_code), pgs.at[core])
    out1.wait()
    out2.wait()


def hand_over(a, b, c, a_out, b_out, c_out):
    a_out[...] = a[...]
    b_out[...] = b[...]
    c_out[...] = c[...]


def tables():
    freq = THETA ** (-(2.0 * np.arange(64, dtype=np.float64)) / HEAD)
    angles = np.arange(SEQ, dtype=np.float64)[:, None] * freq[None, :]
    cosine, sine = np.cos(angles), np.sin(angles)
    pick = np.zeros((4, SEQ, 8 * 48), np.float32)
    for e in range(4):
        for t in range(8):
            for i in range(12):
                pick[e, t * 12 + i, t * 48 + e * 12 + i] = 1.0
    return (
        np.concatenate([cosine, cosine], axis=1).astype(np.float32),
        np.concatenate([-sine, sine], axis=1).astype(np.float32),
        pick,
    )


def local(
    lm_inputs,
    top_grad,
    phase_gain,
    query_weight,
    kv_weight,
    out_weight,
    segment_ids,
    visual_pos,
    patches,
    ln_gain,
    ln_bias,
    fc1_weight,
    fc1_bias,
    fc2_weight,
):
    cosine, sine, pick = tables()
    shards = top_grad[0].reshape(2, 12, 2, 4, 1024).transpose(0, 2, 3, 1, 4)
    shards = shards.reshape(2, 2, 48, 1024)
    vmem = pl.BlockSpec(memory_space=pltpu.VMEM)
    hbm = pl.BlockSpec(memory_space=pl.ANY)
    v = pltpu.VMEM
    pg, fc1_grad, fc2_grad = pl.pallas_call(
        kernel,
        out_shape=(
            jax.ShapeDtypeStruct((1, 24, 4 * CTX), BF16),
            jax.ShapeDtypeStruct((PIECE, PIECE), F32),
            jax.ShapeDtypeStruct((PIECE, BLK), F32),
        ),
        in_specs=[
            hbm, hbm, vmem, hbm, hbm, hbm, vmem, vmem, vmem, vmem, vmem, hbm, vmem, hbm,
            hbm, hbm, hbm,
        ],
        out_specs=(vmem, hbm, hbm),
        scratch_shapes=[
            v((SEQ, HEAD), F32),
            v((SEQ, HEAD), F32),
            v((4, SEQ, 8 * 48), BF16),
            v((PIECE, PIECE), F32),
            v((PIECE, BLK), F32),
            v((3, HALF, 256), BF16),
            v((512, HALF), BF16),
            v((3, 256, HALF), BF16),
            v((HALF, 512), BF16),
            v((PIECE, 4 * CTX), BF16),
            v((PIECE, HALF), BF16),
            v((SEQ, WIDTH), BF16),
            v((2, SEQ, HALF), BF16),
            v((2, SEQ, HEAD), F32),
            v((8, 1, BLK), F32),
            v((2, 8, 48, 1024), BF16),
            v((2, 8, SEQ, BLK), BF16),
            v((8, 2 * SEQ, BLK), BF16),
            v((3, 2 * SEQ, 256), F32),
            v((3, 2 * SEQ, 256), F32),
            v((2 * SEQ, 768), F32),
            v((2, 4 * SEQ, HEAD), BF16),
            v((2, SEQ, HEAD), BF16),
            v((2, SEQ, HEAD), BF16),
            v((2, 4 * SEQ, SEQ), F32),
            v((2, SEQ, 512), F32),
            v((2, SEQ, 512), F32),
            v((2, SEQ, 768), BF16),
            v((2, 8, HEAD), F32),
            v((2, 8, 8, HEAD), F32),
            v((2, 8, SEQ, BLK), BF16),
            v((2, 8, SEQ, BLK), BF16),
            v((2, SEQ, BLK), BF16),
            v((8, VIS, BLK), BF16),
            v((2, 4, 24, CTX), F32),
            v((2, 4, 24, HEAD), F32),
            v((VIS, 4 * CTX), BF16),
            v((16, VIS, LANES), BF16),
            v((VIS, LANES), BF16),
            v((VIS, PIECE), F32),
            v((8, VIS, PIECE), F32),
            v((4, 1, PIECE), F32),
            v((VIS, PIECE), F32),
            v((VIS, PIECE), F32),
            v((VIS, LANES), BF16),
            v((8, VIS, LANES), BF16),
            v((8, VIS, LANES), BF16),
            v((8, VIS, LANES), BF16),
            v((8, VIS, BLK), BF16),
            v((8, VIS, LANES), BF16),
            v((8, VIS, LANES), BF16),
            v((2, 16, BLK), BF16),
            v((16, 16, BLK), BF16),
            pltpu.SemaphoreType.DMA((288,)),
            pltpu.SemaphoreType.DMA((288,)),
            pltpu.SemaphoreType.DMA((20,)),
            pltpu.SemaphoreType.REGULAR((2,)),
        ],
        compiler_params=pltpu.CompilerParams(
            collective_id=0, has_side_effects=True, vmem_limit_bytes=60 * 1024 * 1024
        ),
    )(
        lm_inputs[0, 0],
        shards,
        phase_gain,
        query_weight.reshape(WIDTH, 256),
        kv_weight.reshape(WIDTH, HEAD),
        out_weight.reshape(256, WIDTH),
        segment_ids,
        visual_pos,
        patches,
        ln_gain,
        ln_bias,
        fc1_weight.T,
        fc1_bias,
        fc2_weight,
        cosine,
        sine,
        jnp.asarray(pick, BF16),
    )
    pg, fc1_grad, fc2_grad = pl.pallas_call(
        hand_over,
        out_shape=tuple(jax.ShapeDtypeStruct(a.shape, a.dtype) for a in (pg, fc1_grad, fc2_grad)),
        in_specs=[vmem, vmem, vmem],
        out_specs=(vmem, vmem, vmem),
    )(pg, fc1_grad, fc2_grad)
    return (pg, fc1_grad, fc2_grad.T)


def solution(mesh):
    in_specs = (
        P("dp", "pipe", None, None),
        P("dp", None, "tensor", None),
        P(),
        P("pipe", None, "tensor", None),
        P("pipe", None, "tensor", None),
        P("pipe", "tensor", None, None),
        P("dp", None, None),
        P("dp", None),
        P("dp", "pipe", None),
        P(),
        P(),
        P(None, "tensor"),
        P("tensor"),
        P("tensor", None),
    )
    out_specs = (P("dp", "pipe", None), P(("dp", "pipe"), "tensor"), P(("dp", "pipe"), "tensor"))
    return jax.shard_map(local, mesh=mesh, in_specs=in_specs, out_specs=out_specs, check_vma=False)
```

```python
import functools

import jax
import jax.numpy as jnp
import numpy as np
from jax import lax
from jax.experimental import pallas as pl
from jax.experimental.pallas import tpu as pltpu
from jax.sharding import PartitionSpec as P

EPS_RMS = 1e-06
EPS_LN = 1e-06
THETA = 1000000.0
MESH = pl.DeviceIdType.MESH
F32 = jnp.float32
BF16 = jnp.bfloat16
SEQ = 96
WIDTH = 8192
HALF = 4096
BLK = 512
HEAD = 128
FACTOR = HEAD**-0.5
VIS = 48
CTX = 1280
PIECE = 320
LANES = 384


def nn(a, b):
    return lax.dot_general(a, b, (((1,), (0,)), ((), ())), preferred_element_type=F32)


def nt(a, b):
    return lax.dot_general(a, b, (((1,), (1,)), ((), ())), preferred_element_type=F32)


def tn(a, b):
    return lax.dot_general(a, b, (((0,), (0,)), ((), ())), preferred_element_type=F32)


def each(count, body):
    def step(i, carry):
        body(i)
        return carry

    lax.fori_loop(0, count, step, 0)


def eye_mask(size):
    return lax.broadcasted_iota(jnp.int32, (size, size), 0) == lax.broadcasted_iota(
        jnp.int32, (size, size), 1
    )


def to_row(column):
    size = column.shape[0]
    return jnp.sum(jnp.where(eye_mask(size), column, 0.0), axis=0, keepdims=True)


def to_column(row):
    size = row.shape[1]
    return jnp.sum(jnp.where(eye_mask(size), row, 0.0), axis=1, keepdims=True)


class Sems:
    def __init__(self):
        self.numbers = {}

    def __call__(self, *name):
        return self.numbers.setdefault(name, len(self.numbers))


def kernel(
    x_hbm,
    tg_hbm,
    gain_ref,
    wq_hbm,
    wkv_hbm,
    wo_hbm,
    seg_ref,
    pos_ref,
    patches_ref,
    lng_ref,
    lnb_ref,
    fc1_hbm,
    fc1b_ref,
    fc2_hbm,
    cos_hbm,
    sin_hbm,
    tgsel_hbm,
    pg_out,
    fc1_out,
    fc2_out,
    cos_ref,
    sin_ref,
    tgsel_ref,
    fc1_val,
    fc2_val,
    w3,
    wo,
    w3t,
    wot,
    f1,
    f2,
    xo,
    xb,
    sc,
    gb,
    tg,
    inc,
    normed,
    own_p,
    other_p,
    pf,
    qs,
    ks,
    vs,
    probs,
    gx_own,
    gx_other,
    acts,
    ins,
    inr,
    part,
    r1,
    out_block,
    vis,
    pu,
    iv,
    mn,
    mns,
    act,
    slope,
    nblk,
    lgb,
    ga_own,
    ga_other,
    gpre,
    mnr,
    actr,
    gpr,
    visr,
    pgp,
    pgpr,
    pgs,
    pgr,
    send_sem,
    recv_sem,
    local_sem,
    y_sem,
):
    dp = lax.axis_index("dp")
    pipe = lax.axis_index("pipe")
    ten = lax.axis_index("tensor")
    phase = pipe // 2
    core = pipe % 2
    zl = ten // 4
    xx = ten % 4
    sems = Sems()
    locals_ = Sems()

    def device(s=None, b=None, z=None, x=None, d=None, t=None):
        s = phase if s is None else s
        b = core if b is None else b
        if t is None:
            t = (zl if z is None else z) * 4 + (xx if x is None else x)
        return (dp if d is None else d, 2 * s + b, t)

    sibling = device(b=1 - core)
    cross = device(s=1 - phase, z=1 - zl)

    barrier = pltpu.get_barrier_semaphore()
    up_y = device(d=lax.rem(dp + 1, 4))
    down_y = device(d=lax.rem(dp + 3, 4))
    greeted = [device(s=1 - phase, z=1 - zl, x=lax.rem(xx + 4 - o, 4)) for o in range(1, 5)]
    greeted += [device(s=1 - phase)]
    greeted += [device(t=lax.rem(ten + 8 - o, 8)) for o in range(1, 8)]
    greeted += [up_y, down_y, sibling]
    for to in greeted:
        pl.semaphore_signal(barrier, inc=1, device_id=to, device_id_type=MESH)

    def local(name, src, dst):
        copy = pltpu.make_async_copy(src, dst, local_sem.at[locals_(name)])
        copy.start()
        return copy

    def remote(name, src, dst, to):
        number = sems(*name)
        copy = pltpu.make_async_remote_copy(
            src_ref=src,
            dst_ref=dst,
            send_sem=send_sem.at[number],
            recv_sem=recv_sem.at[number],
            device_id=to,
            device_id_type=MESH,
        )
        copy.start()
        return copy

    def arrive(name, ref):
        pltpu.make_async_copy(ref, ref, recv_sem.at[sems(*name)]).wait()

    mine = core * HALF
    theirs = (1 - core) * HALF
    lx = local("x", x_hbm, xo)
    lxh = local("xh", x_hbm.at[:, pl.ds(mine, HALF)], xb.at[core])
    lq = local("q", wq_hbm.at[pl.ds(mine, HALF), :], w3.at[core])
    lkv = local(
        "kv", wkv_hbm.at[pl.ds(mine, HALF), :], w3.at[2, :, pl.ds(core * HEAD, HEAD)]
    )
    lo = local("o", wo_hbm.at[:, pl.ds(mine, HALF)], wo.at[pl.ds(core * 256, 256), :])
    lsel = local("sel", tgsel_hbm, tgsel_ref)
    lcos = local("cos", cos_hbm, cos_ref)
    lsin = local("sin", sin_hbm, sin_ref)
    lf1 = local("f1", fc1_hbm, f1)
    lf2 = local("f2", fc2_hbm.at[:, pl.ds(mine, HALF)], f2)

    pl.semaphore_wait(barrier, len(greeted))

    def peer(o):
        return lax.rem(ten + o, 8)

    def push(name, src, dst):
        return [remote((name, o), src, dst, device(t=peer(o))) for o in range(1, 8)]

    def part_rows(h):
        return pl.ds(h * VIS, VIS)

    def send_term(m, h, o):
        j = peer(o)
        return remote(
            ("rs", m, h, o),
            part.at[m, j, part_rows(h), :],
            r1.at[m, ten, part_rows(h), :],
            device(t=j),
        )

    def send_terms(m, product):
        halves = 0
        for o in list(range(1, 8)) + [0]:
            j = peer(o)
            acc = product(pl.ds(pl.multiple_of(j * BLK, BLK), BLK))
            halves = acc.shape[0] // VIS
            part[m, j, pl.ds(0, acc.shape[0]), :] = acc.astype(BF16)
            if o:
                send_term(m, 0, o)
        for h in range(1, halves):
            for o in range(1, 8):
                send_term(m, h, o)

    def drain_phase(halves):
        for m in (1, 0):
            sent_wait(("gx", m), gx_own.at[m])
            for o in range(1, 8):
                sent_wait(("in", m, o), ins.at[m])
                for h in range(halves):
                    sent_wait(("rs", m, h, o), part.at[m, peer(o), part_rows(h), :])

    def sum_terms(m, h):
        total = part[m, ten, part_rows(h), :].astype(F32)
        for o in range(1, 8):
            src = peer(8 - o)
            ref = r1.at[m, src, part_rows(h), :]
            arrive(("rs", m, h, o), ref)
            total += ref[...].astype(F32)
        return total

    sent = []
    upper = phase == 1
    lower = jnp.logical_not(upper)
    cut_at = 384

    def tg_send(m):
        @pl.when(upper)
        def _():
            local(("tg", m), tg_hbm.at[m, core], tg.at[m, ten])
            for o in range(1, 4):
                remote(
                    ("tgx", m, o),
                    tg_hbm.at[m, core],
                    tg.at[m, ten],
                    device(x=lax.rem(xx + o, 4)),
                )
            for o in range(4):
                remote(
                    ("tgz", m, o),
                    tg_hbm.at[m, core, :, pl.ds(0, cut_at)],
                    tg.at[m, ten, :, pl.ds(0, cut_at)],
                    device(z=1 - zl, x=lax.rem(xx + o, 4)),
                )

        @pl.when(lower)
        def _():
            for o in range(4):
                remote(
                    ("tgc", m, o),
                    tg_hbm.at[m, core, :, pl.ds(cut_at, 1024 - cut_at)],
                    tg.at[m, ten, :, pl.ds(cut_at, 1024 - cut_at)],
                    device(s=1, z=1 - zl, x=lax.rem(xx + o, 4)),
                )

    tg_send(1)

    def tg_wait(m):
        pltpu.make_async_copy(
            tg.at[m, ten], tg.at[m, ten], local_sem.at[locals_(("tg", m))]
        ).wait()
        for o in range(1, 4):
            arrive(("tgx", m, o), tg.at[m, zl * 4 + lax.rem(xx + 4 - o, 4)])
        for o in range(4):
            slot = (1 - zl) * 4 + lax.rem(xx + 4 - o, 4)
            arrive(("tgz", m, o), tg.at[m, slot, :, pl.ds(0, cut_at)])
            arrive(("tgc", m, o), tg.at[m, slot, :, pl.ds(cut_at, 1024 - cut_at)])

    def sent_wait(name, ref):
        pltpu.make_async_copy(ref, ref, send_sem.at[sems(*name)]).wait()

    def tg_drain():
        for m in (1, 0):

            @pl.when(upper)
            def _(m=m):
                for o in range(1, 4):
                    sent_wait(("tgx", m, o), tg_hbm.at[m, core])
                for o in range(4):
                    sent_wait(("tgz", m, o), tg_hbm.at[m, core, :, pl.ds(0, cut_at)])

            @pl.when(lower)
            def _(m=m):
                for o in range(4):
                    sent_wait(
                        ("tgc", m, o), tg_hbm.at[m, core, :, pl.ds(cut_at, 1024 - cut_at)]
                    )

    sent.append(remote(("x",), x_hbm.at[:, pl.ds(theirs, HALF)], xb.at[core], sibling))
    sent.append(remote(("wq",), wq_hbm.at[pl.ds(theirs, HALF), :], w3.at[core], sibling))
    sent.append(
        remote(
            ("wkv",),
            wkv_hbm.at[pl.ds(theirs, HALF), :],
            w3.at[2, :, pl.ds(core * HEAD, HEAD)],
            sibling,
        )
    )
    sent.append(
        remote(
            ("wo",),
            wo_hbm.at[:, pl.ds(theirs, HALF)],
            wo.at[pl.ds(core * 256, 256), :],
            sibling,
        )
    )

    for i in range(8):
        pair = gain_ref[:, pl.ds(pl.multiple_of(mine + i * BLK, BLK), BLK)]
        gb[i] = jnp.where(upper, pair[1:2, :], pair[0:1, :])

    lx.wait()
    acc = jnp.zeros((SEQ, 1), F32)

    def square(i, acc):
        v = xo[:, pl.ds(pl.multiple_of(i * 1024, 1024), 1024)].astype(F32)
        return acc + jnp.sum(v * v, axis=1, keepdims=True)

    acc = lax.fori_loop(0, 8, square, acc)
    sc[core] = jnp.broadcast_to(lax.rsqrt(acc / WIDTH + EPS_RMS), (SEQ, HEAD))
    sent.append(remote(("sc",), sc.at[core], sc.at[core], sibling))

    def normalize(i):
        cols = pl.ds(pl.multiple_of(i * BLK, BLK), BLK)
        rows = [
            (xb[m, :, cols].astype(F32) * sc[m][:, 0:1] * gb[i]).astype(BF16) for m in range(2)
        ]
        normed[i] = jnp.concatenate(rows, axis=0)

    def own_product(j):
        acc = jnp.zeros((2 * SEQ, 256), F32)
        for i in range(8):
            acc += nn(normed[i], w3[j, i * BLK : (i + 1) * BLK, :])
        return acc

    lxh.wait()
    arrive(("x",), xb.at[1 - core])
    arrive(("sc",), sc.at[1 - core])
    each(8, normalize)
    lq.wait()
    own_p[core] = own_product(core)
    sent.append(remote(("p", 0), own_p.at[core], other_p.at[core], sibling))
    tg_send(0)
    arrive(("wq",), w3.at[1 - core])
    own_p[1 - core] = own_product(1 - core)
    sent.append(remote(("p", 1), own_p.at[1 - core], other_p.at[1 - core], sibling))
    lkv.wait()
    arrive(("wkv",), w3.at[2, :, pl.ds((1 - core) * HEAD, HEAD)])
    own_p[2] = own_product(2)
    sent.append(remote(("p", 2), own_p.at[2], other_p.at[2], sibling))

    def head_grads(m, slots, product):
        acc = jnp.zeros((SEQ, 512), F32)
        for slot in slots():
            acc += product(inc[m, slot], pl.ds(pl.multiple_of(slot * BLK, BLK), BLK))
        gx_own[m] = acc
        remote(("gx", m), gx_own.at[m], gx_other.at[m], sibling)

    def upper_heads(m):
        tg_wait(m)
        flat = tg[m].reshape(8 * 48, 1024)
        for e in range(4):
            wide = nn(tgsel_ref[e], flat).astype(BF16)
            inc[m, 2 * e] = wide[:, 0:BLK]
            inc[m, 2 * e + 1] = wide[:, BLK : 2 * BLK]
        head_grads(m, lambda: range(8), lambda block, cols: nt(block, wo[:, cols]))

    lsel.wait()
    lo.wait()
    arrive(("wo",), wo.at[pl.ds((1 - core) * 256, 256), :])
    pl.when(upper)(lambda: upper_heads(1))

    arrive(("p", 0), other_p.at[1 - core])
    arrive(("p", 1), other_p.at[core])
    arrive(("p", 2), other_p.at[2])
    for j in range(3):
        pf[:, j * 256 : (j + 1) * 256] = own_p[j] + other_p[j]

    lane = lax.broadcasted_iota(jnp.int32, (SEQ, HEAD), 1)
    low = lane < 64

    def rope(v, direction):
        return v * cos_ref[...] + direction * pltpu.roll(v, 64, 1) * sin_ref[...]

    def stacked(v):
        return jnp.concatenate([v[:, h * HEAD : (h + 1) * HEAD] for h in range(4)], axis=0)

    def forward(m):
        rows = pf[m * SEQ : (m + 1) * SEQ, :]
        q = jnp.concatenate(
            [rope(rows[:, h * HEAD : (h + 1) * HEAD], 1.0) for h in range(4)], axis=0
        ).astype(BF16)
        kv0 = rows[:, 512:640].astype(BF16).astype(F32)
        kv1 = rows[:, 640:768].astype(BF16).astype(F32)
        k = rope(jnp.where(low, kv0, pltpu.roll(kv1, 64, 1)), 1.0).astype(BF16)
        v = jnp.where(low, pltpu.roll(kv0, 64, 1), kv1).astype(BF16)
        qs[m] = q
        ks[m] = k
        vs[m] = v
        scores = nt(q, k) * FACTOR
        seg = seg_ref[0, m : m + 1, :].astype(F32)
        seg_col = to_column(seg)
        index_row = lax.broadcasted_iota(jnp.int32, (SEQ, SEQ), 0)
        index_col = lax.broadcasted_iota(jnp.int32, (SEQ, SEQ), 1)
        allowed = jnp.where((index_col <= index_row) & (seg_col == seg), 1.0, 0.0)
        allowed = jnp.concatenate([allowed] * 4, axis=0) > 0.5
        scores = jnp.where(allowed, scores, -1e30)
        top = jnp.max(scores, axis=1, keepdims=True)
        weights = jnp.where(allowed, jnp.exp(scores - top), 0.0)
        probs[m] = weights / jnp.sum(weights, axis=1, keepdims=True)

    def backward(m):
        arrive(("gx", m), gx_other.at[m])
        go = stacked(gx_own[m] + gx_other[m]).astype(BF16)
        pr = probs[m]
        gp = nt(go, vs[m])
        delta = jnp.sum(pr * gp, axis=1, keepdims=True)
        gs = (pr * (gp - delta) * FACTOR).astype(BF16)
        gq = nn(gs, ks[m])
        gk = rope(tn(gs, qs[m]), -1.0)
        gv = tn(pr.astype(BF16), go)
        pieces = [rope(gq[h * SEQ : (h + 1) * SEQ, :], -1.0) for h in range(4)]
        pieces.append(jnp.where(low, gk, pltpu.roll(gv, 64, 1)))
        pieces.append(jnp.where(low, pltpu.roll(gk, 64, 1), gv))
        inner = jnp.zeros((SEQ, 1), F32)
        for h in range(6):
            low_piece = pieces[h].astype(BF16)
            acts[m, :, h * HEAD : (h + 1) * HEAD] = low_piece
            inner += jnp.sum(
                low_piece.astype(F32) * pf[m * SEQ : (m + 1) * SEQ, h * HEAD : (h + 1) * HEAD],
                axis=1,
                keepdims=True,
            )
        row = to_row(inner / WIDTH)
        ins[m, :, 0:SEQ] = jnp.broadcast_to(row, (8, SEQ))
        for o in range(1, 8):
            remote(("in", m, o), ins.at[m], inr.at[m, ten], device(t=peer(o)))

    def inner_row(m):
        total = ins[m, 0:1, 0:SEQ]
        for o in range(1, 8):
            src = peer(8 - o)
            arrive(("in", m, o), inr.at[m, src])
            total += inr[m, src, 0:1, 0:SEQ]
        return total

    def merger_forward():
        for q in range(4):
            v = patches_ref[0, :, q * CTX : (q + 1) * CTX].astype(F32)
            v = v - jnp.mean(v, axis=1, keepdims=True)
            inv = lax.rsqrt(jnp.mean(v * v, axis=1, keepdims=True) + EPS_LN)
            pu[core, q] = v * inv
            iv[core, q] = jnp.broadcast_to(inv, (24, HEAD))
        remote(("pu",), pu.at[core], pu.at[core], sibling)
        remote(("iv",), iv.at[core], iv.at[core], sibling)
        for name in ("y1", "y2"):
            number = ("y1", "y2").index(name)
            for to in (up_y, down_y):
                pl.semaphore_signal(y_sem.at[number], inc=1, device_id=to, device_id_type=MESH)
            pl.semaphore_wait(y_sem.at[number], 2)
        lf1.wait()
        lf2.wait()
        arrive(("pu",), pu.at[1 - core])
        arrive(("iv",), iv.at[1 - core])
        gain = lng_ref[...].reshape(1, CTX)
        bias = lnb_ref[...].reshape(1, CTX)
        hidden = jnp.zeros((VIS, PIECE), F32)
        for q in range(4):
            n = jnp.concatenate([pu[0, q], pu[1, q]], axis=0)
            low_n = (n * gain + bias).astype(BF16)
            mn[:, q * CTX : (q + 1) * CTX] = low_n
            for j in range(4):
                mns[q * 4 + j, :, 0:PIECE] = low_n[:, j * PIECE : (j + 1) * PIECE]
            hidden += nt(low_n, f1[:, q * CTX : (q + 1) * CTX])
            lgb[q] = gain[:, q * PIECE : (q + 1) * PIECE]
        for q in range(2):
            n = jnp.concatenate([pu[0, 2 * core + q], pu[1, 2 * core + q]], axis=0)
            for j in range(4):
                nblk[q * 4 + j] = n[:, j * PIECE : (j + 1) * PIECE]
        hidden += fc1b_ref[...].reshape(1, PIECE)
        cdf = 0.5 * (1.0 + lax.erf(hidden * 0.7071067811865476))
        density = jnp.exp(-0.5 * hidden * hidden) * 0.3989422804014327
        slope[...] = cdf + hidden * density
        act[:, 0:PIECE] = (hidden * cdf).astype(BF16)
        spread("mn", lambda k: mns.at[8 * core + k], mnr)
        spread("act", lambda k: act, actr)

    my_slot = dp * 2 + phase

    def target(k):
        return (2 * core + k // 4, (k // 2) % 2 * 2 + k % 2, ten)

    def is_self(k):
        to = target(k)
        return (to[0] == dp) & (to[1] == pipe)

    def spread_one(name, k, source, slots):
        number = sems(name, 0) + k
        got = recv_sem.at[sems(name, "got") + my_slot]

        @pl.when(jnp.logical_not(is_self(k)))
        def _():
            pltpu.make_async_remote_copy(
                src_ref=source,
                dst_ref=slots.at[my_slot],
                send_sem=send_sem.at[number],
                recv_sem=got,
                device_id=target(k),
                device_id_type=MESH,
            ).start()

        @pl.when(is_self(k))
        def _():
            pltpu.make_async_copy(source, slots.at[my_slot], got).start()

    def spread(name, source, slots):
        for k in range(8):
            spread_one(name, k, source(k), slots)

    def spread_numbers():
        for name in ("mn", "act", "gp", "vis"):
            sems(name, "got")
            for i in range(1, 8):
                sems(name, "got+", i)
            for k in range(8):
                sems(name, k)

    spread_numbers()

    def collect(name, slots):
        for i in range(8):
            pltpu.make_async_copy(
                slots.at[i], slots.at[i], recv_sem.at[sems(name, "got") + i]
            ).wait()

    def drain_spread(name, source):
        for k in range(8):
            number = sems(name, k)

            @pl.when(jnp.logical_not(is_self(k)))
            def _(k=k, number=number):
                pltpu.make_async_copy(source(k), source(k), send_sem.at[number]).wait()

    own_cols = pl.ds(pl.multiple_of(ten * BLK, BLK), BLK)

    def ga_send():
        remote(("ga",), ga_own, ga_other, sibling)

    def upper_product(m):
        def product(cols):
            acc = nt(acts[m, :, 0:256], w3[0, cols, :])
            acc += nt(acts[m, :, 256:512], w3[1, cols, :])
            return acc + nt(acts[m, :, 512:768], w3[2, cols, :])

        return product

    lcos.wait()
    lsin.wait()
    forward(1)

    @pl.when(upper)
    def _():
        backward(1)
        send_terms(1, upper_product(1))

    forward(0)

    @pl.when(upper)
    def _():
        out = []
        upper_heads(0)
        backward(0)
        send_terms(0, upper_product(0))
        for m in (1, 0):
            inner = None
            for h in range(2):
                total = sum_terms(m, h)
                if h == 0:
                    inner = to_column(inner_row(m))
                low_row, high_row = h * VIS, (h + 1) * VIS
                scale = sc[m, low_row:high_row, 0:1]
                cols = pl.ds(pl.multiple_of(ten * BLK, BLK), BLK)
                unit = xb[m, low_row:high_row, cols].astype(F32) * scale
                w = total * gb[ten]
                out_block[m, low_row:high_row, :] = (
                    inc[m, ten, part_rows(h), :].astype(F32)
                    + scale * (w - unit * inner[low_row:high_row, :])
                ).astype(BF16)
                out.append(
                    remote(
                        ("down", m, h),
                        out_block.at[m, part_rows(h), :],
                        inc.at[m, ten, part_rows(h), :],
                        cross,
                    )
                )
        merger_forward()
        for copy in out:
            copy.wait_send()
        drain_phase(2)
        ga_own[...] = jnp.zeros_like(ga_own)
        for o in range(8):
            slot = peer(8 - o)
            arrive(("up", o), vis.at[slot])
            spread_one("vis", slot, vis.at[slot], visr)
            ga_own[...] += nt(vis[slot], f2[:, pl.ds(pl.multiple_of(slot * BLK, BLK), BLK)])
        ga_send()

    @pl.when(lower)
    def _():
        merger_forward()
        out = []
        held = (1 - zl) * 4 + xx

        def pass_on(m, h):
            ref = inc.at[m, held, part_rows(h), :]
            arrive(("down", m, h), ref)
            out.extend(push(("inc", m, h), ref, ref))

        def blocks(m):
            yield held
            for o in range(1, 8):
                if m == 1 and o == 4:
                    pass_on(0, 1)
                slot = lax.rem(peer(8 - o) + 4, 8)
                for h in range(2):
                    arrive((("inc", m, h), o), inc.at[m, slot, part_rows(h), :])
                yield slot

        def turn(i):
            cols = pl.ds(pl.multiple_of(i * BLK, BLK), BLK)
            wot[cols, :] = wo[:, cols].T
            for j in range(3):
                w3t[j, :, cols] = w3[j, cols, :].T

        each(8, turn)
        pass_on(1, 0)
        pass_on(1, 1)
        pass_on(0, 0)
        picks = {}

        def pick_rows(m):
            wide = lax.broadcasted_iota(jnp.int32, (VIS, SEQ), 0) + m * VIS
            across = lax.broadcasted_iota(jnp.int32, (VIS, SEQ), 1)
            tokens = jnp.sum(jnp.where(across == wide, pos_ref[...], 0), axis=1, keepdims=True)
            picks[m] = (tokens - m * SEQ) == across

        def lower_terms(m):
            pick = jnp.where(picks[m], 1.0, 0.0).astype(BF16)
            picked = nn(pick, acts[m]).astype(BF16)

            def product(cols):
                acc = nn(picked[:, 0:256], w3t[0, :, cols])
                acc += nn(picked[:, 256:512], w3t[1, :, cols])
                return acc + nn(picked[:, 512:768], w3t[2, :, cols])

            send_terms(m, product)

        def lower_block(m):
            mask = picks[m]
            pick = jnp.where(mask, 1.0, 0.0).astype(BF16)
            scale_row = to_row(sc[m][:, 0:1])
            scale = jnp.sum(jnp.where(mask, scale_row, 0.0), axis=1, keepdims=True)
            unit = nn(pick, xb[m, :, own_cols]) * scale
            rows = nn(pick, inc[m, ten])
            total = sum_terms(m, 0)
            inner = jnp.sum(jnp.where(mask, inner_row(m), 0.0), axis=1, keepdims=True)
            w = total * gb[ten]
            return (rows + scale * (w - unit * inner)).astype(BF16)

        for m in (1, 0):
            pick_rows(m)
            head_grads(m, lambda: blocks(m), lambda block, cols: nn(block, wot[cols, :]))
            backward(m)
            lower_terms(m)
        out_block[0, 0:VIS, :] = lower_block(1)
        for o in range(8):
            out.append(
                remote(
                    ("up", o),
                    out_block.at[0, pl.ds(0, VIS), :],
                    vis.at[ten],
                    device(s=1, t=peer(o)),
                )
            )
        vis[ten] = lower_block(0)
        out.extend(push("visp", vis.at[ten], vis.at[ten]))
        spread_one("vis", ten, vis.at[ten], visr)
        ga_own[...] = nt(vis[ten], f2[:, own_cols])
        for o in range(1, 8):
            slot = peer(8 - o)
            arrive(("visp", o), vis.at[slot])
            spread_one("vis", slot, vis.at[slot], visr)
            ga_own[...] += nt(vis[slot], f2[:, pl.ds(pl.multiple_of(slot * BLK, BLK), BLK)])
        ga_send()
        for copy in out:
            copy.wait_send()
        drain_phase(1)

    arrive(("ga",), ga_other)
    grad_pre = ((ga_own[...] + ga_other[...]) * slope[...]).astype(BF16)
    gpre[:, 0:PIECE] = grad_pre
    stat_lane = lax.broadcasted_iota(jnp.int32, (VIS, LANES - PIECE), 1)
    for q in range(2):
        cols = pl.ds(pl.multiple_of(core * 2 * CTX + q * CTX, CTX), CTX)
        gm = nn(grad_pre, f1[:, cols])
        u = gm * lng_ref[...].reshape(1, CTX)
        n = jnp.concatenate([pu[0, 2 * core + q], pu[1, 2 * core + q]], axis=0)
        s1 = jnp.sum(u, axis=1, keepdims=True)
        s2 = jnp.sum(u * n, axis=1, keepdims=True)
        h1 = s1.astype(BF16).astype(F32)
        h2 = s2.astype(BF16).astype(F32)
        stats = jnp.where(
            stat_lane == 0,
            h1,
            jnp.where(
                stat_lane == 1,
                s1 - h1,
                jnp.where(stat_lane == 2, h2, jnp.where(stat_lane == 3, s2 - h2, 0.0)),
            ),
        ).astype(BF16)
        for j in range(4):
            pgp[q * 4 + j, :, 0:PIECE] = gm[:, j * PIECE : (j + 1) * PIECE].astype(BF16)
            pgp[q * 4 + j, :, PIECE:LANES] = stats
    for o in range(1, 8):
        to = lax.rem(ten + o, 8)
        sent.append(remote(("pg", o), pgp.at[to], pgpr.at[ten], device(t=to)))
    spread("gp", lambda k: gpre, gpr)

    total = pgp[ten].astype(F32)
    for o in range(1, 8):
        src = lax.rem(ten + 8 - o, 8)
        arrive(("pg", o), pgpr.at[src])
        total += pgpr[src].astype(F32)
    s1 = (total[:, PIECE : PIECE + 1] + total[:, PIECE + 1 : PIECE + 2]) / CTX
    s2 = (total[:, PIECE + 2 : PIECE + 3] + total[:, PIECE + 3 : PIECE + 4]) / CTX
    patch = 2 * core + zl
    inv = jnp.concatenate([iv[0, patch], iv[1, patch]], axis=0)[:, 0:1]
    block = inv * (total[:, 0:PIECE] * lgb[xx] - s1 - nblk[ten] * s2)
    for b in range(2):
        rows = block[b * 24 : (b + 1) * 24, :]
        pgs[b, :, 0:PIECE] = rows[0:16, :].astype(BF16)
        pgs[b, :, PIECE : PIECE + 160] = jnp.concatenate(
            [rows[16:24, 0:160], rows[16:24, 160:320]], axis=0
        ).astype(BF16)
    my_code = core * 8 + ten
    for o in range(1, 16):
        code = lax.rem(my_code + o, 16)
        sent.append(
            remote(
                ("po", o),
                pgs.at[code // 8],
                pgr.at[my_code],
                device(b=code // 8, t=lax.rem(code, 8)),
            )
        )
    pgr[my_code] = pgs[core]

    collect("act", actr)
    collect("vis", visr)
    fc2_val[...] = tn(
        actr[...].reshape(8 * VIS, LANES)[:, 0:PIECE], visr[...].reshape(8 * VIS, BLK)
    )
    out2 = local("fc2", fc2_val, fc2_out)
    collect("mn", mnr)
    collect("gp", gpr)
    fc1_val[...] = tn(
        mnr[...].reshape(8 * VIS, LANES)[:, 0:PIECE], gpr[...].reshape(8 * VIS, LANES)[:, 0:PIECE]
    )
    out1 = local("fc1", fc1_val, fc1_out)
    for o in range(1, 16):
        arrive(("po", o), pgr.at[lax.rem(my_code + 16 - o, 16)])
    for q in range(4):
        pieces = []
        for j in range(4):
            msg = pgr[q * 4 + j].astype(F32)
            tail = jnp.concatenate(
                [msg[0:8, PIECE : PIECE + 160], msg[8:16, PIECE : PIECE + 160]], axis=1
            )
            pieces.append(jnp.concatenate([msg[:, 0:PIECE], tail], axis=0))
        pg_out[0, :, q * CTX : (q + 1) * CTX] = jnp.concatenate(pieces, axis=1).astype(BF16)

    for copy in sent:
        copy.wait_send()
    out1.wait()
    out2.wait()
    tg_drain()
    sent_wait(("ga",), ga_own)
    sent_wait(("pu",), pu.at[core])
    sent_wait(("iv",), iv.at[core])
    drain_spread("mn", lambda k: mns.at[8 * core + k])
    drain_spread("act", lambda k: act)
    drain_spread("gp", lambda k: gpre)
    drain_spread("vis", lambda k: vis.at[k])


def hand_over(a, b, c, a_out, b_out, c_out):
    a_out[...] = a[...]
    b_out[...] = b[...]
    c_out[...] = c[...]


def tables():
    freq = THETA ** (-(2.0 * np.arange(64, dtype=np.float64)) / HEAD)
    angles = np.arange(SEQ, dtype=np.float64)[:, None] * freq[None, :]
    cosine, sine = np.cos(angles), np.sin(angles)
    pick = np.zeros((4, SEQ, 8 * 48), np.float32)
    for e in range(4):
        for t in range(8):
            for i in range(12):
                pick[e, t * 12 + i, t * 48 + i * 4 + e] = 1.0
    return (
        np.concatenate([cosine, cosine], axis=1).astype(np.float32),
        np.concatenate([-sine, sine], axis=1).astype(np.float32),
        pick,
    )


def local(
    lm_inputs,
    top_grad,
    phase_gain,
    query_weight,
    kv_weight,
    out_weight,
    segment_ids,
    visual_pos,
    patches,
    ln_gain,
    ln_bias,
    fc1_weight,
    fc1_bias,
    fc2_weight,
):
    cosine, sine, pick = tables()
    shards = top_grad[0].reshape(2, 12, 2, HALF).transpose(0, 2, 1, 3)
    shards = shards.reshape(2, 2, 48, 1024)
    vmem = pl.BlockSpec(memory_space=pltpu.VMEM)
    hbm = pl.BlockSpec(memory_space=pl.ANY)
    v = pltpu.VMEM
    pg, fc1_grad, fc2_grad = pl.pallas_call(
        kernel,
        out_shape=(
            jax.ShapeDtypeStruct((1, 24, 4 * CTX), BF16),
            jax.ShapeDtypeStruct((PIECE, PIECE), F32),
            jax.ShapeDtypeStruct((PIECE, BLK), F32),
        ),
        in_specs=[
            hbm, hbm, vmem, hbm, hbm, hbm, vmem, vmem, vmem, vmem, vmem, hbm, vmem, hbm,
            hbm, hbm, hbm,
        ],
        out_specs=(vmem, hbm, hbm),
        scratch_shapes=[
            v((SEQ, HEAD), F32),
            v((SEQ, HEAD), F32),
            v((4, SEQ, 8 * 48), BF16),
            v((PIECE, PIECE), F32),
            v((PIECE, BLK), F32),
            v((3, HALF, 256), BF16),
            v((512, HALF), BF16),
            v((3, 256, HALF), BF16),
            v((HALF, 512), BF16),
            v((PIECE, 4 * CTX), BF16),
            v((PIECE, HALF), BF16),
            v((SEQ, WIDTH), BF16),
            v((2, SEQ, HALF), BF16),
            v((2, SEQ, HEAD), F32),
            v((8, 1, BLK), F32),
            v((2, 8, 48, 1024), BF16),
            v((2, 8, SEQ, BLK), BF16),
            v((8, 2 * SEQ, BLK), BF16),
            v((3, 2 * SEQ, 256), F32),
            v((3, 2 * SEQ, 256), F32),
            v((2 * SEQ, 768), F32),
            v((2, 4 * SEQ, HEAD), BF16),
            v((2, SEQ, HEAD), BF16),
            v((2, SEQ, HEAD), BF16),
            v((2, 4 * SEQ, SEQ), F32),
            v((2, SEQ, 512), F32),
            v((2, SEQ, 512), F32),
            v((2, SEQ, 768), BF16),
            v((2, 8, HEAD), F32),
            v((2, 8, 8, HEAD), F32),
            v((2, 8, SEQ, BLK), BF16),
            v((2, 8, SEQ, BLK), BF16),
            v((2, SEQ, BLK), BF16),
            v((8, VIS, BLK), BF16),
            v((2, 4, 24, CTX), F32),
            v((2, 4, 24, HEAD), F32),
            v((VIS, 4 * CTX), BF16),
            v((16, VIS, LANES), BF16),
            v((VIS, LANES), BF16),
            v((VIS, PIECE), F32),
            v((8, VIS, PIECE), F32),
            v((4, 1, PIECE), F32),
            v((VIS, PIECE), F32),
            v((VIS, PIECE), F32),
            v((VIS, LANES), BF16),
            v((8, VIS, LANES), BF16),
            v((8, VIS, LANES), BF16),
            v((8, VIS, LANES), BF16),
            v((8, VIS, BLK), BF16),
            v((8, VIS, LANES), BF16),
            v((8, VIS, LANES), BF16),
            v((2, 16, BLK), BF16),
            v((16, 16, BLK), BF16),
            pltpu.SemaphoreType.DMA((288,)),
            pltpu.SemaphoreType.DMA((288,)),
            pltpu.SemaphoreType.DMA((20,)),
            pltpu.SemaphoreType.REGULAR((2,)),
        ],
        compiler_params=pltpu.CompilerParams(
            collective_id=0, has_side_effects=True, vmem_limit_bytes=60 * 1024 * 1024
        ),
    )(
        lm_inputs[0, 0],
        shards,
        phase_gain,
        query_weight.reshape(WIDTH, 256),
        kv_weight.reshape(WIDTH, HEAD),
        out_weight.reshape(256, WIDTH),
        segment_ids,
        visual_pos,
        patches,
        ln_gain,
        ln_bias,
        fc1_weight.T,
        fc1_bias,
        fc2_weight,
        cosine,
        sine,
        jnp.asarray(pick, BF16),
    )
    pg, fc1_grad, fc2_grad = pl.pallas_call(
        hand_over,
        out_shape=tuple(jax.ShapeDtypeStruct(a.shape, a.dtype) for a in (pg, fc1_grad, fc2_grad)),
        in_specs=[vmem, vmem, vmem],
        out_specs=(vmem, vmem, vmem),
    )(pg, fc1_grad, fc2_grad)
    return (pg, fc1_grad, fc2_grad.T)


def solution(mesh):
    in_specs = (
        P("dp", "pipe", None, None),
        P("dp", None, "tensor", None),
        P(),
        P("pipe", None, "tensor", None),
        P("pipe", None, "tensor", None),
        P("pipe", "tensor", None, None),
        P("dp", None, None),
        P("dp", None),
        P("dp", "pipe", None),
        P(),
        P(),
        P(None, "tensor"),
        P("tensor"),
        P("tensor", None),
    )
    out_specs = (P("dp", "pipe", None), P(("dp", "pipe"), "tensor"), P(("dp", "pipe"), "tensor"))
    return jax.shard_map(local, mesh=mesh, in_specs=in_specs, out_specs=out_specs, check_vma=False)
```
